32 devices in a mesh: lat: 4 (over x, core), lon: 8 (over z, y).
Axes of the slice: x: 2, y: 2, z: 4, core: 2. Of those that a mesh axis runs over, the one named last changes fastest.
Arguments:
- field: bfloat16 [512, 256, 128], P('lat', 'lon'), may hold values from -6 to 6
- land: int32 [512, 256], P('lat', 'lon'), may hold values 0 or 1
- mirror: int32 [256], replicated, may hold values from 0 to 255, as said below
- depth_weight: bfloat16 [49, 128], replicated, may hold values from -2 to 2
- norm_gain: bfloat16 [128], replicated, may hold values from 0.5 to 2
- up_weight: bfloat16 [128, 512], replicated, may hold values from -0.5 to 0.5
- up_bias: bfloat16 [512], replicated, may hold values from -3 to 3
- down_proj: bfloat16 [512, 128], replicated, may hold values from -0.25 to 0.25
- layer_scale: bfloat16 [128], replicated, may hold values from 0.25 to 1
- section_gain: bfloat16 [3, 128], replicated, may hold values from 0.5 to 2
- section_weight: bfloat16 [3, 512, 128], replicated, may hold values from -0.25 to 0.25
- section_bias: bfloat16 [3, 128], replicated, may hold values from -3 to 3
- cotangent: bfloat16 [64, 32, 128], P('lat', 'lon'), may hold values from -6 to 6
Outputs:
- bottleneck: bfloat16 [64, 32, 128], P('lat', 'lon')
- grad_field: bfloat16 [512, 256, 128], P('lat', 'lon')
- grad_depth: float32 [49, 128], replicated
- grad_up: float32 [128, 512], replicated
- grad_down: float32 [512, 128], replicated
- grad_section: float32 [3, 512, 128], replicated
The draws below stay inside these ranges and needn't reach their ends.
Inputs may be any that keep to these rules, and one draw needn't show every extreme that they name: mirror[i] = (s - i) mod 256 for one s, the same for all i; mirror is its own inverse.
All inputs are finite; a program needn't handle non-finite values. No bound on the sum of `land` on one device may be relied on, other than what follows from the above.
Results may differ from the reference program's by a relative error of at most 0.017.
Values may be sent and summed in bfloat16 or wider, within the bound.
No kernel may reach another device: no remote copies, remote signals or barrier semaphores. Data moves between devices by JAX's collectives and lax.ppermute only.
A program may use at most 128 MiB of HBM per device.

```python
import math
import jax
import jax.numpy as jnp
from jax import lax

C = 128
HID = 512
SECTIONS = 3
ROWS = 512
LON = 256


def draw_mirror(key, part):
    pivot = jax.random.randint(jax.random.fold_in(key, 11), (), 0, LON, dtype=jnp.int32)
    return jnp.mod(pivot - jnp.arange(LON, dtype=jnp.int32), LON).astype(jnp.int32)


def touch_ends(values, stream_key, least, top_value):
    longest = values.shape.index(max(values.shape))
    spots = []
    for shift in (0, 1):
        where = [jax.random.randint(jax.random.fold_in(stream_key, axis), (), 0, length) for axis, length in enumerate(values.shape)]
        where[longest] = (where[longest] + shift) % values.shape[longest]
        spots.append(tuple(where))
    return values.at[spots[0]].set(least).at[spots[1]].set(top_value)


def block_scale(rng, dims, shards, low, top_value):
    factor_of, own = 1.0, jax.random.fold_in(rng, 6)
    for axis_at, shards_of in shards:
        draws = jnp.exp(jax.random.uniform(jax.random.fold_in(own, axis_at), (shards_of,), jnp.float32, low / len(shards), top_value / len(shards)))
        factor_of = factor_of * jnp.repeat(draws, dims[axis_at] // shards_of).reshape([-1 if axis == axis_at else 1 for axis in range(len(dims))])
    return factor_of


def scatter_about(key, shape, deviation, limit, pieces=(), held_as=jnp.bfloat16):
    values = deviation * jax.random.normal(key, shape, jnp.float32)
    if pieces:
        values = values * block_scale(key, shape, pieces, -0.22, 0.18)
    return jnp.clip(values, -limit, limit).astype(held_as)


def setup_inputs(seed: int = 0) -> dict:
    key_of = jax.random.split(jax.random.key(seed), 14)
    return {
        "field": scatter_about(key_of[0], (ROWS, LON, C), 1.0, 6.0, ((0, 4), (1, 8))),
        "land": touch_ends((jax.random.randint(key_of[1], (ROWS, LON), 0, 4) < 3).astype(jnp.int32), jax.random.fold_in(key_of[1], 1), 0, 1),
        "mirror": draw_mirror(jax.random.fold_in(key_of[13], 71), 0),
        "depth_weight": scatter_about(key_of[3], (49, C), 7 ** -0.5, 2.0),
        "norm_gain": jnp.clip(jnp.exp(jax.random.uniform(key_of[4], (C,), jnp.float32, math.log(0.5), math.log(2.0))), 0.5, 2.0).astype(jnp.bfloat16),
        "up_weight": scatter_about(key_of[5], (C, HID), C ** -0.5, 0.5),
        "up_bias": scatter_about(key_of[6], (HID,), 0.5, 3.0),
        "down_proj": scatter_about(key_of[7], (HID, C), HID ** -0.5, 0.25),
        "layer_scale": jnp.clip(jnp.exp(jax.random.uniform(key_of[8], (C,), jnp.float32, math.log(0.25), math.log(1.0))), 0.25, 1.0).astype(jnp.bfloat16),
        "section_gain": jnp.clip(jnp.exp(jax.random.uniform(key_of[9], (SECTIONS, C), jnp.float32, math.log(0.5), math.log(2.0))), 0.5, 2.0).astype(jnp.bfloat16),
        "section_weight": scatter_about(key_of[10], (SECTIONS, 4 * C, C), (4 * C) ** -0.5, 0.25),
        "section_bias": scatter_about(key_of[11], (SECTIONS, C), 0.5, 3.0),
        "cotangent": scatter_about(key_of[12], (ROWS // 8, LON // 8, C), 1.0, 6.0, ((0, 4), (1, 8))),
    }


epsilon = 1e-06

def norm_parts(values):
    center = values - lax.optimization_barrier(jnp.mean(values, axis=-1, keepdims=True))
    rstd = lax.rsqrt(lax.optimization_barrier(jnp.mean(center * center, axis=-1, keepdims=True)) + epsilon)
    return (center * rstd, rstd)

def norm_back(grad_hat, normed_hat, rstd):
    first = lax.optimization_barrier(jnp.mean(grad_hat, axis=-1, keepdims=True))
    second = lax.optimization_barrier(jnp.mean(grad_hat * normed_hat, axis=-1, keepdims=True))
    return rstd * (grad_hat - first - normed_hat * second)

def gelu_parts(hidden):
    cdf = 0.5 * (1.0 + jax.scipy.special.erf(hidden * 0.7071067811865476))
    dens = jnp.exp(-0.5 * hidden * hidden) * 0.3989422804014327
    return (hidden * cdf, cdf + hidden * dens)

def block_pass(ext_rows, x_rows, land_rows, cot_rows, taps, norm_gain, up_weight, up_bias, down_proj, layer_scale, section_gain, section_weight, section_bias):
    block_rows = x_rows.shape[0]
    block_cols = x_rows.shape[1]
    chans = x_rows.shape[2]
    depth_out = jnp.zeros((block_rows, block_cols, chans), jnp.float32)
    for tap in range(49):
        tap_row = tap // 7
        tap_col = tap % 7
        depth_out = depth_out + ext_rows[tap_row:tap_row + block_rows, tap_col:tap_col + block_cols] * taps[tap]
    depth_hat, depth_rstd = norm_parts(depth_out)
    normed = (depth_hat * norm_gain.astype(jnp.float32)).astype(jnp.bfloat16)
    flat = normed.reshape(-1, chans)
    hidden = jnp.dot(flat, up_weight, preferred_element_type=jnp.float32) + up_bias.astype(jnp.float32)
    active_full, slope = gelu_parts(hidden)
    active = active_full.astype(jnp.bfloat16)
    mixed = jnp.dot(active, down_proj, preferred_element_type=jnp.float32).reshape(block_rows, block_cols, chans)
    scale_f = layer_scale.astype(jnp.float32)
    level = (land_rows * (x_rows.astype(jnp.float32) + scale_f * mixed)).astype(jnp.bfloat16)
    saved = []
    for section in range(SECTIONS):
        section_hat, section_rstd = norm_parts(level.astype(jnp.float32))
        section_norm = (section_hat * section_gain[section].astype(jnp.float32)).astype(jnp.bfloat16)
        size_r = section_norm.shape[0]
        size_c = section_norm.shape[1]
        patches = section_norm.reshape(size_r // 2, 2, size_c // 2, 2, chans).astype(jnp.float32)
        kernel = section_weight[section].reshape(2, 2, chans, chans).astype(jnp.float32)
        level = (jnp.einsum('iajbc,abcd->ijd', patches, kernel, precision=lax.Precision.HIGHEST) + section_bias[section].astype(jnp.float32)).astype(jnp.bfloat16)
        saved.append((section_hat, section_rstd, patches, kernel))
    upstream = cot_rows
    section_list = [None] * SECTIONS
    for section in range(SECTIONS - 1, -1, -1):
        section_hat, section_rstd, patches, kernel = saved[section]
        up_f = upstream.astype(jnp.float32)
        section_list[section] = jnp.einsum('iajbc,ijd->abcd', patches, up_f, precision=lax.Precision.HIGHEST).reshape(4 * chans, chans)
        spread = jnp.einsum('ijd,abcd->iajbc', up_f, kernel, precision=lax.Precision.HIGHEST).reshape(section_hat.shape)
        upstream = norm_back(spread * section_gain[section].astype(jnp.float32), section_hat, section_rstd).astype(jnp.bfloat16)
    section_total = jnp.stack(section_list)
    direct = land_rows * upstream.astype(jnp.float32)
    mix_grad = (direct * scale_f).astype(jnp.bfloat16).reshape(-1, chans)
    down_sums = jnp.dot(active.T, mix_grad, preferred_element_type=jnp.float32)
    act_grad = jnp.dot(mix_grad, down_proj.T, preferred_element_type=jnp.float32)
    hidden_grad = (act_grad * slope).astype(jnp.bfloat16)
    up_sums = jnp.dot(flat.T, hidden_grad, preferred_element_type=jnp.float32)
    normed_grad = jnp.dot(hidden_grad, up_weight.T, preferred_element_type=jnp.float32).reshape(block_rows, block_cols, chans)
    depth_grad = norm_back(normed_grad * norm_gain.astype(jnp.float32), depth_hat, depth_rstd).astype(jnp.bfloat16)
    depth_f = depth_grad.astype(jnp.float32)
    tap_list = []
    for tap in range(49):
        tap_row = tap // 7
        tap_col = tap % 7
        tap_list.append(lax.optimization_barrier(jnp.sum(ext_rows[tap_row:tap_row + block_rows, tap_col:tap_col + block_cols] * depth_f, axis=(0, 1))))
    tap_sums = jnp.stack(tap_list)
    padded = jnp.pad(depth_f, ((6, 6), (6, 6), (0, 0)))
    back_sum = jnp.zeros((block_rows + 6, block_cols + 6, chans), jnp.float32)
    for tap in range(49):
        tap_row = tap // 7
        tap_col = tap % 7
        back_sum = back_sum + padded[6 - tap_row:12 - tap_row + block_rows, 6 - tap_col:12 - tap_col + block_cols] * taps[tap]
    return (level, direct, back_sum, (tap_sums, up_sums, down_sums, section_total))

def reference(field, land, mirror, depth_weight, norm_gain, up_weight, up_bias, down_proj, layer_scale, section_gain, section_weight, section_bias, cotangent):
    x_full = field.astype(jnp.float32)
    fold = jnp.take(x_full[ROWS - 3:][::-1], mirror, axis=1)
    core = jnp.concatenate([jnp.zeros((3, LON, C), jnp.float32), x_full, fold], axis=0)
    extended = jnp.concatenate([core[:, LON - 3:], core, core[:, :3]], axis=1)
    taps = depth_weight.astype(jnp.float32)

    def step(carry, index):
        grad_ext, acc_taps, acc_up, acc_down, acc_section = carry
        start = (index * 8).astype(jnp.int32)
        ext_rows = lax.dynamic_slice_in_dim(extended, start, 14, 0)
        x_rows = lax.dynamic_slice_in_dim(field, start, 8, 0)
        land_rows = lax.dynamic_slice_in_dim(land, start, 8, 0).astype(jnp.float32)[:, :, None]
        cot_rows = lax.dynamic_slice_in_dim(cotangent, index.astype(jnp.int32), 1, 0)
        out_rows, direct, back_sum, grads = block_pass(ext_rows, x_rows, land_rows, cot_rows, taps, norm_gain, up_weight, up_bias, down_proj, layer_scale, section_gain, section_weight, section_bias)
        old = lax.dynamic_slice_in_dim(grad_ext, start, 14, 0)
        grad_ext = lax.dynamic_update_slice_in_dim(grad_ext, old + back_sum, start, 0)
        carry = (grad_ext, acc_taps + grads[0], acc_up + grads[1], acc_down + grads[2], acc_section + grads[3])
        return (carry, (out_rows, direct))
    start_carry = (jnp.zeros((ROWS + 6, LON + 6, C), jnp.float32), jnp.zeros((49, C), jnp.float32), jnp.zeros((C, HID), jnp.float32), jnp.zeros((HID, C), jnp.float32), jnp.zeros((SECTIONS, 4 * C, C), jnp.float32))
    carry, stacked = lax.scan(step, start_carry, jnp.arange(ROWS // 8, dtype=jnp.int32))
    bottleneck = stacked[0].reshape(ROWS // 8, LON // 8, C)
    direct_all = stacked[1].reshape(ROWS, LON, C)
    grad_ext = carry[0]
    core_grad = grad_ext[:, 3:3 + LON]
    core_grad = core_grad.at[:, LON - 3:].add(grad_ext[:, :3])
    core_grad = core_grad.at[:, :3].add(grad_ext[:, LON + 3:])
    grad_x = core_grad[3:3 + ROWS]
    fold_grad = lax.optimization_barrier(core_grad[ROWS + 3:ROWS + 6].astype(jnp.bfloat16)).astype(jnp.float32)
    for level_k in range(3):
        grad_x = grad_x.at[ROWS - 1 - level_k, mirror].add(fold_grad[level_k])
    grad_field = (direct_all + grad_x).astype(jnp.bfloat16)
    factor = 1.0 / math.sqrt(ROWS * LON / 64.0)
    return (bottleneck, grad_field, carry[1] * factor, carry[2] * factor, carry[3] * factor, carry[4] * factor)
```

```python
import functools
import math

import jax
import jax.numpy as jnp
from jax import lax
from jax.experimental import pallas as pl
from jax.experimental.pallas import tpu as pltpu
from jax.sharding import PartitionSpec as P

SECTIONS = 3
EPS = 1e-6
f32, bf16 = jnp.float32, jnp.bfloat16
S = 16
LOG2E = 1.4426950408889634
VMEM = pl.BlockSpec(memory_space=pltpu.VMEM)
SMEM = pl.BlockSpec(memory_space=pltpu.SMEM)
PARAMS = pltpu.CompilerParams(vmem_limit_bytes=60 * 2**20)


def dot(a, b):
    return jnp.dot(a, b, preferred_element_type=f32)


def dot_t(a, b):
    return lax.dot_general(a, b, (((0,), (0,)), ((), ())), preferred_element_type=f32)


def dot_r(a, b):
    return lax.dot_general(a, b, (((1,), (1,)), ((), ())), preferred_element_type=f32)


def ones_mean(n):
    return jnp.full((n, 128), 1.0 / 128, bf16)


def pair_mean():
    r = lax.broadcasted_iota(jnp.int32, (256, 256), 0) // 128
    c = lax.broadcasted_iota(jnp.int32, (256, 256), 1) // 128
    return jnp.where(r == c, 1.0 / 128, 0.0).astype(bf16)


def split2(x):
    hi = x.astype(bf16)
    lo = (x - hi.astype(f32)).astype(bf16)
    return jnp.concatenate([hi, lo], axis=1)


def norm_bwd(u, hat, rstd, pm):
    m = dot(jnp.concatenate([u.astype(bf16), (u * hat).astype(bf16)], axis=1), pm)
    return rstd * (u - m[:, :128] - hat * m[:, 128:])


def gelu(h):
    cdf = 0.5 + 0.5 * lax.erf(h * 0.7071067811865476)
    e = jnp.exp2(h * h * (-0.5 * LOG2E))
    return h * cdf, cdf + h * (e * 0.3989422804014327)


def weights_table(dw, w49, flip):
    for t in range(49):
        w49[48 - t if flip else t] = jnp.broadcast_to(dw[t : t + 1, :].astype(f32), (S, 128))


def conv49(el, w49, emit, I, CW):
    CE = CW + 6
    CG = 8

    def step(n, _):
        i = n // (CW // CG)
        c0 = (n % (CW // CG)) * CG
        acc = [None] * CG
        for a in range(7):
            row = [el[(i + a) * CE + c0 + m].astype(f32) for m in range(CG + 6)]
            for b in range(7):
                w = w49[a * 7 + b]
                for k in range(CG):
                    pr = row[k + b] * w
                    acc[k] = pr if acc[k] is None else acc[k] + pr
        for k in range(CG):
            emit(i, c0 + k, acc[k])
        return 0

    lax.fori_loop(0, I * (CW // CG), step, 0)


def block_body(
    R, CW,
    field, south, north, left, right, landb, dw, gain, up, down, scale, sgain, sw, sbias, cot,
    bott, gout, dirout, first, last, lcol, rcol, sums,
    x2d, el, w49, dep, hat, rst, nrm, act, slp, shat, srst, p1, back, tacc, downs, ups,
):
    I = R // S
    CE = CW + 6
    XW = 40
    n0 = R * CW

    def asm(r, _):
        x2d[pl.ds((r + 3) * XW + 3, CW), :] = field[r].astype(f32)
        return 0

    lax.fori_loop(0, R, asm, 0, unroll=4)
    for k in range(3):
        x2d[pl.ds(k * XW + 3, CW), :] = south[k].astype(f32)
        x2d[pl.ds((R + 3 + k) * XW + 3, CW), :] = north[k].astype(f32)
        x2d[pl.ds(k, R + 6, stride=XW), :] = left[k].astype(f32)
        x2d[pl.ds(CW + 3 + k, R + 6, stride=XW), :] = right[k].astype(f32)

    def tr(i, _):
        for c in range(CE):
            el[i * CE + c] = x2d[pl.ds(i * XW + c, S, stride=I * XW), :].astype(bf16)
        return 0

    lax.fori_loop(0, I + 6, tr, 0)
    weights_table(dw, w49, False)

    def emit(i, c, v):
        dep[pl.ds((i * CW + c) * S, S), :] = v

    conv49(el, w49, emit, I, CW)

    jj, j1, pm = ones_mean(256), ones_mean(128), pair_mean()
    g_n = gain[...].astype(f32)
    sc = scale[...].astype(f32)
    sg0 = sgain[0:1, :].astype(f32)
    T1 = 1024

    def nfwd(n, _):
        base = pl.multiple_of(n * T1, T1)
        x = dep[pl.ds(base, T1), :]
        cen = x - dot(split2(x), jj)
        rs = lax.rsqrt(dot((cen * cen).astype(bf16), j1) + EPS)
        ht = cen * rs
        hat[pl.ds(base, T1), :] = ht
        rst[pl.ds(base, T1), :] = rs
        nrm[pl.ds(base, T1), :] = (ht * g_n).astype(bf16)
        return 0

    lax.fori_loop(0, n0 // T1, nfwd, 0)

    T2 = 512
    onec = (lax.broadcasted_iota(jnp.int32, (T2, 128), 1) == 0).astype(f32).astype(bf16)

    def upf(n, _):
        base = pl.multiple_of(n * T2, T2)
        lhs = jnp.concatenate([nrm[pl.ds(base, T2), :], onec], axis=1)
        for q in range(2):
            hid = dot(lhs, up[:, q * 256 : (q + 1) * 256])
            ac, sl = gelu(hid)
            act[pl.ds(base, T2), q * 256 : (q + 1) * 256] = ac.astype(bf16)
            slp[pl.ds(base, T2), q * 256 : (q + 1) * 256] = sl.astype(bf16)
        return 0

    lax.fori_loop(0, n0 // T2, upf, 0)

    TP = 2 * CW * S

    def sect_norm(lv, s):
        cen = lv.astype(f32) - dot(lv, j1)
        rs1 = lax.rsqrt(dot((cen * cen).astype(bf16), j1) + EPS)
        h1 = cen * rs1
        return h1, rs1, (h1 * sgain[s : s + 1, :].astype(f32)).astype(bf16)

    def dnf(i2, _):
        base = pl.multiple_of(i2 * TP, TP)
        mixed = dot(act[pl.ds(base, TP), :], down[...])
        xs = jnp.concatenate(
            [el[pl.ds((i2 * 2 + a + 3) * CE + 3, CW)].reshape(CW * S, 128) for a in range(2)], axis=0
        ).astype(f32)
        lv = (landb[pl.ds(base, TP), :].astype(f32) * (xs + sc * mixed)).astype(bf16)
        h1, rs1, sn = sect_norm(lv, 0)
        shat[pl.ds(base, TP), :] = h1
        srst[pl.ds(base, TP), :] = rs1
        sn = sn.reshape(2, CW // 2, 2, S, 128)
        pb = pl.multiple_of(i2 * (TP // 4), TP // 4)
        for a in range(2):
            for b in range(2):
                k = 2 * a + b
                p1[pl.ds(pb, TP // 4), k * 128 : (k + 1) * 128] = sn[a, :, b].reshape(TP // 4, 128)
        return 0

    lax.fori_loop(0, I // 2, dnf, 0)

    def to_patches(sn, ii, cc):
        v = sn.reshape(ii // 2, 2, cc // 2, 2, S, 128)
        return jnp.concatenate(
            [v[:, a, :, b].reshape(ii * cc * S // 4, 128) for a in range(2) for b in range(2)], axis=1
        )

    def from_patches(sp, ii, cc):
        ps = [sp[:, k * 128 : (k + 1) * 128].reshape(ii // 2, cc // 2, S, 128) for k in range(4)]
        rows = [jnp.stack([ps[2 * a], ps[2 * a + 1]], axis=2).reshape(ii // 2, cc, S, 128) for a in range(2)]
        return jnp.stack(rows, axis=1).reshape(ii * cc * S, 128)

    def put(at, value, blocks):
        for q in range(blocks):
            sums[at + q * 128 : at + (q + 1) * 128, :] = value[:, q * 128 : (q + 1) * 128].astype(bf16)

    l1 = (dot(p1[...], sw[0]) + sbias[0:1, :].astype(f32)).astype(bf16)
    h1, r1, sn1 = sect_norm(l1, 1)
    P2 = to_patches(sn1, I // 2, CW // 2)
    l2 = (dot(P2, sw[1]) + sbias[1:2, :].astype(f32)).astype(bf16)
    h2, r2, sn2 = sect_norm(l2, 2)
    P3 = to_patches(sn2, I // 4, CW // 4)
    l3 = (dot(P3, sw[2]) + sbias[2:3, :].astype(f32)).astype(bf16)
    bott[...] = l3
    b3 = cot[...]
    put(1024, dot_t(b3, P3), 4)
    u2 = from_patches(dot_r(b3, sw[2]), I // 4, CW // 4) * sgain[2:3, :].astype(f32)
    b2 = norm_bwd(u2, h2, r2, pm).astype(bf16)
    put(512, dot_t(b2, P2), 4)
    u1 = from_patches(dot_r(b2, sw[1]), I // 2, CW // 2) * sgain[1:2, :].astype(f32)
    b1 = norm_bwd(u1, h1, r1, pm).astype(bf16)
    put(0, dot_t(b1, p1[...]), 4)
    back[...] = b1

    downs[...] = jnp.zeros_like(downs)
    ups[...] = jnp.zeros_like(ups)
    T = 256
    TC = T // S

    def bwd(n, _):
        i2 = n // (CW // TC)
        h = n % (CW // TC)
        pb = pl.multiple_of((i2 * (CW // 2) + h * (TC // 2)) * S, T // 2)
        bk = back[pl.ds(pb, T // 2), :]
        for a in range(2):
            base = pl.multiple_of(((i2 * 2 + a) * CW + h * TC) * S, T)
            sp = dot_r(bk, sw[0, a * 256 : (a + 1) * 256, :])
            sp = jnp.stack(
                [sp[:, :128].reshape(TC // 2, S, 128), sp[:, 128:].reshape(TC // 2, S, 128)], axis=1
            ).reshape(T, 128)
            b0 = norm_bwd(sp * sg0, shat[pl.ds(base, T), :], srst[pl.ds(base, T), :], pm).astype(bf16).astype(f32)
            dr = landb[pl.ds(base, T), :].astype(f32) * b0
            dirout[pl.ds(base, T), :] = dr.astype(bf16)
            mg = (dr * sc).astype(bf16)
            downs[...] += dot_t(mg, act[pl.ds(base, T), :])
            hgs = []
            for q in range(2):
                ag = dot_r(mg, down[q * 256 : (q + 1) * 256, :])
                hgs.append((ag * slp[pl.ds(base, T), q * 256 : (q + 1) * 256].astype(f32)).astype(bf16))
            hg = jnp.concatenate(hgs, axis=1)
            ups[...] += dot_t(nrm[pl.ds(base, T), :], hg)
            ng = dot_r(hg, up[0:128, :])
            dg = norm_bwd(ng * g_n, hat[pl.ds(base, T), :], rst[pl.ds(base, T), :], pm)
            gout[pl.ds(base, T), :] = dg.astype(bf16)
        return 0

    lax.fori_loop(0, (I // 2) * (CW // TC), bwd, 0)
    put(1536, downs[...], 4)
    put(2048, ups[...], 4)

    tacc[...] = jnp.zeros_like(tacc)

    def tap(n, _):
        i = n // (CW // 8)
        c0 = (n % (CW // 8)) * 8
        g = [gout[pl.ds((i * CW + c0 + k) * S, S), :].astype(f32) for k in range(8)]
        for a in range(7):
            row = [el[(i + a) * CE + c0 + m].astype(f32) for m in range(14)]
            for b in range(7):
                s = None
                for k in range(8):
                    pr = row[k + b] * g[k]
                    s = pr if s is None else s + pr
                tacc[a * 7 + b] += s[:8] + s[8:]
        return 0

    lax.fori_loop(0, I * (CW // 8), tap, 0)
    ts = [jnp.sum(tacc[t], axis=0, keepdims=True) for t in range(49)]
    ts = jnp.concatenate(ts + [jnp.zeros((15, 128), f32)], axis=0)
    sums[2560:2624, :] = ts.astype(bf16)
    sums[2624:2688, :] = jnp.zeros((64, 128), bf16)

    x2d[0:n0, :] = gout[...].astype(f32)
    for k in range(3):
        first[k] = x2d[pl.ds(k * CW * S, CW, stride=S), :].astype(bf16)
        last[k] = x2d[pl.ds((I - 3 + k) * CW * S + S - 1, CW, stride=S), :].astype(bf16)
    for i in range(I):
        lcol[i * 3 * S : (i + 1) * 3 * S, :] = gout[i * CW * S : (i * CW + 3) * S, :]
        rcol[i * 3 * S : (i + 1) * 3 * S, :] = gout[((i + 1) * CW - 3) * S : (i + 1) * CW * S, :]


def block_pass(field, south, north, left, right, landb, dw, gain, upx, down, scale, sgain, sw, sbias, cot):
    R, CW, C = field.shape
    n = R * CW
    I = R // S
    sd = jax.ShapeDtypeStruct
    out_shape = (
        sd((n // 64, C), bf16),
        sd((n, C), bf16),
        sd((n, C), bf16),
        sd((3, CW, C), bf16),
        sd((3, CW, C), bf16),
        sd((I * 3 * S, C), bf16),
        sd((I * 3 * S, C), bf16),
        sd((2688, C), bf16),
    )
    V = pltpu.VMEM
    scratch = [
        V(((R + 6) * 40, C), f32),
        V(((I + 6) * (CW + 6), S, C), bf16),
        V((49, S, C), f32),
        V((n, C), f32),
        V((n, C), f32),
        V((n, C), f32),
        V((n, C), bf16),
        V((n, 512), bf16),
        V((n, 512), bf16),
        V((n, C), f32),
        V((n, C), f32),
        V((n // 4, 512), bf16),
        V((n // 4, C), bf16),
        V((49, 8, C), f32),
        V((C, 512), f32),
        V((C, 512), f32),
    ]
    return pl.pallas_call(
        functools.partial(block_body, R, CW),
        out_shape=out_shape,
        in_specs=[VMEM] * 15,
        out_specs=[VMEM] * 8,
        scratch_shapes=scratch,
        compiler_params=PARAMS,
        name="block_pass",
    )(field, south, north, left, right, landb, dw, gain, upx, down, scale, sgain, sw, sbias, cot)


def conv_back_body(R, CW, g, dirin, south, north, gl, gr, dw, flag, out, gx, gext, w49, acc):
    I = R // S
    CE = CW + 6
    n0 = R * CW
    isn = flag[...].astype(f32)
    nots = 1.0 - isn
    core = I * 3 * S

    for i in range(I):
        at = (i + 3) * CE * S
        gx[pl.ds(at, 3 * S), :] = gl[i * 3 * S : (i + 1) * 3 * S, :].astype(f32)
        gx[pl.ds(at + 3 * S, CW * S), :] = g[i * CW * S : (i + 1) * CW * S, :].astype(f32)
        gx[pl.ds(at + (3 + CW) * S, 3 * S), :] = gr[i * 3 * S : (i + 1) * 3 * S, :].astype(f32)
    row = lax.broadcasted_iota(jnp.int32, (S, 128), 0)

    for k in range(3):
        sk = jnp.concatenate([gl[core + k * 3 : core + k * 3 + 3, :].astype(f32), south[k].astype(f32), gr[core + k * 3 : core + k * 3 + 3, :].astype(f32)], axis=0)
        nk = jnp.concatenate([gl[core + 9 + k * 3 : core + 12 + k * 3, :].astype(f32), north[k].astype(f32), gr[core + 9 + k * 3 : core + 12 + k * 3, :].astype(f32)], axis=0)
        acc[k * 40 : k * 40 + CE, :] = sk
        acc[(3 + k) * 40 : (3 + k) * 40 + CE, :] = nk
    for k in range(3):
        def lo(c, _, k=k):
            v = gx[pl.ds(((I + k) * CE + c) * S, S), :]
            v = pltpu.roll(v, 1, 0)
            h = acc[pl.ds(k * 40 + c, 1), :]
            gext[k * CE + c] = jnp.where(row == 0, h, v).astype(bf16)
            v = gx[pl.ds(((3 + k) * CE + c) * S, S), :]
            v = pltpu.roll(v, S - 1, 0)
            h = acc[pl.ds((3 + k) * 40 + c, 1), :] * nots
            gext[(I + 3 + k) * CE + c] = jnp.where(row == S - 1, h, v).astype(bf16)
            return 0
        lax.fori_loop(0, CE, lo, 0, unroll=2)

    def cpy(i, _):
        gext[pl.ds((i + 3) * CE, CE)] = gx[pl.ds((i + 3) * CE * S, CE * S), :].astype(bf16).reshape(CE, S, 128)
        return 0

    lax.fori_loop(0, I, cpy, 0)
    weights_table(dw, w49, True)
    fold = []
    for k in range(1, 4):
        s = None
        for rho in range(k - 1, 3):
            a = 5 + k - rho
            for b in range(7):
                pr = acc[pl.ds((3 + rho) * 40 + b, CW), :] * w49[48 - (7 * a + b), 0:1, :]
                s = pr if s is None else s + pr
        fold.append(s * isn)

    def emit(i, c, v):
        at = pl.multiple_of((i * CW + c) * S, S)
        gx[pl.ds(at, S), :] = v + dirin[pl.ds(at, S), :].astype(f32)

    conv49(gext, w49, emit, I, CW)

    def unt(r, _):
        s = r // I
        i = r % I
        out[r] = gx[pl.ds(i * CW * S + s, CW, stride=S), :].astype(bf16)
        return 0

    lax.fori_loop(0, R - 3, unt, 0, unroll=4)
    for k in range(1, 4):
        r = R - k
        v = gx[pl.ds((r % I) * CW * S + r // I, CW, stride=S), :]
        out[r] = (v + fold[k - 1]).astype(bf16)


def conv_back(g, dirin, south, north, gl, gr, dw, flag, R, CW):
    C = g.shape[1]
    I = R // S
    return pl.pallas_call(
        functools.partial(conv_back_body, R, CW),
        out_shape=jax.ShapeDtypeStruct((R, CW, C), bf16),
        in_specs=[VMEM] * 8,
        out_specs=VMEM,
        scratch_shapes=[
            pltpu.VMEM(((I + 6) * (CW + 6) * S, C), f32),
            pltpu.VMEM(((I + 6) * (CW + 6), S, C), bf16),
            pltpu.VMEM((49, S, C), f32),
            pltpu.VMEM((240, C), f32),
        ],
        compiler_params=PARAMS,
        name="conv_back",
    )(g, dirin, south, north, gl, gr, dw, flag)


def finish_body(factor, chunk, idx, mine, other, o_depth, o_up, o_down, o_sec, full):
    core = idx[0]
    place = idx[1]
    half = 4 * chunk
    for j in range(4):
        src = lax.bitwise_xor(place, j)
        at = pl.multiple_of(core * half + j * chunk, 16)
        full[pl.ds(at, chunk), :] = mine[src]
        at = pl.multiple_of((1 - core) * half + j * chunk, 16)
        full[pl.ds(at, chunk), :] = other[src]

    def block(n):
        return full[n * 128 : (n + 1) * 128, :].astype(f32) * factor

    for s in range(3):
        for q in range(4):
            o_sec[s, q * 128 : (q + 1) * 128, :] = block(s * 4 + q).T
    for q in range(4):
        o_down[q * 128 : (q + 1) * 128, :] = block(12 + q).T
        o_up[:, q * 128 : (q + 1) * 128] = block(16 + q)
    o_depth[...] = block(20)[:49, :]


def finish(idx, mine, other, factor):
    chunk = mine.shape[1]
    sd = jax.ShapeDtypeStruct
    return pl.pallas_call(
        functools.partial(finish_body, factor, chunk),
        out_shape=(sd((49, 128), f32), sd((128, 512), f32), sd((512, 128), f32), sd((3, 512, 128), f32)),
        in_specs=[SMEM, VMEM, VMEM],
        out_specs=[VMEM] * 4,
        scratch_shapes=[pltpu.VMEM((8 * chunk, 128), bf16)],
        compiler_params=PARAMS,
        name="finish_sums",
    )(idx, mine, other)


def add_bf(*vals):
    vals = [v.astype(f32) for v in vals]
    while len(vals) > 1:
        vals = [vals[i] + vals[i + 1] for i in range(0, len(vals), 2)]
    return vals[0].astype(bf16)


def flip_pairs(axis, bits):
    return [(i, i ^ bits) for i in range(lax.axis_size(axis))]


def both_pairs(lat_bits, lon_bits):
    nl = lax.axis_size("lon")
    return [
        (a * nl + b, (a ^ lat_bits) * nl + (b ^ lon_bits))
        for a in range(lax.axis_size("lat"))
        for b in range(nl)
    ]


def all_sums(sums):
    lat = lax.axis_index("lat")
    lon = lax.axis_index("lon")
    core = lat % 2
    place = (lat // 2) * 2 + lon % 2
    half = sums.shape[0] // 2
    chunk = half // 4
    keep = lax.dynamic_slice_in_dim(sums, core * half, half, 0)
    away = lax.dynamic_slice_in_dim(sums, (1 - core) * half, half, 0)
    got = lax.ppermute(away, "lat", flip_pairs("lat", 1))
    held = add_bf(keep, got).reshape(4, chunk, 128)
    own = lax.dynamic_index_in_dim(held, place, 0, keepdims=False)
    came = []
    for k in (1, 2, 3):
        part = lax.dynamic_index_in_dim(held, lax.bitwise_xor(place, k), 0, keepdims=False)
        came.append(lax.ppermute(part, ("lat", "lon"), both_pairs((k // 2) * 2, k % 2)))
    total = add_bf(own, *came)
    left = lax.axis_size("lon") // 2
    bit = 2
    while left > 1:
        if left % 4 == 0:
            total = add_bf(total, *[lax.ppermute(total, "lon", flip_pairs("lon", bit * k)) for k in (1, 2, 3)])
            left //= 4
            bit *= 4
        else:
            total = add_bf(total, lax.ppermute(total, "lon", flip_pairs("lon", bit)))
            left //= 2
            bit *= 2
    back = [lax.ppermute(total, ("lat", "lon"), both_pairs((k // 2) * 2, k % 2)) for k in (1, 2, 3)]
    mine = jnp.stack([total, *back])
    other = lax.ppermute(mine, "lat", flip_pairs("lat", 1))
    return jnp.stack([core, place]).astype(jnp.int32), mine, other


def halo_rows(first, last, quot, rem, north):
    nl = lax.axis_size("lon")
    nt = lax.axis_size("lat")
    cols = first.shape[1]
    top = (nt - 1) * nl

    def branch(q):
        def run(first, last):
            up = [(a * nl + b, (a + 1) * nl + b) for a in range(nt - 1) for b in range(nl)]
            down = [(j, i) for i, j in up]
            fa = [(top + e, top + (q - e) % nl) for e in range(nl)]
            fb = [(top + e, top + (q - 1 - e) % nl) for e in range(nl)]
            axes = ("lat", "lon")
            return (
                lax.ppermute(last, axes, up),
                lax.ppermute(first, axes, down),
                lax.ppermute(last, axes, fa),
                lax.ppermute(last, axes, fb),
            )

        return run

    south, above, blk_a, blk_b = lax.switch(quot, [branch(q) for q in range(nl)], first, last)
    both = jnp.concatenate([blk_b, blk_a], axis=1)
    window = lax.dynamic_slice_in_dim(both, rem + 1, cols, 1)
    return south, above, window[:, ::-1]


def shift_pairs(axis, by):
    n = lax.axis_size(axis)
    return [(i, (i + by) % n) for i in range(n)]


def on_device(
    field, land, mirror, depth_weight, norm_gain, up_weight, up_bias, down_proj, layer_scale,
    section_gain, section_weight, section_bias, cotangent,
):
    R, CW, C = field.shape
    I = R // S
    n = R * CW
    total = R * CW * lax.axis_size("lat") * lax.axis_size("lon")
    factor = 1.0 / math.sqrt(total / 64.0)
    north = lax.axis_index("lat") == lax.axis_size("lat") - 1
    quot = mirror[0] // CW
    rem = mirror[0] % CW

    south_f, above_f, fold_f = halo_rows(field[:3], field[R - 3 :], quot, rem, north)
    north_f = jnp.where(north, fold_f[::-1], above_f)

    def edge(lo):
        return jnp.stack(
            [jnp.concatenate([south_f[:, c], field[:, c], north_f[:, c]], axis=0) for c in range(lo, lo + 3)]
        )

    right_f = lax.ppermute(edge(0), "lon", shift_pairs("lon", -1))
    left_f = lax.ppermute(edge(CW - 3), "lon", shift_pairs("lon", 1))

    landb = jnp.broadcast_to(
        land.astype(bf16).reshape(S, I, CW).transpose(1, 2, 0).reshape(n, 1), (n, C)
    )
    upx = jnp.concatenate([up_weight, up_bias[None, :], jnp.zeros((127, up_bias.shape[0]), bf16)], axis=0)
    cot = cotangent.transpose(1, 0, 2).reshape(n // 64, C)
    bott, g, direct, first, last, lcol, rcol, sums = block_pass(
        field, south_f, north_f, left_f, right_f, landb, depth_weight, norm_gain[None, :], upx, down_proj,
        layer_scale[None, :], section_gain, section_weight, section_bias, cot,
    )
    level = bott.reshape(CW // 8, S, C).transpose(1, 0, 2)

    south_g, above_g, fold_g = halo_rows(first, last, quot, rem, north)
    north_g = jnp.where(north, fold_g, above_g)

    def pack(cols, lo):
        return jnp.concatenate(
            [cols, south_g[:, lo : lo + 3].reshape(9, C), north_g[:, lo : lo + 3].reshape(9, C)], axis=0
        )

    gr = lax.ppermute(pack(lcol, 0), "lon", shift_pairs("lon", -1))
    gl = lax.ppermute(pack(rcol, CW - 3), "lon", shift_pairs("lon", 1))
    flag = jnp.broadcast_to(north.astype(bf16), (1, C))
    idx, mine, other = all_sums(sums)
    grad_field = conv_back(g, direct, south_g, north_g, gl, gr, depth_weight, flag, R, CW)
    g_depth, g_up, g_down, g_sec = finish(idx, mine, other, factor)
    return level, grad_field, g_depth, g_up, g_down, g_sec


def solution(mesh):
    cells = P("lat", "lon", None)
    in_specs = (cells, P("lat", "lon")) + (P(),) * 10 + (cells,)
    out_specs = (cells, cells, P(), P(), P(), P())
    return jax.shard_map(on_device, mesh=mesh, in_specs=in_specs, out_specs=out_specs, check_vma=False)
```

```python
import functools
import math

import jax
import jax.numpy as jnp
from jax import lax
from jax.experimental import pallas as pl
from jax.experimental.pallas import tpu as pltpu
from jax.sharding import PartitionSpec as P

SECTIONS = 3
EPS = 1e-6
f32, bf16 = jnp.float32, jnp.bfloat16
S = 16
LOG2E = 1.4426950408889634
VMEM = pl.BlockSpec(memory_space=pltpu.VMEM)
SMEM = pl.BlockSpec(memory_space=pltpu.SMEM)
PARAMS = pltpu.CompilerParams(vmem_limit_bytes=60 * 2**20)
SMALL = pltpu.CompilerParams(vmem_limit_bytes=24 * 2**20)


def dot(a, b):
    return jnp.dot(a, b, preferred_element_type=f32)


def dot_t(a, b):
    return lax.dot_general(a, b, (((0,), (0,)), ((), ())), preferred_element_type=f32)


def dot_r(a, b):
    return lax.dot_general(a, b, (((1,), (1,)), ((), ())), preferred_element_type=f32)


def ones_mean(n):
    return jnp.full((n, 128), 1.0 / 128, bf16)


def pair_mean():
    r = lax.broadcasted_iota(jnp.int32, (256, 256), 0) // 128
    c = lax.broadcasted_iota(jnp.int32, (256, 256), 1) // 128
    return jnp.where(r == c, 1.0 / 128, 0.0).astype(bf16)


def split2(x):
    hi = x.astype(bf16)
    lo = (x - hi.astype(f32)).astype(bf16)
    return jnp.concatenate([hi, lo], axis=1)


def norm_bwd(u, hat, rstd, pm):
    m = dot(jnp.concatenate([u.astype(bf16), (u * hat).astype(bf16)], axis=1), pm)
    return rstd * (u - m[:, :128] - hat * m[:, 128:])


def gelu(h):
    cdf = 0.5 + 0.5 * lax.erf(h * 0.7071067811865476)
    e = jnp.exp2(h * h * (-0.5 * LOG2E))
    return h * cdf, cdf + h * (e * 0.3989422804014327)


def weights_table(dw, w49, flip):
    for t in range(49):
        w49[48 - t if flip else t] = jnp.broadcast_to(dw[t : t + 1, :].astype(f32), (S, 128)).astype(w49.dtype)


def conv49(el, w49, emit, I, CW):
    CE = CW + 6
    CG = 4

    def step(n, _):
        i = n // (CW // CG)
        c0 = (n % (CW // CG)) * CG
        acc = [None] * CG
        for a in range(7):
            row = [el[(i + a) * CE + c0 + m].astype(f32) for m in range(CG + 6)]
            for b in range(7):
                w = w49[a * 7 + b].astype(f32)
                for k in range(CG):
                    pr = row[k + b] * w
                    acc[k] = pr if acc[k] is None else acc[k] + pr
        for k in range(CG):
            emit(i, c0 + k, acc[k])
        return 0

    lax.fori_loop(0, I * (CW // CG), step, 0)


def block_body(
    R, CW,
    field, south, north, left, right, landb, dw, gain, up, down, scale, sgain, sw, sbias, cot,
    bott, gout, dirout, first, last, lcol, rcol, sums,
    x2d, el, w49, dep, hat, rst, nrm, act, slp, shat, srst, p1, back, tacc, downs, ups, mgs,
):
    I = R // S
    CE = CW + 6
    XW = 40
    n0 = R * CW

    def asm(r, _):
        x2d[pl.ds((r + 3) * XW + (r + 3) // I + 3, CW), :] = field[r].astype(f32)
        return 0

    lax.fori_loop(0, R, asm, 0, unroll=4)
    PB = I * XW + 1
    for k in range(3):
        x2d[pl.ds(k * XW + 3, CW), :] = south[k].astype(f32)
        x2d[pl.ds((R + 3 + k) * XW + (R + 3 + k) // I + 3, CW), :] = north[k].astype(f32)
        for m in range((R + 6 + I - 1) // I):
            rows = min(I, R + 6 - m * I)
            x2d[pl.ds(m * PB + k, rows, stride=XW), :] = left[k, m * I : m * I + rows, :].astype(f32)
            x2d[pl.ds(m * PB + CW + 3 + k, rows, stride=XW), :] = right[k, m * I : m * I + rows, :].astype(f32)

    def tr(i, _):
        for c in range(CE):
            el[i * CE + c] = x2d[pl.ds(i * XW + i // I + c, S, stride=PB), :].astype(bf16)
        return 0

    lax.fori_loop(0, I + 6, tr, 0)
    weights_table(dw, w49, False)

    def emit(i, c, v):
        dep[pl.ds((i * CW + c) * S, S), :] = v

    conv49(el, w49, emit, I, CW)

    jj, j1, pm = ones_mean(256), ones_mean(128), pair_mean()
    g_n = gain[...].astype(f32)
    sc = scale[...].astype(f32)
    sg0 = sgain[0:1, :].astype(f32)
    T1 = 1024

    def nfwd(n, _):
        base = pl.multiple_of(n * T1, T1)
        x = dep[pl.ds(base, T1), :]
        cen = x - dot(split2(x), jj)
        rs = lax.rsqrt(dot((cen * cen).astype(bf16), j1) + EPS)
        ht = cen * rs
        hat[pl.ds(base, T1), :] = ht
        rst[pl.ds(base, T1), :] = rs
        nrm[pl.ds(base, T1), :] = (ht * g_n).astype(bf16)
        return 0

    lax.fori_loop(0, n0 // T1, nfwd, 0)

    T2 = 512
    onec = (lax.broadcasted_iota(jnp.int32, (T2, 128), 1) == 0).astype(f32).astype(bf16)

    def upf(n, _):
        base = pl.multiple_of(n * T2, T2)
        lhs = jnp.concatenate([nrm[pl.ds(base, T2), :], onec], axis=1)
        for q in range(2):
            hid = dot(lhs, up[:, q * 256 : (q + 1) * 256])
            ac, sl = gelu(hid)
            act[pl.ds(base, T2), q * 256 : (q + 1) * 256] = ac.astype(bf16)
            slp[pl.ds(base, T2), q * 256 : (q + 1) * 256] = sl.astype(bf16)
        return 0

    lax.fori_loop(0, n0 // T2, upf, 0)

    TP = 2 * CW * S

    def sect_norm(lv, s):
        cen = lv.astype(f32) - dot(lv, j1)
        rs1 = lax.rsqrt(dot((cen * cen).astype(bf16), j1) + EPS)
        h1 = cen * rs1
        return h1, rs1, (h1 * sgain[s : s + 1, :].astype(f32)).astype(bf16)

    def dnf(i2, _):
        base = pl.multiple_of(i2 * TP, TP)
        mixed = dot(act[pl.ds(base, TP), :], down[...])
        xs = jnp.concatenate(
            [el[pl.ds((i2 * 2 + a + 3) * CE + 3, CW)].reshape(CW * S, 128) for a in range(2)], axis=0
        ).astype(f32)
        lv = (landb[pl.ds(base, TP), :].astype(f32) * (xs + sc * mixed)).astype(bf16)
        h1, rs1, sn = sect_norm(lv, 0)
        shat[pl.ds(base, TP), :] = h1
        srst[pl.ds(base, TP), :] = rs1
        sn = sn.reshape(2, CW // 2, 2, S, 128)
        pb = pl.multiple_of(i2 * (TP // 4), TP // 4)
        for a in range(2):
            for b in range(2):
                k = 2 * a + b
                p1[pl.ds(pb, TP // 4), k * 128 : (k + 1) * 128] = sn[a, :, b].reshape(TP // 4, 128)
        return 0

    lax.fori_loop(0, I // 2, dnf, 0)

    def to_patches(sn, ii, cc):
        v = sn.reshape(ii // 2, 2, cc // 2, 2, S, 128)
        return jnp.concatenate(
            [v[:, a, :, b].reshape(ii * cc * S // 4, 128) for a in range(2) for b in range(2)], axis=1
        )

    def from_patches(sp, ii, cc):
        ps = [sp[:, k * 128 : (k + 1) * 128].reshape(ii // 2, cc // 2, S, 128) for k in range(4)]
        rows = [jnp.stack([ps[2 * a], ps[2 * a + 1]], axis=2).reshape(ii // 2, cc, S, 128) for a in range(2)]
        return jnp.stack(rows, axis=1).reshape(ii * cc * S, 128)

    def put(at, value, blocks):
        for q in range(blocks):
            sums[at + q * 128 : at + (q + 1) * 128, :] = value[:, q * 128 : (q + 1) * 128].astype(bf16)

    l1 = (dot(p1[...], sw[0]) + sbias[0:1, :].astype(f32)).astype(bf16)
    h1, r1, sn1 = sect_norm(l1, 1)
    P2 = to_patches(sn1, I // 2, CW // 2)
    l2 = (dot(P2, sw[1]) + sbias[1:2, :].astype(f32)).astype(bf16)
    h2, r2, sn2 = sect_norm(l2, 2)
    P3 = to_patches(sn2, I // 4, CW // 4)
    l3 = (dot(P3, sw[2]) + sbias[2:3, :].astype(f32)).astype(bf16)
    bott[...] = l3
    b3 = cot[...]
    put(1024, dot_t(b3, P3), 4)
    u2 = from_patches(dot_r(b3, sw[2]), I // 4, CW // 4) * sgain[2:3, :].astype(f32)
    b2 = norm_bwd(u2, h2, r2, pm).astype(bf16)
    put(512, dot_t(b2, P2), 4)
    u1 = from_patches(dot_r(b2, sw[1]), I // 2, CW // 2) * sgain[1:2, :].astype(f32)
    b1 = norm_bwd(u1, h1, r1, pm).astype(bf16)
    put(0, dot_t(b1, p1[...]), 4)
    back[...] = b1

    QP = TP // 4

    def bk1(i2, _):
        pb = pl.multiple_of(i2 * QP, QP)
        bk = back[pl.ds(pb, QP), :]
        base = pl.multiple_of(i2 * TP, TP)
        us = []
        for a in range(2):
            sp = dot_r(bk, sw[0, a * 256 : (a + 1) * 256, :])
            us.append(
                jnp.stack(
                    [sp[:, :128].reshape(CW // 2, S, 128), sp[:, 128:].reshape(CW // 2, S, 128)], axis=1
                ).reshape(TP // 2, 128)
            )
        u = jnp.concatenate(us, axis=0) * sg0
        b0 = norm_bwd(u, shat[pl.ds(base, TP), :], srst[pl.ds(base, TP), :], pm).astype(bf16).astype(f32)
        dr = landb[pl.ds(base, TP), :].astype(f32) * b0
        dirout[pl.ds(base, TP), :] = dr.astype(bf16)
        mgs[pl.ds(base, TP), :] = (dr * sc).astype(bf16)
        return 0

    lax.fori_loop(0, I // 2, bk1, 0)

    def bk2(n, _):
        base = pl.multiple_of(n * T2, T2)
        mg = mgs[pl.ds(base, T2), :]
        for q in range(2):
            ag = dot_r(mg, down[q * 256 : (q + 1) * 256, :])
            sl = slp[pl.ds(base, T2), q * 256 : (q + 1) * 256].astype(f32)
            slp[pl.ds(base, T2), q * 256 : (q + 1) * 256] = (ag * sl).astype(bf16)
        return 0

    lax.fori_loop(0, n0 // T2, bk2, 0)

    def bk3(n, _):
        base = pl.multiple_of(n * T1, T1)
        ng = dot_r(slp[pl.ds(base, T1), :], up[0:128, :])
        dg = norm_bwd(ng * g_n, hat[pl.ds(base, T1), :], rst[pl.ds(base, T1), :], pm)
        gout[pl.ds(base, T1), :] = dg.astype(bf16)
        return 0

    lax.fori_loop(0, n0 // T1, bk3, 0)
    downs[...] = dot_t(mgs[...], act[...])
    ups[...] = dot_t(nrm[...], slp[...])
    put(1536, downs[...], 4)
    put(2048, ups[...], 4)

    tacc[...] = jnp.zeros_like(tacc)

    def tap(n, _):
        i = n // (CW // 8)
        c0 = (n % (CW // 8)) * 8
        g = [gout[pl.ds((i * CW + c0 + k) * S, S), :].astype(f32) for k in range(8)]
        for a in range(7):
            row = [el[(i + a) * CE + c0 + m].astype(f32) for m in range(14)]
            for b in range(7):
                s = None
                for k in range(8):
                    pr = row[k + b] * g[k]
                    s = pr if s is None else s + pr
                tacc[a * 7 + b] += s[:8] + s[8:]
        return 0

    lax.fori_loop(0, I * (CW // 8), tap, 0)
    ts = [jnp.sum(tacc[t], axis=0, keepdims=True) for t in range(49)]
    ts = jnp.concatenate(ts + [jnp.zeros((15, 128), f32)], axis=0)
    sums[2560:2624, :] = ts.astype(bf16)
    sums[2624:2688, :] = jnp.zeros((64, 128), bf16)

    x2d[0:n0, :] = gout[...].astype(f32)
    for k in range(3):
        first[k] = x2d[pl.ds(k * CW * S, CW, stride=S), :].astype(bf16)
        last[k] = x2d[pl.ds((I - 3 + k) * CW * S + S - 1, CW, stride=S), :].astype(bf16)
    for i in range(I):
        lcol[i * 3 * S : (i + 1) * 3 * S, :] = gout[i * CW * S : (i * CW + 3) * S, :]
        rcol[i * 3 * S : (i + 1) * 3 * S, :] = gout[((i + 1) * CW - 3) * S : (i + 1) * CW * S, :]


def block_pass(field, south, north, left, right, landb, dw, gain, upx, down, scale, sgain, sw, sbias, cot):
    R, CW, C = field.shape
    n = R * CW
    I = R // S
    sd = jax.ShapeDtypeStruct
    out_shape = (
        sd((n // 64, C), bf16),
        sd((n, C), bf16),
        sd((n, C), bf16),
        sd((3, CW, C), bf16),
        sd((3, CW, C), bf16),
        sd((I * 3 * S, C), bf16),
        sd((I * 3 * S, C), bf16),
        sd((2688, C), bf16),
    )
    V = pltpu.VMEM
    scratch = [
        V(((R + 6) * 40 + (R + 6) // I + 16, C), f32),
        V(((I + 6) * (CW + 6), S, C), bf16),
        V((49, S, C), bf16),
        V((n, C), f32),
        V((n, C), f32),
        V((n, C), f32),
        V((n, C), bf16),
        V((n, 512), bf16),
        V((n, 512), bf16),
        V((n, C), f32),
        V((n, C), f32),
        V((n // 4, 512), bf16),
        V((n // 4, C), bf16),
        V((49, 8, C), f32),
        V((C, 512), f32),
        V((C, 512), f32),
        V((n, C), bf16),
    ]
    return pl.pallas_call(
        functools.partial(block_body, R, CW),
        out_shape=out_shape,
        in_specs=[VMEM] * 15,
        out_specs=[VMEM] * 8,
        scratch_shapes=scratch,
        compiler_params=PARAMS,
        name="block_pass",
    )(field, south, north, left, right, landb, dw, gain, upx, down, scale, sgain, sw, sbias, cot)


def conv_back_body(R, CW, g, dirin, dw, out, gx, gext, w49):
    I = R // S
    CE = CW + 6
    row = lax.broadcasted_iota(jnp.int32, (S, 128), 0)
    zero = jnp.zeros((3, S, 128), bf16)

    def cpy(i, _):
        gext[pl.ds((i + 3) * CE, 3)] = zero
        gext[pl.ds((i + 3) * CE + 3, CW)] = g[pl.ds(pl.multiple_of(i * CW * S, CW * S), CW * S), :].reshape(CW, S, 128)
        gext[pl.ds((i + 3) * CE + 3 + CW, 3)] = zero
        return 0

    lax.fori_loop(0, I, cpy, 0)
    for k in range(3):

        def shift(c, _, k=k):
            v = pltpu.roll(gext[(I + k) * CE + c].astype(f32), 1, 0)
            gext[k * CE + c] = jnp.where(row == 0, 0.0, v).astype(bf16)
            v = pltpu.roll(gext[(3 + k) * CE + c].astype(f32), S - 1, 0)
            gext[(I + 3 + k) * CE + c] = jnp.where(row == S - 1, 0.0, v).astype(bf16)
            return 0

        lax.fori_loop(0, CE, shift, 0, unroll=2)
    weights_table(dw, w49, True)

    def emit(i, c, v):
        at = pl.multiple_of((i * CW + c) * S, S)
        out[pl.ds(at, S), :] = v + dirin[pl.ds(at, S), :].astype(f32)

    conv49(gext, w49, emit, I, CW)


def conv_back(g, dirin, dw, R, CW):
    C = g.shape[1]
    I = R // S
    return pl.pallas_call(
        functools.partial(conv_back_body, R, CW),
        out_shape=jax.ShapeDtypeStruct((R * CW, C), f32),
        in_specs=[VMEM] * 3,
        out_specs=VMEM,
        scratch_shapes=[
            pltpu.VMEM((8, C), f32),
            pltpu.VMEM(((I + 6) * (CW + 6), S, C), bf16),
            pltpu.VMEM((49, S, C), bf16),
        ],
        compiler_params=SMALL,
        cost_estimate=pl.CostEstimate(flops=10**8, bytes_accessed=30 * 2**20, transcendentals=0),
        name="conv_back",
    )(g, dirin, dw)


def edges_body(R, CW, base, south, north, gl, gr, dw, flag, out, acc, rows, cols, w49):
    I = R // S
    CE = CW + 6
    isn = flag[...].astype(f32)
    nots = 1.0 - isn
    core = I * 3 * S
    row = lax.broadcasted_iota(jnp.int32, (S, 128), 0)
    for t in range(49):
        w49[t] = jnp.broadcast_to(dw[t : t + 1, :].astype(f32), (S, 128))
    for side in range(2):
        for k in range(3):
            at = core + side * 9 + k * 3
            mid = (north if side else south)[k]
            rows[pl.ds((side * 3 + k) * 40, CE), :] = jnp.concatenate(
                [gl[at : at + 3, :], mid, gr[at : at + 3, :]], axis=0
            ).astype(f32)

    def taps(k, a, flip):
        s = None
        for b in range(7):
            o = 6 - b if flip else b
            pr = rows[pl.ds(k * 40 + o, CW), :] * w49[7 * a + b, 0:1, :]
            s = pr if s is None else s + pr
        return s

    low = []
    for r in range(3):
        low.append(sum(taps(k, r + 6 - k, True) for k in range(r, 3)))
    high = []
    for t in range(3):
        v = sum(taps(3 + k, 2 - t - k, True) for k in range(3 - t)) * nots
        k1 = t + 1
        f = sum(taps(3 + rho, 5 + k1 - rho, False) for rho in range(k1 - 1, 3)) * isn
        high.append(v + f)
    for side in range(2):
        src = gr if side else gl

        def fill(i, _, src=src, side=side):
            for j in range(3):
                at = pl.multiple_of((i * 3 + j) * S, S)
                cols[side * (I + 6) * 3 + (i + 3) * 3 + j] = src[pl.ds(at, S), :].astype(f32)
            return 0

        lax.fori_loop(0, I, fill, 0)
        for k in range(3):
            for j in range(3):
                at = side * (I + 6) * 3
                v = pltpu.roll(cols[at + (I + k) * 3 + j], 1, 0)
                cols[at + k * 3 + j] = jnp.where(row == 0, 0.0, v)
                v = pltpu.roll(cols[at + (3 + k) * 3 + j], S - 1, 0)
                cols[at + (I + 3 + k) * 3 + j] = jnp.where(row == S - 1, 0.0, v)

    PITCH = CW * S

    def step(i, _):
        at = pl.multiple_of(i * PITCH, PITCH)
        acc[pl.ds(at, PITCH), :] = base[pl.ds(at, PITCH), :]
        for side in range(2):
            for t in range(3):
                s = None
                for j in range(3):
                    b = 2 - t - j if side else t + 6 - j
                    if b < 0 or b > 6:
                        continue
                    for a in range(7):
                        pr = cols[side * (I + 6) * 3 + (i + 6 - a) * 3 + j] * w49[7 * a + b]
                        s = pr if s is None else s + pr
                c = CW - 1 - t if side else t
                at = pl.multiple_of(i * PITCH + c * S, S)
                acc[pl.ds(at, S), :] += s
        return 0

    lax.fori_loop(0, I, step, 0)

    def unt(r, _):
        s = r // I
        i = r % I
        out[r] = acc[pl.ds(i * PITCH + s, CW, stride=S), :].astype(bf16)
        return 0

    lax.fori_loop(3, R - 3, unt, 0, unroll=2)
    for r in list(range(3)) + list(range(R - 3, R)):
        v = acc[pl.ds((r % I) * PITCH + r // I, CW, stride=S), :]
        v = v + (low[r] if r < 3 else high[R - 1 - r])
        out[r] = v.astype(bf16)


def edges(base, south, north, gl, gr, dw, flag, R, CW):
    C = base.shape[1]
    I = R // S
    return pl.pallas_call(
        functools.partial(edges_body, R, CW),
        out_shape=jax.ShapeDtypeStruct((R, CW, C), bf16),
        in_specs=[VMEM] * 7,
        out_specs=VMEM,
        scratch_shapes=[
            pltpu.VMEM((R * CW, C), f32),
            pltpu.VMEM((240, C), f32),
            pltpu.VMEM((2 * (I + 6) * 3, S, C), f32),
            pltpu.VMEM((49, S, C), f32),
        ],
        compiler_params=SMALL,
        cost_estimate=pl.CostEstimate(flops=10**8, bytes_accessed=10 * 2**20, transcendentals=0),
        name="edges",
    )(base, south, north, gl, gr, dw, flag)


def finish_body(factor, chunk, idx, mine, other, o_depth, o_up, o_down, o_sec, full):
    core = idx[0]
    place = idx[1]
    half = 4 * chunk
    for j in range(4):
        src = lax.bitwise_xor(place, j)
        at = pl.multiple_of(core * half + j * chunk, 16)
        full[pl.ds(at, chunk), :] = mine[src]
        at = pl.multiple_of((1 - core) * half + j * chunk, 16)
        full[pl.ds(at, chunk), :] = other[src]

    def block(n):
        return full[n * 128 : (n + 1) * 128, :].astype(f32) * factor

    for s in range(3):
        for q in range(4):
            o_sec[s, q * 128 : (q + 1) * 128, :] = block(s * 4 + q).T
    for q in range(4):
        o_down[q * 128 : (q + 1) * 128, :] = block(12 + q).T
        o_up[:, q * 128 : (q + 1) * 128] = block(16 + q)
    o_depth[...] = block(20)[:49, :]


def finish(idx, mine, other, factor):
    chunk = mine.shape[1]
    sd = jax.ShapeDtypeStruct
    return pl.pallas_call(
        functools.partial(finish_body, factor, chunk),
        out_shape=(sd((49, 128), f32), sd((128, 512), f32), sd((512, 128), f32), sd((3, 512, 128), f32)),
        in_specs=[SMEM, VMEM, VMEM],
        out_specs=[VMEM] * 4,
        scratch_shapes=[pltpu.VMEM((8 * chunk, 128), bf16)],
        compiler_params=PARAMS,
        name="finish_sums",
    )(idx, mine, other)


def add_bf(*vals):
    vals = [v.astype(f32) for v in vals]
    while len(vals) > 1:
        vals = [vals[i] + vals[i + 1] for i in range(0, len(vals), 2)]
    return vals[0].astype(bf16)


def flip_pairs(axis, bits):
    return [(i, i ^ bits) for i in range(lax.axis_size(axis))]


def both_pairs(lat_bits, lon_bits):
    nl = lax.axis_size("lon")
    return [
        (a * nl + b, (a ^ lat_bits) * nl + (b ^ lon_bits))
        for a in range(lax.axis_size("lat"))
        for b in range(nl)
    ]


def square_pairs(k):
    return both_pairs((k // 2) * 2, k % 2)


def sums_core(sums, core):
    half = sums.shape[0] // 2
    keep = lax.dynamic_slice_in_dim(sums, core * half, half, 0)
    away = lax.dynamic_slice_in_dim(sums, (1 - core) * half, half, 0)
    return add_bf(keep, lax.ppermute(away, "lat", flip_pairs("lat", 1))).reshape(4, half // 4, -1)


def square_sum(held, place):
    own = lax.dynamic_index_in_dim(held, place, 0, keepdims=False)
    came = []
    for k in (1, 2, 3):
        part = lax.dynamic_index_in_dim(held, lax.bitwise_xor(place, k), 0, keepdims=False)
        came.append(lax.ppermute(part, ("lat", "lon"), square_pairs(k)))
    return add_bf(own, *came)


def line_sum(total):
    left = lax.axis_size("lon") // 2
    bit = 2
    while left > 1:
        if left % 4 == 0:
            total = add_bf(total, *[lax.ppermute(total, "lon", flip_pairs("lon", bit * k)) for k in (1, 2, 3)])
            left //= 4
            bit *= 4
        else:
            total = add_bf(total, lax.ppermute(total, "lon", flip_pairs("lon", bit)))
            left //= 2
            bit *= 2
    return total


def halo_rows(first, last, quot, rem):
    nl = lax.axis_size("lon")
    nt = lax.axis_size("lat")
    lat = lax.axis_index("lat")
    odd = lat % 2 == 1
    cols = first.shape[1]
    top = (nt - 1) * nl
    axes = ("lat", "lon")
    near = lax.ppermute(jnp.where(odd, first, last), "lat", flip_pairs("lat", 1))
    send = jnp.where(odd, last, first)
    swap = [(a * nl + e, (a + 1) * nl + e) for a in range(1, nt - 1, 2) for e in range(nl)]
    swap += [(j, i) for i, j in swap]

    def branch(q):
        def run(send, last):
            fa = [(top + e, top + (q - e) % nl) for e in range(nl)]
            fb = [(top + e, top + (q - 1 - e) % nl) for e in range(nl)]
            return lax.ppermute(send, axes, swap + fa), lax.ppermute(last, axes, fb)

        return run

    far, blk_b = lax.switch(quot, [branch(q) for q in range(nl)], send, last)
    south = jnp.where(odd, near, far)
    both = jnp.concatenate([blk_b, far], axis=1)
    window = lax.dynamic_slice_in_dim(both, rem + 1, cols, 1)
    return south, jnp.where(odd, far, near), window[:, ::-1]


def shift_pairs(axis, by):
    n = lax.axis_size(axis)
    return [(i, (i + by) % n) for i in range(n)]


def on_device(
    field, land, mirror, depth_weight, norm_gain, up_weight, up_bias, down_proj, layer_scale,
    section_gain, section_weight, section_bias, cotangent,
):
    R, CW, C = field.shape
    I = R // S
    n = R * CW
    total = R * CW * lax.axis_size("lat") * lax.axis_size("lon")
    factor = 1.0 / math.sqrt(total / 64.0)
    north = lax.axis_index("lat") == lax.axis_size("lat") - 1
    quot = mirror[0] // CW
    rem = mirror[0] % CW

    south_f, above_f, fold_f = halo_rows(field[:3], field[R - 3 :], quot, rem)
    north_f = jnp.where(north, fold_f[::-1], above_f)

    def edge(lo):
        return jnp.stack(
            [jnp.concatenate([south_f[:, c], field[:, c], north_f[:, c]], axis=0) for c in range(lo, lo + 3)]
        )

    right_f = lax.ppermute(edge(0), "lon", shift_pairs("lon", -1))
    left_f = lax.ppermute(edge(CW - 3), "lon", shift_pairs("lon", 1))

    landb = jnp.broadcast_to(
        land.astype(bf16).reshape(S, I, CW).transpose(1, 2, 0).reshape(n, 1), (n, C)
    )
    upx = jnp.concatenate([up_weight, up_bias[None, :], jnp.zeros((127, up_bias.shape[0]), bf16)], axis=0)
    cot = cotangent.transpose(1, 0, 2).reshape(n // 64, C)
    bott, g, direct, first, last, lcol, rcol, sums = block_pass(
        field, south_f, north_f, left_f, right_f, landb, depth_weight, norm_gain[None, :], upx, down_proj,
        layer_scale[None, :], section_gain, section_weight, section_bias, cot,
    )
    level = bott.reshape(CW // 8, S, C).transpose(1, 0, 2)

    core = lax.axis_index("lat") % 2
    place = (lax.axis_index("lat") // 2) * 2 + lax.axis_index("lon") % 2
    held = sums_core(sums, core)

    south_g, above_g, fold_g = halo_rows(first, last, quot, rem)
    north_g = jnp.where(north, fold_g, above_g)

    def pack(cols, lo):
        return jnp.concatenate(
            [cols, south_g[:, lo : lo + 3].reshape(9, C), north_g[:, lo : lo + 3].reshape(9, C)], axis=0
        )

    gr = lax.ppermute(pack(lcol, 0), "lon", shift_pairs("lon", -1))
    gl = lax.ppermute(pack(rcol, CW - 3), "lon", shift_pairs("lon", 1))
    flag = jnp.broadcast_to(north.astype(bf16), (1, C))
    held, south_g = lax.optimization_barrier((held, south_g))
    chunk = square_sum(held, place)
    g, _ = lax.optimization_barrier((g, south_g))
    base = conv_back(g, direct, depth_weight, R, CW)
    chunk, base = lax.optimization_barrier((chunk, base))
    chunk = line_sum(chunk)
    grad_field = edges(base, south_g, north_g, gl, gr, depth_weight, flag, R, CW)
    chunk, grad_field = lax.optimization_barrier((chunk, grad_field))
    axes = ("lat", "lon")
    mine = jnp.stack([chunk] + [lax.ppermute(chunk, axes, square_pairs(k)) for k in (1, 2, 3)])
    other = lax.ppermute(mine, "lat", flip_pairs("lat", 1))
    idx = jnp.stack([core, place]).astype(jnp.int32)
    g_depth, g_up, g_down, g_sec = finish(idx, mine, other, factor)
    return level, grad_field, g_depth, g_up, g_down, g_sec


def solution(mesh):
    cells = P("lat", "lon", None)
    in_specs = (cells, P("lat", "lon")) + (P(),) * 10 + (cells,)
    out_specs = (cells, cells, P(), P(), P(), P())
    return jax.shard_map(on_device, mesh=mesh, in_specs=in_specs, out_specs=out_specs, check_vma=False)
```

```python
import functools
import math

import jax
import jax.numpy as jnp
from jax import lax
from jax.experimental import pallas as pl
from jax.experimental.pallas import tpu as pltpu
from jax.sharding import PartitionSpec as P

SECTIONS = 3
EPS = 1e-6
f32, bf16 = jnp.float32, jnp.bfloat16
S = 16
LOG2E = 1.4426950408889634
HALF = 1344
VMEM = pl.BlockSpec(memory_space=pltpu.VMEM)
SMEM = pl.BlockSpec(memory_space=pltpu.SMEM)
PARAMS = pltpu.CompilerParams(vmem_limit_bytes=60 * 2**20)
SMALL = pltpu.CompilerParams(vmem_limit_bytes=24 * 2**20)


def dot(a, b):
    return jnp.dot(a, b, preferred_element_type=f32)


def dot_t(a, b):
    return lax.dot_general(a, b, (((0,), (0,)), ((), ())), preferred_element_type=f32)


def dot_r(a, b):
    return lax.dot_general(a, b, (((1,), (1,)), ((), ())), preferred_element_type=f32)


def ones_mean(n):
    return jnp.full((n, 128), 1.0 / 128, bf16)


def pair_mean():
    r = lax.broadcasted_iota(jnp.int32, (256, 256), 0) // 128
    c = lax.broadcasted_iota(jnp.int32, (256, 256), 1) // 128
    return jnp.where(r == c, 1.0 / 128, 0.0).astype(bf16)


def split2(x):
    hi = x.astype(bf16)
    lo = (x - hi.astype(f32)).astype(bf16)
    return jnp.concatenate([hi, lo], axis=1)


def norm_bwd(u, hat, rstd, pm):
    m = dot(jnp.concatenate([u.astype(bf16), (u * hat).astype(bf16)], axis=1), pm)
    return rstd * (u - m[:, :128] - hat * m[:, 128:])


def gelu(h):
    cdf = 0.5 + 0.5 * lax.erf(h * 0.7071067811865476)
    e = jnp.exp2(h * h * (-0.5 * LOG2E))
    return h * cdf, cdf + h * (e * 0.3989422804014327)


def weights_table(dw, w49, flip):
    for t in range(49):
        w49[48 - t if flip else t] = jnp.broadcast_to(dw[t : t + 1, :].astype(f32), (S, 128)).astype(w49.dtype)


def conv49(el, w49, emit, I, CW):
    CE = CW + 6
    CG = 4

    def step(n, _):
        i = n // (CW // CG)
        c0 = (n % (CW // CG)) * CG
        acc = [None] * CG
        for a in range(7):
            row = [el[(i + a) * CE + c0 + m].astype(f32) for m in range(CG + 6)]
            for b in range(7):
                w = w49[a * 7 + b].astype(f32)
                for k in range(CG):
                    pr = row[k + b] * w
                    acc[k] = pr if acc[k] is None else acc[k] + pr
        for k in range(CG):
            emit(i, c0 + k, acc[k])
        return 0

    lax.fori_loop(0, I * (CW // CG), step, 0)


def block_body(
    R, CW,
    field, south, north, left, right, land, dw, gain, upw, bias, down, scale, sgain, sw, sbias, cot,
    bott, gout, dirout, send, last, lcol, rcol, keep, away,
    x2d, el, w49, dep, hat, rst, nrm, act, slp, shat, srst, p1, back, tacc, downs, ups, mgs, landb, up, sums,
):
    I = R // S
    CE = CW + 6
    XW = 40
    n0 = R * CW

    def asm(r, _):
        x2d[pl.ds((r + 3) * XW + (r + 3) // I + 3, CW), :] = field[r].astype(f32)
        return 0

    lax.fori_loop(0, R, asm, 0, unroll=4)
    PB = I * XW + 1
    for k in range(3):
        x2d[pl.ds(k * XW + 3, CW), :] = south[k].astype(f32)
        x2d[pl.ds((R + 3 + k) * XW + (R + 3 + k) // I + 3, CW), :] = north[k].astype(f32)
        for m in range((R + 6 + I - 1) // I):
            rows = min(I, R + 6 - m * I)
            x2d[pl.ds(m * PB + k, rows, stride=XW), :] = left[k, m * I : m * I + rows, :].astype(f32)
            x2d[pl.ds(m * PB + CW + 3 + k, rows, stride=XW), :] = right[k, m * I : m * I + rows, :].astype(f32)

    def tr(i, _):
        for c in range(CE):
            el[i * CE + c] = x2d[pl.ds(i * XW + i // I + c, S, stride=PB), :].astype(bf16)
        return 0

    lax.fori_loop(0, I + 6, tr, 0)
    weights_table(dw, w49, False)
    p_at = lax.broadcasted_iota(jnp.int32, (R, R), 0)
    p_row = lax.broadcasted_iota(jnp.int32, (R, R), 1)
    order = (p_row == (p_at % S) * I + p_at // S).astype(f32).astype(bf16)
    land_p = dot_r(order, land[...].astype(f32).astype(bf16)).astype(bf16)
    spread = (
        lax.broadcasted_iota(jnp.int32, (CW, CW * 128), 1) // 128
        == lax.broadcasted_iota(jnp.int32, (CW, CW * 128), 0)
    )
    land_w = dot(land_p, spread.astype(f32).astype(bf16)).astype(bf16)
    for i in range(I):
        for c in range(CW):
            at = (i * CW + c) * S
            landb[at : at + S, :] = land_w[i * S : (i + 1) * S, c * 128 : (c + 1) * 128]
    up[0:128, :] = upw[...]
    up[128:256, :] = jnp.where(
        lax.broadcasted_iota(jnp.int32, (128, 512), 0) == 0, bias[...].astype(f32).reshape(1, 512), 0.0
    ).astype(bf16)

    def emit(i, c, v):
        dep[pl.ds((i * CW + c) * S, S), :] = v

    conv49(el, w49, emit, I, CW)

    jj, j1, pm = ones_mean(256), ones_mean(128), pair_mean()
    g_n = gain[...].astype(f32).reshape(1, 128)
    sc = scale[...].astype(f32).reshape(1, 128)
    sg0 = sgain[0:1, :].astype(f32)
    T1 = 1024

    def nfwd(n, _):
        base = pl.multiple_of(n * T1, T1)
        x = dep[pl.ds(base, T1), :]
        cen = x - dot(split2(x), jj)
        rs = lax.rsqrt(dot((cen * cen).astype(bf16), j1) + EPS)
        ht = cen * rs
        hat[pl.ds(base, T1), :] = ht
        rst[pl.ds(base, T1), :] = rs
        nrm[pl.ds(base, T1), :] = (ht * g_n).astype(bf16)
        return 0

    lax.fori_loop(0, n0 // T1, nfwd, 0)

    T2 = 512
    onec = (lax.broadcasted_iota(jnp.int32, (T2, 128), 1) == 0).astype(f32).astype(bf16)

    def upf(n, _):
        base = pl.multiple_of(n * T2, T2)
        lhs = jnp.concatenate([nrm[pl.ds(base, T2), :], onec], axis=1)
        for q in range(2):
            hid = dot(lhs, up[:, q * 256 : (q + 1) * 256])
            ac, sl = gelu(hid)
            act[pl.ds(base, T2), q * 256 : (q + 1) * 256] = ac.astype(bf16)
            slp[pl.ds(base, T2), q * 256 : (q + 1) * 256] = sl.astype(bf16)
        return 0

    lax.fori_loop(0, n0 // T2, upf, 0)

    TP = 2 * CW * S

    def sect_norm(lv, s):
        cen = lv.astype(f32) - dot(lv, j1)
        rs1 = lax.rsqrt(dot((cen * cen).astype(bf16), j1) + EPS)
        h1 = cen * rs1
        return h1, rs1, (h1 * sgain[s : s + 1, :].astype(f32)).astype(bf16)

    def dnf(i2, _):
        base = pl.multiple_of(i2 * TP, TP)
        mixed = dot(act[pl.ds(base, TP), :], down[...])
        xs = jnp.concatenate(
            [el[pl.ds((i2 * 2 + a + 3) * CE + 3, CW)].reshape(CW * S, 128) for a in range(2)], axis=0
        ).astype(f32)
        lv = (landb[pl.ds(base, TP), :].astype(f32) * (xs + sc * mixed)).astype(bf16)
        h1, rs1, sn = sect_norm(lv, 0)
        shat[pl.ds(base, TP), :] = h1
        srst[pl.ds(base, TP), :] = rs1
        sn = sn.reshape(2, CW // 2, 2, S, 128)
        pb = pl.multiple_of(i2 * (TP // 4), TP // 4)
        for a in range(2):
            for b in range(2):
                k = 2 * a + b
                p1[pl.ds(pb, TP // 4), k * 128 : (k + 1) * 128] = sn[a, :, b].reshape(TP // 4, 128)
        return 0

    lax.fori_loop(0, I // 2, dnf, 0)

    def to_patches(sn, ii, cc):
        v = sn.reshape(ii // 2, 2, cc // 2, 2, S, 128)
        return jnp.concatenate(
            [v[:, a, :, b].reshape(ii * cc * S // 4, 128) for a in range(2) for b in range(2)], axis=1
        )

    def from_patches(sp, ii, cc):
        ps = [sp[:, k * 128 : (k + 1) * 128].reshape(ii // 2, cc // 2, S, 128) for k in range(4)]
        rows = [jnp.stack([ps[2 * a], ps[2 * a + 1]], axis=2).reshape(ii // 2, cc, S, 128) for a in range(2)]
        return jnp.stack(rows, axis=1).reshape(ii * cc * S, 128)

    def put(at, value, blocks):
        for q in range(blocks):
            sums[at + q * 128 : at + (q + 1) * 128, :] = value[:, q * 128 : (q + 1) * 128].astype(bf16)

    l1 = (dot(p1[...], sw[0]) + sbias[0:1, :].astype(f32)).astype(bf16)
    h1, r1, sn1 = sect_norm(l1, 1)
    P2 = to_patches(sn1, I // 2, CW // 2)
    l2 = (dot(P2, sw[1]) + sbias[1:2, :].astype(f32)).astype(bf16)
    h2, r2, sn2 = sect_norm(l2, 2)
    P3 = to_patches(sn2, I // 4, CW // 4)
    l3 = (dot(P3, sw[2]) + sbias[2:3, :].astype(f32)).astype(bf16)
    Q = CW // 8
    for c in range(Q):
        x2d[pl.ds(c, S, stride=Q), :] = l3[c * S : (c + 1) * S, :].astype(f32)
    for r in range(S):
        bott[r] = x2d[r * Q : (r + 1) * Q, :].astype(bf16)
        x2d[128 + r * Q : 128 + (r + 1) * Q, :] = cot[r].astype(f32)
    b3 = jnp.concatenate([x2d[pl.ds(128 + c, S, stride=Q), :] for c in range(Q)], axis=0).astype(bf16)
    put(1024, dot_t(b3, P3), 4)
    u2 = from_patches(dot_r(b3, sw[2]), I // 4, CW // 4) * sgain[2:3, :].astype(f32)
    b2 = norm_bwd(u2, h2, r2, pm).astype(bf16)
    put(512, dot_t(b2, P2), 4)
    u1 = from_patches(dot_r(b2, sw[1]), I // 2, CW // 2) * sgain[1:2, :].astype(f32)
    b1 = norm_bwd(u1, h1, r1, pm).astype(bf16)
    put(0, dot_t(b1, p1[...]), 4)
    back[...] = b1

    QP = TP // 4

    def bk1(i2, _):
        pb = pl.multiple_of(i2 * QP, QP)
        bk = back[pl.ds(pb, QP), :]
        base = pl.multiple_of(i2 * TP, TP)
        us = []
        for a in range(2):
            sp = dot_r(bk, sw[0, a * 256 : (a + 1) * 256, :])
            us.append(
                jnp.stack(
                    [sp[:, :128].reshape(CW // 2, S, 128), sp[:, 128:].reshape(CW // 2, S, 128)], axis=1
                ).reshape(TP // 2, 128)
            )
        u = jnp.concatenate(us, axis=0) * sg0
        b0 = norm_bwd(u, shat[pl.ds(base, TP), :], srst[pl.ds(base, TP), :], pm).astype(bf16).astype(f32)
        dr = landb[pl.ds(base, TP), :].astype(f32) * b0
        dirout[pl.ds(base, TP), :] = dr.astype(bf16)
        mgs[pl.ds(base, TP), :] = (dr * sc).astype(bf16)
        return 0

    lax.fori_loop(0, I // 2, bk1, 0)

    def bk2(n, _):
        base = pl.multiple_of(n * T2, T2)
        mg = mgs[pl.ds(base, T2), :]
        for q in range(2):
            ag = dot_r(mg, down[q * 256 : (q + 1) * 256, :])
            sl = slp[pl.ds(base, T2), q * 256 : (q + 1) * 256].astype(f32)
            slp[pl.ds(base, T2), q * 256 : (q + 1) * 256] = (ag * sl).astype(bf16)
        return 0

    lax.fori_loop(0, n0 // T2, bk2, 0)

    def bk3(n, _):
        base = pl.multiple_of(n * T1, T1)
        ng = dot_r(slp[pl.ds(base, T1), :], up[0:128, :])
        dg = norm_bwd(ng * g_n, hat[pl.ds(base, T1), :], rst[pl.ds(base, T1), :], pm)
        gout[pl.ds(base, T1), :] = dg.astype(bf16)
        return 0

    lax.fori_loop(0, n0 // T1, bk3, 0)
    downs[...] = dot_t(mgs[...], act[...])
    ups[...] = dot_t(nrm[...], slp[...])
    put(1536, downs[...], 4)
    put(2048, ups[...], 4)

    tacc[...] = jnp.zeros_like(tacc)

    def tap(n, _):
        i = n // (CW // 8)
        c0 = (n % (CW // 8)) * 8
        g = [gout[pl.ds((i * CW + c0 + k) * S, S), :].astype(f32) for k in range(8)]
        for a in range(7):
            row = [el[(i + a) * CE + c0 + m].astype(f32) for m in range(14)]
            for b in range(7):
                s = None
                for k in range(8):
                    pr = row[k + b] * g[k]
                    s = pr if s is None else s + pr
                tacc[a * 7 + b] += s[:8] + s[8:]
        return 0

    lax.fori_loop(0, I * (CW // 8), tap, 0)
    ts = [jnp.sum(tacc[t], axis=0, keepdims=True) for t in range(49)]
    ts = jnp.concatenate(ts + [jnp.zeros((15, 128), f32)], axis=0)
    sums[2560:2624, :] = ts.astype(bf16)
    sums[2624:2688, :] = jnp.zeros((64, 128), bf16)

    odd = lax.axis_index("lat") % 2
    keep[...] = sums[pl.ds(pl.multiple_of(odd * HALF, 64), HALF), :]
    away[0:HALF, :] = sums[pl.ds(pl.multiple_of((1 - odd) * HALF, 64), HALF), :]
    x2d[0:n0, :] = gout[...].astype(f32)
    for k in range(3):
        lo = x2d[pl.ds(k * CW * S, CW, stride=S), :].astype(bf16)
        hi = x2d[pl.ds((I - 3 + k) * CW * S + S - 1, CW, stride=S), :].astype(bf16)
        last[k] = hi
        send[k] = jnp.where(odd == 1, hi, lo)
        away[HALF + k * CW : HALF + (k + 1) * CW, :] = jnp.where(odd == 1, lo, hi)
    for i in range(I):
        lcol[i * 3 * S : (i + 1) * 3 * S, :] = gout[i * CW * S : (i * CW + 3) * S, :]
        rcol[i * 3 * S : (i + 1) * 3 * S, :] = gout[((i + 1) * CW - 3) * S : (i + 1) * CW * S, :]


def block_pass(field, south, north, left, right, land, dw, gain, upw, bias, down, scale, sgain, sw, sbias, cot):
    R, CW, C = field.shape
    n = R * CW
    I = R // S
    sd = jax.ShapeDtypeStruct
    out_shape = (
        sd((S, CW // 8, C), bf16),
        sd((n, C), bf16),
        sd((n, C), bf16),
        sd((3, CW, C), bf16),
        sd((3, CW, C), bf16),
        sd((I * 3 * S, C), bf16),
        sd((I * 3 * S, C), bf16),
        sd((HALF, C), bf16),
        sd((HALF + 3 * CW, C), bf16),
    )
    V = pltpu.VMEM
    scratch = [
        V(((R + 6) * 40 + (R + 6) // I + 16, C), f32),
        V(((I + 6) * (CW + 6), S, C), bf16),
        V((49, S, C), bf16),
        V((n, C), f32),
        V((n, C), f32),
        V((n, C), f32),
        V((n, C), bf16),
        V((n, 512), bf16),
        V((n, 512), bf16),
        V((n, C), f32),
        V((n, C), f32),
        V((n // 4, 512), bf16),
        V((n // 4, C), bf16),
        V((49, 8, C), f32),
        V((C, 512), f32),
        V((C, 512), f32),
        V((n, C), bf16),
        V((n, C), bf16),
        V((256, 512), bf16),
        V((2 * HALF, C), bf16),
    ]
    return pl.pallas_call(
        functools.partial(block_body, R, CW),
        out_shape=out_shape,
        in_specs=[VMEM] * 16,
        out_specs=[VMEM] * 9,
        scratch_shapes=scratch,
        compiler_params=PARAMS,
        name="block_pass",
    )(field, south, north, left, right, land, dw, gain, upw, bias, down, scale, sgain, sw, sbias, cot)


def conv_back_body(R, CW, g, dirin, dw, out, gx, gext, w49):
    I = R // S
    CE = CW + 6
    row = lax.broadcasted_iota(jnp.int32, (S, 128), 0)
    zero = jnp.zeros((3, S, 128), bf16)

    def cpy(i, _):
        gext[pl.ds((i + 3) * CE, 3)] = zero
        gext[pl.ds((i + 3) * CE + 3, CW)] = g[pl.ds(pl.multiple_of(i * CW * S, CW * S), CW * S), :].reshape(CW, S, 128)
        gext[pl.ds((i + 3) * CE + 3 + CW, 3)] = zero
        return 0

    lax.fori_loop(0, I, cpy, 0)
    for k in range(3):

        def shift(c, _, k=k):
            v = pltpu.roll(gext[(I + k) * CE + c].astype(f32), 1, 0)
            gext[k * CE + c] = jnp.where(row == 0, 0.0, v).astype(bf16)
            v = pltpu.roll(gext[(3 + k) * CE + c].astype(f32), S - 1, 0)
            gext[(I + 3 + k) * CE + c] = jnp.where(row == S - 1, 0.0, v).astype(bf16)
            return 0

        lax.fori_loop(0, CE, shift, 0, unroll=2)
    weights_table(dw, w49, True)

    def emit(i, c, v):
        at = pl.multiple_of((i * CW + c) * S, S)
        out[pl.ds(at, S), :] = v + dirin[pl.ds(at, S), :].astype(f32)

    conv49(gext, w49, emit, I, CW)


def conv_back(g, dirin, dw, R, CW):
    C = g.shape[1]
    I = R // S
    return pl.pallas_call(
        functools.partial(conv_back_body, R, CW),
        out_shape=jax.ShapeDtypeStruct((R * CW, C), f32),
        in_specs=[VMEM] * 3,
        out_specs=VMEM,
        scratch_shapes=[
            pltpu.VMEM((8, C), f32),
            pltpu.VMEM(((I + 6) * (CW + 6), S, C), bf16),
            pltpu.VMEM((49, S, C), bf16),
        ],
        compiler_params=SMALL,
        cost_estimate=pl.CostEstimate(flops=10**8, bytes_accessed=30 * 2**20, transcendentals=0),
        name="conv_back",
    )(g, dirin, dw)


def edges_body(R, CW, base, south, north, gl, gr, dw, out, acc, rows, cols, w49):
    I = R // S
    CE = CW + 6
    isn = on_top().astype(f32)
    nots = 1.0 - isn
    core = I * 3 * S
    row = lax.broadcasted_iota(jnp.int32, (S, 128), 0)
    for t in range(49):
        w49[t] = jnp.broadcast_to(dw[t : t + 1, :].astype(f32), (S, 128))
    for side in range(2):
        for k in range(3):
            at = core + side * 9 + k * 3
            mid = (north if side else south)[k]
            rows[pl.ds((side * 3 + k) * 40, CE), :] = jnp.concatenate(
                [gl[at : at + 3, :], mid, gr[at : at + 3, :]], axis=0
            ).astype(f32)

    def taps(k, a, flip):
        s = None
        for b in range(7):
            o = 6 - b if flip else b
            pr = rows[pl.ds(k * 40 + o, CW), :] * w49[7 * a + b, 0:1, :]
            s = pr if s is None else s + pr
        return s

    low = []
    for r in range(3):
        low.append(sum(taps(k, r + 6 - k, True) for k in range(r, 3)))
    high = []
    for t in range(3):
        v = sum(taps(3 + k, 2 - t - k, True) for k in range(3 - t)) * nots
        k1 = t + 1
        f = sum(taps(3 + rho, 5 + k1 - rho, False) for rho in range(k1 - 1, 3)) * isn
        high.append(v + f)
    for side in range(2):
        src = gr if side else gl

        def fill(i, _, src=src, side=side):
            for j in range(3):
                at = pl.multiple_of((i * 3 + j) * S, S)
                cols[side * (I + 6) * 3 + (i + 3) * 3 + j] = src[pl.ds(at, S), :].astype(f32)
            return 0

        lax.fori_loop(0, I, fill, 0)
        for k in range(3):
            for j in range(3):
                at = side * (I + 6) * 3
                v = pltpu.roll(cols[at + (I + k) * 3 + j], 1, 0)
                cols[at + k * 3 + j] = jnp.where(row == 0, 0.0, v)
                v = pltpu.roll(cols[at + (3 + k) * 3 + j], S - 1, 0)
                cols[at + (I + 3 + k) * 3 + j] = jnp.where(row == S - 1, 0.0, v)

    PITCH = CW * S

    def step(i, _):
        at = pl.multiple_of(i * PITCH, PITCH)
        acc[pl.ds(at, PITCH), :] = base[pl.ds(at, PITCH), :]
        for side in range(2):
            for t in range(3):
                s = None
                for j in range(3):
                    b = 2 - t - j if side else t + 6 - j
                    if b < 0 or b > 6:
                        continue
                    for a in range(7):
                        pr = cols[side * (I + 6) * 3 + (i + 6 - a) * 3 + j] * w49[7 * a + b]
                        s = pr if s is None else s + pr
                c = CW - 1 - t if side else t
                at = pl.multiple_of(i * PITCH + c * S, S)
                acc[pl.ds(at, S), :] += s
        return 0

    lax.fori_loop(0, I, step, 0)

    def unt(r, _):
        s = r // I
        i = r % I
        out[r] = acc[pl.ds(i * PITCH + s, CW, stride=S), :].astype(bf16)
        return 0

    lax.fori_loop(3, R - 3, unt, 0, unroll=2)
    for r in list(range(3)) + list(range(R - 3, R)):
        v = acc[pl.ds((r % I) * PITCH + r // I, CW, stride=S), :]
        v = v + (low[r] if r < 3 else high[R - 1 - r])
        out[r] = v.astype(bf16)


def edges(base, south, north, gl, gr, dw, R, CW):
    C = base.shape[1]
    I = R // S
    return pl.pallas_call(
        functools.partial(edges_body, R, CW),
        out_shape=jax.ShapeDtypeStruct((R, CW, C), bf16),
        in_specs=[VMEM] * 6,
        out_specs=VMEM,
        scratch_shapes=[
            pltpu.VMEM((R * CW, C), f32),
            pltpu.VMEM((240, C), f32),
            pltpu.VMEM((2 * (I + 6) * 3, S, C), f32),
            pltpu.VMEM((49, S, C), f32),
        ],
        compiler_params=SMALL,
        cost_estimate=pl.CostEstimate(flops=10**8, bytes_accessed=10 * 2**20, transcendentals=0),
        name="edges",
    )(base, south, north, gl, gr, dw)


def finish_body(factor, chunk, mine, other, o_depth, o_up, o_down, o_sec, full):
    core = lax.axis_index("lat") % 2
    place = (lax.axis_index("lat") // 2) * 2 + lax.axis_index("lon") % 2
    half = 4 * chunk
    for j in range(4):
        src = lax.bitwise_xor(place, j)
        at = pl.multiple_of(core * half + j * chunk, 16)
        full[pl.ds(at, chunk), :] = mine[src]
        at = pl.multiple_of((1 - core) * half + j * chunk, 16)
        full[pl.ds(at, chunk), :] = other[src]

    def block(n):
        return full[n * 128 : (n + 1) * 128, :].astype(f32) * factor

    for s in range(3):
        for q in range(4):
            o_sec[s, q * 128 : (q + 1) * 128, :] = block(s * 4 + q).T
    for q in range(4):
        o_down[q * 128 : (q + 1) * 128, :] = block(12 + q).T
        o_up[:, q * 128 : (q + 1) * 128] = block(16 + q)
    o_depth[...] = block(20)[:49, :]


def finish(mine, other, factor):
    chunk = mine.shape[1]
    sd = jax.ShapeDtypeStruct
    return pl.pallas_call(
        functools.partial(finish_body, factor, chunk),
        out_shape=(sd((49, 128), f32), sd((128, 512), f32), sd((512, 128), f32), sd((3, 512, 128), f32)),
        in_specs=[VMEM, VMEM],
        out_specs=[VMEM] * 4,
        scratch_shapes=[pltpu.VMEM((8 * chunk, 128), bf16)],
        compiler_params=PARAMS,
        name="finish_sums",
    )(mine, other)


def add_bf(*vals):
    vals = [v.astype(f32) for v in vals]
    while len(vals) > 1:
        vals = [vals[i] + vals[i + 1] for i in range(0, len(vals), 2)]
    return vals[0].astype(bf16)


def flip_pairs(axis, bits):
    return [(i, i ^ bits) for i in range(lax.axis_size(axis))]


def both_pairs(lat_bits, lon_bits):
    nl = lax.axis_size("lon")
    return [
        (a * nl + b, (a ^ lat_bits) * nl + (b ^ lon_bits))
        for a in range(lax.axis_size("lat"))
        for b in range(nl)
    ]


def square_pairs(k):
    return both_pairs((k // 2) * 2, k % 2)


def square_sum(held, place):
    own = lax.dynamic_index_in_dim(held, place, 0, keepdims=False)
    came = []
    for k in (1, 2, 3):
        part = lax.dynamic_index_in_dim(held, lax.bitwise_xor(place, k), 0, keepdims=False)
        came.append(lax.ppermute(part, ("lat", "lon"), square_pairs(k)))
    return add_bf(own, *came)


def line_sum(total):
    left = lax.axis_size("lon") // 2
    bit = 2
    while left > 1:
        if left % 4 == 0:
            total = add_bf(total, *[lax.ppermute(total, "lon", flip_pairs("lon", bit * k)) for k in (1, 2, 3)])
            left //= 4
            bit *= 4
        else:
            total = add_bf(total, lax.ppermute(total, "lon", flip_pairs("lon", bit)))
            left //= 2
            bit *= 2
    return total


def on_top():
    return lax.axis_index("lat") == lax.axis_size("lat") - 1


def rim_body(R, CW, field, mirror, near, send, last, lc, rc, place, scr):
    odd = lax.axis_index("lat") % 2
    for k in range(3):
        lo = field[k]
        hi = field[R - 3 + k]
        last[k] = hi
        send[k] = jnp.where(odd == 1, hi, lo)
        near[k] = jnp.where(odd == 1, lo, hi)
    place[0] = mirror[0] // CW
    place[1] = mirror[0] % CW
    scr[0 : R * 8, :] = field[:, 0:8, :].astype(f32).reshape(R * 8, 128)
    scr[R * 8 :, :] = field[:, CW - 8 : CW, :].astype(f32).reshape(R * 8, 128)
    for k in range(3):
        lc[k] = scr[pl.ds(k, R, stride=8), :].astype(bf16)
        rc[k] = scr[pl.ds(R * 8 + 5 + k, R, stride=8), :].astype(bf16)


def rim(field, mirror):
    R, CW, C = field.shape
    sd = jax.ShapeDtypeStruct
    return pl.pallas_call(
        functools.partial(rim_body, R, CW),
        out_shape=(sd((3, CW, C), bf16),) * 3 + (sd((3, R, C), bf16),) * 2 + (sd((2,), jnp.int32),),
        in_specs=[VMEM, SMEM],
        out_specs=[VMEM] * 5 + [SMEM],
        scratch_shapes=[pltpu.VMEM((2 * R * 8, C), f32)],
        compiler_params=SMALL,
        name="rim",
    )(field, mirror)


def join_body(CW, width, flip, place, near, far, blk_b, lc, rc, south, north, lp, rp, cat, scr):
    odd = lax.axis_index("lat") % 2 == 1
    top = on_top()
    rem = place[1]
    at = lax.broadcasted_iota(jnp.int32, (CW, CW), 0)
    turn = (at + lax.broadcasted_iota(jnp.int32, (CW, CW), 1) == CW - 1).astype(f32).astype(bf16)
    for k in range(3):
        cat[0:CW, :] = blk_b[k].astype(f32)
        cat[CW : 2 * CW, :] = far[k].astype(f32)
        win = cat[pl.ds(rem + 1, CW), :].astype(bf16)
        scr[k * CW : (k + 1) * CW, :] = dot(turn, win)
    for k in range(3):
        m = 2 - k if flip else k
        beyond = scr[m * CW : (m + 1) * CW, :]
        above = jnp.where(odd, far[k].astype(f32), near[k].astype(f32))
        below = jnp.where(odd, near[k].astype(f32), far[k].astype(f32))
        above = jnp.where(top, beyond, above)
        south[k] = below.astype(bf16)
        north[k] = above.astype(bf16)
        scr[(3 + k) * CW : (4 + k) * CW, :] = below
        scr[(6 + k) * CW : (7 + k) * CW, :] = above
    for pay, core, lo in ((lp, lc, 0), (rp, rc, CW - 3)):
        if flip:
            for j in range(3):
                for k in range(3):
                    cat[k : k + 1, :] = scr[(3 + k) * CW + lo + j : (3 + k) * CW + lo + j + 1, :]
                    cat[3 + width + k : 4 + width + k, :] = scr[(6 + k) * CW + lo + j : (6 + k) * CW + lo + j + 1, :]
                cat[3 : 3 + width, :] = core[j].astype(f32)
                pay[j] = cat[0 : width + 6, :].astype(bf16)
        else:
            pay[0:width, :] = core[...]
            for side in range(2):
                for k in range(3):
                    src = (3 + 3 * side + k) * CW + lo
                    cat[side * 9 + k * 3 : side * 9 + k * 3 + 3, :] = scr[src : src + 3, :]
            pay[width : width + 32, :] = cat[0:32, :].astype(bf16)


def join(place, near, far, blk_b, lc, rc, flip):
    CW, C = near.shape[1:]
    width = lc.shape[1] if flip else lc.shape[0]
    sd = jax.ShapeDtypeStruct
    pay = sd((3, width + 6, C) if flip else (width + 32, C), bf16)
    return pl.pallas_call(
        functools.partial(join_body, CW, width, flip),
        out_shape=(sd((3, CW, C), bf16),) * 2 + (pay, pay),
        in_specs=[SMEM] + [VMEM] * 5,
        out_specs=[VMEM] * 4,
        scratch_shapes=[pltpu.VMEM((max(2 * CW + 8, width + 8), C), f32), pltpu.VMEM((9 * CW, C), f32)],
        compiler_params=SMALL,
        name="join",
    )(place, near, far, blk_b, lc, rc)


def far_rows(send, last, quot):
    nl = lax.axis_size("lon")
    nt = lax.axis_size("lat")
    top = (nt - 1) * nl
    axes = ("lat", "lon")
    swap = [(a * nl + e, (a + 1) * nl + e) for a in range(1, nt - 1, 2) for e in range(nl)]
    swap += [(j, i) for i, j in swap]

    def branch(q):
        def run(send, last):
            fa = [(top + e, top + (q - e) % nl) for e in range(nl)]
            fb = [(top + e, top + (q - 1 - e) % nl) for e in range(nl)]
            return lax.ppermute(send, axes, swap + fa), lax.ppermute(last, axes, fb)

        return run

    return lax.switch(quot, [branch(q) for q in range(nl)], send, last)


def shift_pairs(axis, by):
    n = lax.axis_size(axis)
    return [(i, (i + by) % n) for i in range(n)]


def on_device(
    field, land, mirror, depth_weight, norm_gain, up_weight, up_bias, down_proj, layer_scale,
    section_gain, section_weight, section_bias, cotangent,
):
    R, CW, C = field.shape
    total = R * CW * lax.axis_size("lat") * lax.axis_size("lon")
    factor = 1.0 / math.sqrt(total / 64.0)
    near, send, last, lc, rc, shift = rim(field, mirror)
    near = lax.ppermute(near, "lat", flip_pairs("lat", 1))
    far, blk_b = far_rows(send, last, shift[0])
    south_f, north_f, lpay, rpay = join(shift, near, far, blk_b, lc, rc, True)
    right_f = lax.ppermute(lpay, "lon", shift_pairs("lon", -1))
    left_f = lax.ppermute(rpay, "lon", shift_pairs("lon", 1))
    level, g, direct, send, last, lcol, rcol, keep, away = block_pass(
        field, south_f, north_f, left_f, right_f, land.T, depth_weight, norm_gain, up_weight, up_bias, down_proj,
        layer_scale, section_gain, section_weight, section_bias, cotangent,
    )

    place = (lax.axis_index("lat") // 2) * 2 + lax.axis_index("lon") % 2
    got = lax.ppermute(away, "lat", flip_pairs("lat", 1))
    near = got[HALF:].reshape(3, CW, C)
    held = add_bf(keep, got[:HALF]).reshape(4, HALF // 4, C)
    send, held = lax.optimization_barrier((send, held))
    chunk = square_sum(held, place)
    far, blk_b = far_rows(send, last, shift[0])
    chunk, far = lax.optimization_barrier((chunk, far))
    south_g, north_g, lpay, rpay = join(shift, near, far, blk_b, lcol, rcol, False)
    chunk, lpay = lax.optimization_barrier((chunk, lpay))
    gr = lax.ppermute(lpay, "lon", shift_pairs("lon", -1))
    gl = lax.ppermute(rpay, "lon", shift_pairs("lon", 1))
    g, _ = lax.optimization_barrier((g, south_g))
    base = conv_back(g, direct, depth_weight, R, CW)
    chunk = line_sum(chunk)
    chunk, base = lax.optimization_barrier((chunk, base))
    grad_field = edges(base, south_g, north_g, gl, gr, depth_weight, R, CW)
    axes = ("lat", "lon")
    back = [lax.ppermute(chunk, axes, square_pairs(k)) for k in (1, 2, 3)]
    back[0], grad_field = lax.optimization_barrier((back[0], grad_field))
    mine = jnp.stack([chunk] + back)
    other = lax.ppermute(mine, "lat", flip_pairs("lat", 1))
    g_depth, g_up, g_down, g_sec = finish(mine, other, factor)
    return level, grad_field, g_depth, g_up, g_down, g_sec


def solution(mesh):
    cells = P("lat", "lon", None)
    in_specs = (cells, P("lat", "lon")) + (P(),) * 10 + (cells,)
    out_specs = (cells, cells, P(), P(), P(), P())
    return jax.shard_map(on_device, mesh=mesh, in_specs=in_specs, out_specs=out_specs, check_vma=False)
```

```python
import functools
import math

import jax
import jax.numpy as jnp
from jax import lax
from jax.experimental import pallas as pl
from jax.experimental.pallas import tpu as pltpu
from jax.sharding import PartitionSpec as P

SECTIONS = 3
EPS = 1e-6
f32, bf16 = jnp.float32, jnp.bfloat16
S = 16
LOG2E = 1.4426950408889634
LOG2_DENS = -0.3257480647361593
HALF = 1344
VMEM = pl.BlockSpec(memory_space=pltpu.VMEM)
SMEM = pl.BlockSpec(memory_space=pltpu.SMEM)
PARAMS = pltpu.CompilerParams(vmem_limit_bytes=44 * 2**20)
WHOLE = pltpu.CompilerParams(vmem_limit_bytes=63 * 2**20 + 2**19)
SMALL = pltpu.CompilerParams(vmem_limit_bytes=24 * 2**20)


def dot(a, b):
    return jnp.dot(a, b, preferred_element_type=f32)


def dot_t(a, b):
    return lax.dot_general(a, b, (((0,), (0,)), ((), ())), preferred_element_type=f32)


def dot_r(a, b):
    return lax.dot_general(a, b, (((1,), (1,)), ((), ())), preferred_element_type=f32)


def ones_mean(n):
    return jnp.full((n, 128), 1.0 / 128, bf16)


def pair_mean():
    r = lax.broadcasted_iota(jnp.int32, (256, 256), 0) // 128
    c = lax.broadcasted_iota(jnp.int32, (256, 256), 1) // 128
    return jnp.where(r == c, 1.0 / 128, 0.0).astype(bf16)


def split2(x):
    hi = x.astype(bf16)
    lo = (x - hi.astype(f32)).astype(bf16)
    return jnp.concatenate([hi, lo], axis=1)


def norm_bwd(u, hat, rstd, pm):
    m = dot(jnp.concatenate([u.astype(bf16), (u * hat).astype(bf16)], axis=1), pm)
    return rstd * (u - m[:, :128] - hat * m[:, 128:])


def gelu2(h):
    g = h * 0.7071067811865476
    c = 1.0 + lax.erf(g)
    e = jnp.exp2(g * g * (-LOG2E) + LOG2_DENS)
    return h * c, c + h * e


def weights_table(dw, w49, flip):
    for t in range(49):
        w49[48 - t if flip else t] = jnp.broadcast_to(dw[t : t + 1, :].astype(f32), (S, 128)).astype(w49.dtype)


def conv49(el, w49, emit, I, CW):
    CE = CW + 6
    CG = 4

    def step(n, _):
        i = n // (CW // CG)
        c0 = (n % (CW // CG)) * CG
        acc = [None] * CG
        for a in range(7):
            row = [el[(i + a) * CE + c0 + m].astype(f32) for m in range(CG + 6)]
            for b in range(7):
                w = w49[a * 7 + b].astype(f32)
                for k in range(CG):
                    pr = row[k + b] * w
                    acc[k] = pr if acc[k] is None else acc[k] + pr
        for k in range(CG):
            emit(i, c0 + k, acc[k])
        return 0

    lax.fori_loop(0, I * (CW // CG), step, 0)


def block_body(
    R, CW,
    field, south, north, left, right, land, dw, gain, upw, bias, down, scale, sgain, sw, sbias, cot,
    bott, gout, dirout, send, last, lcol, rcol, keep, away,
    x2d, el, w49, dep, hat, rst, nrm, act, slp, shat, srst, p1, back, tacc, downs, ups, mgs, landb, up, dn, sums,
):
    I = R // S
    CE = CW + 6
    XW = 40
    n0 = R * CW

    def asm(r, _):
        x2d[pl.ds((r + 3) * XW + (r + 3) // I + 3, CW), :] = field[r].astype(f32)
        return 0

    lax.fori_loop(0, R, asm, 0, unroll=4)
    PB = I * XW + 1
    for k in range(3):
        x2d[pl.ds(k * XW + 3, CW), :] = south[k].astype(f32)
        x2d[pl.ds((R + 3 + k) * XW + (R + 3 + k) // I + 3, CW), :] = north[k].astype(f32)
        for m in range((R + 6 + I - 1) // I):
            rows = min(I, R + 6 - m * I)
            x2d[pl.ds(m * PB + k, rows, stride=XW), :] = left[k, m * I : m * I + rows, :].astype(f32)
            x2d[pl.ds(m * PB + CW + 3 + k, rows, stride=XW), :] = right[k, m * I : m * I + rows, :].astype(f32)

    def tr(i, _):
        for c in range(CE):
            el[i * CE + c] = x2d[pl.ds(i * XW + i // I + c, S, stride=PB), :].astype(bf16)
        return 0

    lax.fori_loop(0, I + 6, tr, 0)
    weights_table(dw, w49, False)
    p_at = lax.broadcasted_iota(jnp.int32, (R, R), 0)
    p_row = lax.broadcasted_iota(jnp.int32, (R, R), 1)
    order = (p_row == (p_at % S) * I + p_at // S).astype(f32).astype(bf16)
    land_p = dot_r(order, land[...].astype(f32).astype(bf16)).astype(bf16)
    spread = (
        lax.broadcasted_iota(jnp.int32, (CW, CW * 128), 1) // 128
        == lax.broadcasted_iota(jnp.int32, (CW, CW * 128), 0)
    )
    land_w = dot(land_p, spread.astype(f32).astype(bf16)).astype(bf16)
    for i in range(I):
        for c in range(CW):
            at = (i * CW + c) * S
            landb[at : at + S, :] = land_w[i * S : (i + 1) * S, c * 128 : (c + 1) * 128]
    dn[...] = (down[...].astype(f32) * 0.5).astype(bf16)
    up[0:128, :] = upw[...]
    up[128:256, :] = jnp.where(
        lax.broadcasted_iota(jnp.int32, (128, 512), 0) == 0, bias[...].astype(f32).reshape(1, 512), 0.0
    ).astype(bf16)

    def emit(i, c, v):
        dep[pl.ds((i * CW + c) * S, S), :] = v

    conv49(el, w49, emit, I, CW)

    jj, j1, pm = ones_mean(256), ones_mean(128), pair_mean()
    g_n = gain[...].astype(f32).reshape(1, 128)
    sc = scale[...].astype(f32).reshape(1, 128)
    sg0 = sgain[0:1, :].astype(f32)
    T1 = n0 // 2

    def nfwd(n, _):
        base = pl.multiple_of(n * T1, T1)
        x = dep[pl.ds(base, T1), :]
        cen = x - dot(split2(x), jj)
        rs = lax.rsqrt(dot((cen * cen).astype(bf16), j1) + EPS)
        ht = cen * rs
        hat[pl.ds(base, T1), :] = ht
        rst[pl.ds(base, T1), :] = rs
        nrm[pl.ds(base, T1), :] = (ht * g_n).astype(bf16)
        return 0

    lax.fori_loop(0, n0 // T1, nfwd, 0)

    T2 = n0 // 4
    onec = (lax.broadcasted_iota(jnp.int32, (T2, 128), 1) == 0).astype(f32).astype(bf16)

    def upf(n, _):
        base = pl.multiple_of(n * T2, T2)
        lhs = jnp.concatenate([nrm[pl.ds(base, T2), :], onec], axis=1)
        for q in range(2):
            hid = dot(lhs, up[:, q * 256 : (q + 1) * 256])
            ac, sl = gelu2(hid)
            act[pl.ds(base, T2), q * 256 : (q + 1) * 256] = ac.astype(bf16)
            slp[pl.ds(base, T2), q * 256 : (q + 1) * 256] = sl.astype(bf16)
        return 0

    lax.fori_loop(0, n0 // T2, upf, 0)

    TP = 2 * CW * S

    def sect_norm(lv, s):
        cen = lv.astype(f32) - dot(lv, j1)
        rs1 = lax.rsqrt(dot((cen * cen).astype(bf16), j1) + EPS)
        h1 = cen * rs1
        return h1, rs1, (h1 * sgain[s : s + 1, :].astype(f32)).astype(bf16)

    def dnf(i2, _):
        base = pl.multiple_of(i2 * TP, TP)
        mixed = dot(act[pl.ds(base, TP), :], dn[...])
        xs = jnp.concatenate(
            [el[pl.ds((i2 * 2 + a + 3) * CE + 3, CW)].reshape(CW * S, 128) for a in range(2)], axis=0
        ).astype(f32)
        lv = (landb[pl.ds(base, TP), :].astype(f32) * (xs + sc * mixed)).astype(bf16)
        h1, rs1, sn = sect_norm(lv, 0)
        shat[pl.ds(base, TP), :] = h1
        srst[pl.ds(base, TP), :] = rs1
        sn = sn.reshape(2, CW // 2, 2, S, 128)
        pb = pl.multiple_of(i2 * (TP // 4), TP // 4)
        for a in range(2):
            for b in range(2):
                k = 2 * a + b
                p1[pl.ds(pb, TP // 4), k * 128 : (k + 1) * 128] = sn[a, :, b].reshape(TP // 4, 128)
        return 0

    lax.fori_loop(0, I // 2, dnf, 0)

    def to_patches(sn, ii, cc):
        v = sn.reshape(ii // 2, 2, cc // 2, 2, S, 128)
        return jnp.concatenate(
            [v[:, a, :, b].reshape(ii * cc * S // 4, 128) for a in range(2) for b in range(2)], axis=1
        )

    def from_patches(sp, ii, cc):
        ps = [sp[:, k * 128 : (k + 1) * 128].reshape(ii // 2, cc // 2, S, 128) for k in range(4)]
        rows = [jnp.stack([ps[2 * a], ps[2 * a + 1]], axis=2).reshape(ii // 2, cc, S, 128) for a in range(2)]
        return jnp.stack(rows, axis=1).reshape(ii * cc * S, 128)

    def put(at, value, blocks):
        for q in range(blocks):
            sums[at + q * 128 : at + (q + 1) * 128, :] = value[:, q * 128 : (q + 1) * 128].astype(bf16)

    l1 = (dot(p1[...], sw[0]) + sbias[0:1, :].astype(f32)).astype(bf16)
    h1, r1, sn1 = sect_norm(l1, 1)
    P2 = to_patches(sn1, I // 2, CW // 2)
    l2 = (dot(P2, sw[1]) + sbias[1:2, :].astype(f32)).astype(bf16)
    h2, r2, sn2 = sect_norm(l2, 2)
    P3 = to_patches(sn2, I // 4, CW // 4)
    l3 = (dot(P3, sw[2]) + sbias[2:3, :].astype(f32)).astype(bf16)
    Q = CW // 8
    for c in range(Q):
        x2d[pl.ds(c, S, stride=Q), :] = l3[c * S : (c + 1) * S, :].astype(f32)
    for r in range(S):
        bott[r] = x2d[r * Q : (r + 1) * Q, :].astype(bf16)
        x2d[128 + r * Q : 128 + (r + 1) * Q, :] = cot[r].astype(f32)
    b3 = jnp.concatenate([x2d[pl.ds(128 + c, S, stride=Q), :] for c in range(Q)], axis=0).astype(bf16)
    put(1024, dot_t(b3, P3), 4)
    u2 = from_patches(dot_r(b3, sw[2]), I // 4, CW // 4) * sgain[2:3, :].astype(f32)
    b2 = norm_bwd(u2, h2, r2, pm).astype(bf16)
    put(512, dot_t(b2, P2), 4)
    u1 = from_patches(dot_r(b2, sw[1]), I // 2, CW // 2) * sgain[1:2, :].astype(f32)
    b1 = norm_bwd(u1, h1, r1, pm).astype(bf16)
    put(0, dot_t(b1, p1[...]), 4)
    back[...] = b1

    QP = TP // 4

    def bk1(i2, _):
        pb = pl.multiple_of(i2 * QP, QP)
        bk = back[pl.ds(pb, QP), :]
        base = pl.multiple_of(i2 * TP, TP)
        us = []
        for a in range(2):
            sp = dot_r(bk, sw[0, a * 256 : (a + 1) * 256, :])
            us.append(
                jnp.stack(
                    [sp[:, :128].reshape(CW // 2, S, 128), sp[:, 128:].reshape(CW // 2, S, 128)], axis=1
                ).reshape(TP // 2, 128)
            )
        u = jnp.concatenate(us, axis=0) * sg0
        b0 = norm_bwd(u, shat[pl.ds(base, TP), :], srst[pl.ds(base, TP), :], pm).astype(bf16).astype(f32)
        dr = landb[pl.ds(base, TP), :].astype(f32) * b0
        dirout[pl.ds(base, TP), :] = dr.astype(bf16)
        mgs[pl.ds(base, TP), :] = (dr * sc).astype(bf16)
        return 0

    lax.fori_loop(0, I // 2, bk1, 0, unroll=2)

    def bk2(n, _):
        base = pl.multiple_of(n * T2, T2)
        mg = mgs[pl.ds(base, T2), :]
        for q in range(2):
            ag = dot_r(mg, dn[q * 256 : (q + 1) * 256, :])
            sl = slp[pl.ds(base, T2), q * 256 : (q + 1) * 256].astype(f32)
            slp[pl.ds(base, T2), q * 256 : (q + 1) * 256] = (ag * sl).astype(bf16)
        return 0

    lax.fori_loop(0, n0 // T2, bk2, 0)

    def bk3(n, _):
        base = pl.multiple_of(n * T1, T1)
        ng = dot_r(slp[pl.ds(base, T1), :], up[0:128, :])
        dg = norm_bwd(ng * g_n, hat[pl.ds(base, T1), :], rst[pl.ds(base, T1), :], pm)
        gout[pl.ds(base, T1), :] = dg.astype(bf16)
        return 0

    lax.fori_loop(0, n0 // T1, bk3, 0)
    downs[...] = dot_t(mgs[...], act[...]) * 0.5
    ups[...] = dot_t(nrm[...], slp[...])
    put(1536, downs[...], 4)
    put(2048, ups[...], 4)

    tacc[...] = jnp.zeros_like(tacc)

    def tap(n, _):
        i = n // (CW // 8)
        c0 = (n % (CW // 8)) * 8
        g = [gout[pl.ds((i * CW + c0 + k) * S, S), :].astype(f32) for k in range(8)]
        for a in range(7):
            row = [el[(i + a) * CE + c0 + m].astype(f32) for m in range(14)]
            for b in range(7):
                s = None
                for k in range(8):
                    pr = row[k + b] * g[k]
                    s = pr if s is None else s + pr
                tacc[a * 7 + b] += s[:8] + s[8:]
        return 0

    lax.fori_loop(0, I * (CW // 8), tap, 0)
    ts = [jnp.sum(tacc[t], axis=0, keepdims=True) for t in range(49)]
    ts = jnp.concatenate(ts + [jnp.zeros((15, 128), f32)], axis=0)
    sums[2560:2624, :] = ts.astype(bf16)
    sums[2624:2688, :] = jnp.zeros((64, 128), bf16)

    odd = lax.axis_index("lat") % 2
    keep[...] = sums[pl.ds(pl.multiple_of(odd * HALF, 64), HALF), :]
    away[0:HALF, :] = sums[pl.ds(pl.multiple_of((1 - odd) * HALF, 64), HALF), :]
    x2d[0:n0, :] = gout[...].astype(f32)
    for k in range(3):
        lo = x2d[pl.ds(k * CW * S, CW, stride=S), :].astype(bf16)
        hi = x2d[pl.ds((I - 3 + k) * CW * S + S - 1, CW, stride=S), :].astype(bf16)
        last[k] = hi
        send[k] = jnp.where(odd == 1, hi, lo)
        away[HALF + k * CW : HALF + (k + 1) * CW, :] = jnp.where(odd == 1, lo, hi)
    for i in range(I):
        lcol[i * 3 * S : (i + 1) * 3 * S, :] = gout[i * CW * S : (i * CW + 3) * S, :]
        rcol[i * 3 * S : (i + 1) * 3 * S, :] = gout[((i + 1) * CW - 3) * S : (i + 1) * CW * S, :]


def block_pass(field, south, north, left, right, land, dw, gain, upw, bias, down, scale, sgain, sw, sbias, cot):
    R, CW, C = field.shape
    n = R * CW
    I = R // S
    sd = jax.ShapeDtypeStruct
    out_shape = (
        sd((S, CW // 8, C), bf16),
        sd((n, C), bf16),
        sd((n, C), bf16),
        sd((3, CW, C), bf16),
        sd((3, CW, C), bf16),
        sd((I * 3 * S, C), bf16),
        sd((I * 3 * S, C), bf16),
        sd((HALF, C), bf16),
        sd((HALF + 3 * CW, C), bf16),
    )
    V = pltpu.VMEM
    scratch = [
        V(((R + 6) * 40 + (R + 6) // I + 16, C), f32),
        V(((I + 6) * (CW + 6), S, C), bf16),
        V((49, S, C), bf16),
        V((n, C), f32),
        V((n, C), f32),
        V((n, C), f32),
        V((n, C), bf16),
        V((n, 512), bf16),
        V((n, 512), bf16),
        V((n, C), f32),
        V((n, C), f32),
        V((n // 4, 512), bf16),
        V((n // 4, C), bf16),
        V((49, 8, C), f32),
        V((C, 512), f32),
        V((C, 512), f32),
        V((n, C), bf16),
        V((n, C), bf16),
        V((256, 512), bf16),
        V((512, 128), bf16),
        V((2 * HALF, C), bf16),
    ]
    return pl.pallas_call(
        functools.partial(block_body, R, CW),
        out_shape=out_shape,
        in_specs=[VMEM] * 16,
        out_specs=[VMEM] * 9,
        scratch_shapes=scratch,
        compiler_params=PARAMS,
        name="block_pass",
    )(field, south, north, left, right, land, dw, gain, upw, bias, down, scale, sgain, sw, sbias, cot)


def conv_back_body(R, CW, g, dirin, dw, out, gx, gext, w49):
    I = R // S
    CE = CW + 6
    row = lax.broadcasted_iota(jnp.int32, (S, 128), 0)
    zero = jnp.zeros((3, S, 128), bf16)

    def cpy(i, _):
        gext[pl.ds((i + 3) * CE, 3)] = zero
        gext[pl.ds((i + 3) * CE + 3, CW)] = g[pl.ds(pl.multiple_of(i * CW * S, CW * S), CW * S), :].reshape(CW, S, 128)
        gext[pl.ds((i + 3) * CE + 3 + CW, 3)] = zero
        return 0

    lax.fori_loop(0, I, cpy, 0)
    for k in range(3):

        def shift(c, _, k=k):
            v = pltpu.roll(gext[(I + k) * CE + c].astype(f32), 1, 0)
            gext[k * CE + c] = jnp.where(row == 0, 0.0, v).astype(bf16)
            v = pltpu.roll(gext[(3 + k) * CE + c].astype(f32), S - 1, 0)
            gext[(I + 3 + k) * CE + c] = jnp.where(row == S - 1, 0.0, v).astype(bf16)
            return 0

        lax.fori_loop(0, CE, shift, 0, unroll=2)
    weights_table(dw, w49, True)

    def emit(i, c, v):
        at = pl.multiple_of((i * CW + c) * S, S)
        out[pl.ds(at, S), :] = v + dirin[pl.ds(at, S), :].astype(f32)

    conv49(gext, w49, emit, I, CW)


def conv_back(g, dirin, dw, R, CW):
    C = g.shape[1]
    I = R // S
    return pl.pallas_call(
        functools.partial(conv_back_body, R, CW),
        out_shape=jax.ShapeDtypeStruct((R * CW, C), f32),
        in_specs=[VMEM] * 3,
        out_specs=VMEM,
        scratch_shapes=[
            pltpu.VMEM((8, C), f32),
            pltpu.VMEM(((I + 6) * (CW + 6), S, C), bf16),
            pltpu.VMEM((49, S, C), bf16),
        ],
        compiler_params=SMALL,
        cost_estimate=pl.CostEstimate(flops=10**8, bytes_accessed=30 * 2**20, transcendentals=0),
        name="conv_back",
    )(g, dirin, dw)


def edges_body(R, CW, base, south, north, gl, gr, dw, out, acc, rows, cols, w49):
    I = R // S
    CE = CW + 6
    isn = on_top().astype(f32)
    nots = 1.0 - isn
    core = I * 3 * S
    row = lax.broadcasted_iota(jnp.int32, (S, 128), 0)
    for t in range(49):
        w49[t] = jnp.broadcast_to(dw[t : t + 1, :].astype(f32), (S, 128))
    for side in range(2):
        for k in range(3):
            at = core + side * 9 + k * 3
            mid = (north if side else south)[k]
            rows[pl.ds((side * 3 + k) * 40, CE), :] = jnp.concatenate(
                [gl[at : at + 3, :], mid, gr[at : at + 3, :]], axis=0
            ).astype(f32)

    def taps(k, a, flip):
        s = None
        for b in range(7):
            o = 6 - b if flip else b
            pr = rows[pl.ds(k * 40 + o, CW), :] * w49[7 * a + b, 0:1, :]
            s = pr if s is None else s + pr
        return s

    low = []
    for r in range(3):
        low.append(sum(taps(k, r + 6 - k, True) for k in range(r, 3)))
    high = []
    for t in range(3):
        v = sum(taps(3 + k, 2 - t - k, True) for k in range(3 - t)) * nots
        k1 = t + 1
        f = sum(taps(3 + rho, 5 + k1 - rho, False) for rho in range(k1 - 1, 3)) * isn
        high.append(v + f)
    for side in range(2):
        src = gr if side else gl

        def fill(i, _, src=src, side=side):
            for j in range(3):
                at = pl.multiple_of((i * 3 + j) * S, S)
                cols[side * (I + 6) * 3 + (i + 3) * 3 + j] = src[pl.ds(at, S), :].astype(f32)
            return 0

        lax.fori_loop(0, I, fill, 0)
        for k in range(3):
            for j in range(3):
                at = side * (I + 6) * 3
                v = pltpu.roll(cols[at + (I + k) * 3 + j], 1, 0)
                cols[at + k * 3 + j] = jnp.where(row == 0, 0.0, v)
                v = pltpu.roll(cols[at + (3 + k) * 3 + j], S - 1, 0)
                cols[at + (I + 3 + k) * 3 + j] = jnp.where(row == S - 1, 0.0, v)

    PITCH = CW * S

    def step(i, _):
        at = pl.multiple_of(i * PITCH, PITCH)
        acc[pl.ds(at, PITCH), :] = base[pl.ds(at, PITCH), :]
        for side in range(2):
            for t in range(3):
                s = None
                for j in range(3):
                    b = 2 - t - j if side else t + 6 - j
                    if b < 0 or b > 6:
                        continue
                    for a in range(7):
                        pr = cols[side * (I + 6) * 3 + (i + 6 - a) * 3 + j] * w49[7 * a + b]
                        s = pr if s is None else s + pr
                c = CW - 1 - t if side else t
                at = pl.multiple_of(i * PITCH + c * S, S)
                acc[pl.ds(at, S), :] += s
        return 0

    lax.fori_loop(0, I, step, 0)

    def unt(r, _):
        s = r // I
        i = r % I
        out[r] = acc[pl.ds(i * PITCH + s, CW, stride=S), :].astype(bf16)
        return 0

    lax.fori_loop(3, R - 3, unt, 0, unroll=2)
    for r in list(range(3)) + list(range(R - 3, R)):
        v = acc[pl.ds((r % I) * PITCH + r // I, CW, stride=S), :]
        v = v + (low[r] if r < 3 else high[R - 1 - r])
        out[r] = v.astype(bf16)


def edges(base, south, north, gl, gr, dw, R, CW):
    C = base.shape[1]
    I = R // S
    return pl.pallas_call(
        functools.partial(edges_body, R, CW),
        out_shape=jax.ShapeDtypeStruct((R, CW, C), bf16),
        in_specs=[VMEM] * 6,
        out_specs=VMEM,
        scratch_shapes=[
            pltpu.VMEM((R * CW, C), f32),
            pltpu.VMEM((240, C), f32),
            pltpu.VMEM((2 * (I + 6) * 3, S, C), f32),
            pltpu.VMEM((49, S, C), f32),
        ],
        compiler_params=SMALL,
        cost_estimate=pl.CostEstimate(flops=10**8, bytes_accessed=10 * 2**20, transcendentals=0),
        name="edges",
    )(base, south, north, gl, gr, dw)


def finish_body(factor, chunk, mine, other, o_depth, o_up, o_down, o_sec, full):
    core = lax.axis_index("lat") % 2
    place = (lax.axis_index("lat") // 2) * 2 + lax.axis_index("lon") % 2
    half = 4 * chunk
    for j in range(4):
        src = lax.bitwise_xor(place, j)
        at = pl.multiple_of(core * half + j * chunk, 16)
        full[pl.ds(at, chunk), :] = mine[src]
        at = pl.multiple_of((1 - core) * half + j * chunk, 16)
        full[pl.ds(at, chunk), :] = other[src]

    def block(n):
        return full[n * 128 : (n + 1) * 128, :].astype(f32) * factor

    for s in range(3):
        for q in range(4):
            o_sec[s, q * 128 : (q + 1) * 128, :] = block(s * 4 + q).T
    for q in range(4):
        o_down[q * 128 : (q + 1) * 128, :] = block(12 + q).T
        o_up[:, q * 128 : (q + 1) * 128] = block(16 + q)
    o_depth[...] = block(20)[:49, :]


def finish(mine, other, factor):
    chunk = mine.shape[1]
    sd = jax.ShapeDtypeStruct
    return pl.pallas_call(
        functools.partial(finish_body, factor, chunk),
        out_shape=(sd((49, 128), f32), sd((128, 512), f32), sd((512, 128), f32), sd((3, 512, 128), f32)),
        in_specs=[VMEM, VMEM],
        out_specs=[VMEM] * 4,
        scratch_shapes=[pltpu.VMEM((8 * chunk, 128), bf16)],
        compiler_params=SMALL,
        name="finish_sums",
    )(mine, other)


def add_bf(*vals):
    vals = [v.astype(f32) for v in vals]
    while len(vals) > 1:
        vals = [vals[i] + vals[i + 1] for i in range(0, len(vals), 2)]
    return vals[0].astype(bf16)


def flip_pairs(axis, bits):
    return [(i, i ^ bits) for i in range(lax.axis_size(axis))]


def both_pairs(lat_bits, lon_bits):
    nl = lax.axis_size("lon")
    return [
        (a * nl + b, (a ^ lat_bits) * nl + (b ^ lon_bits))
        for a in range(lax.axis_size("lat"))
        for b in range(nl)
    ]


def square_pairs(k):
    return both_pairs((k // 2) * 2, k % 2)


def square_sum(held, place):
    own = lax.dynamic_index_in_dim(held, place, 0, keepdims=False)
    came = []
    for k in (1, 2, 3):
        part = lax.dynamic_index_in_dim(held, lax.bitwise_xor(place, k), 0, keepdims=False)
        came.append(lax.ppermute(part, ("lat", "lon"), square_pairs(k)))
    return add_bf(own, *came)


def line_sum(total):
    left = lax.axis_size("lon") // 2
    bit = 2
    while left > 1:
        if left % 4 == 0:
            total = add_bf(total, *[lax.ppermute(total, "lon", flip_pairs("lon", bit * k)) for k in (1, 2, 3)])
            left //= 4
            bit *= 4
        else:
            total = add_bf(total, lax.ppermute(total, "lon", flip_pairs("lon", bit)))
            left //= 2
            bit *= 2
    return total


def on_top():
    return lax.axis_index("lat") == lax.axis_size("lat") - 1


def rim_body(R, CW, field, mirror, near, send, last, place, low, high, mir, sems):
    odd = lax.axis_index("lat") % 2
    copies = [
        pltpu.make_async_copy(mirror, mir, sems.at[0]),
        pltpu.make_async_copy(field.at[0:3], low, sems.at[1]),
        pltpu.make_async_copy(field.at[R - 3 : R], high, sems.at[2]),
    ]
    for c in copies:
        c.start()
    for c in copies:
        c.wait()
    for k in range(3):
        lo = low[k]
        hi = high[k]
        last[k] = hi
        send[k] = jnp.where(odd == 1, hi, lo)
        near[k] = jnp.where(odd == 1, lo, hi)
    place[0] = mir[0] // CW
    place[1] = mir[0] % CW


def rim(field, mirror):
    R, CW, C = field.shape
    sd = jax.ShapeDtypeStruct
    hbm = pl.BlockSpec(memory_space=pltpu.HBM)
    return pl.pallas_call(
        functools.partial(rim_body, R, CW),
        out_shape=(sd((3, CW, C), bf16),) * 3 + (sd((2,), jnp.int32),),
        in_specs=[hbm, hbm],
        out_specs=[VMEM] * 3 + [SMEM],
        scratch_shapes=[
            pltpu.VMEM((3, CW, C), bf16),
            pltpu.VMEM((3, CW, C), bf16),
            pltpu.SMEM(mirror.shape, jnp.int32),
            pltpu.SemaphoreType.DMA((3,)),
        ],
        compiler_params=WHOLE,
        name="rim",
    )(field, mirror)


def sides_body(R, CW, field, lc, rc, low, high, cols, sems):
    copies = [
        pltpu.make_async_copy(field.at[:, 0:16], low, sems.at[0]),
        pltpu.make_async_copy(field.at[:, CW - 16 : CW], high, sems.at[1]),
    ]
    for c in copies:
        c.start()
    for c in copies:
        c.wait()
    cols[0 : R * 8, :] = low[:, 0:8, :].astype(f32).reshape(R * 8, 128)
    cols[R * 8 :, :] = high[:, 8:16, :].astype(f32).reshape(R * 8, 128)
    for k in range(3):
        lc[k] = cols[pl.ds(k, R, stride=8), :].astype(bf16)
        rc[k] = cols[pl.ds(R * 8 + 5 + k, R, stride=8), :].astype(bf16)


def sides(field):
    R, CW, C = field.shape
    sd = jax.ShapeDtypeStruct
    return pl.pallas_call(
        functools.partial(sides_body, R, CW),
        out_shape=(sd((3, R, C), bf16),) * 2,
        in_specs=[pl.BlockSpec(memory_space=pltpu.HBM)],
        out_specs=[VMEM] * 2,
        scratch_shapes=[
            pltpu.VMEM((R, 16, C), bf16),
            pltpu.VMEM((R, 16, C), bf16),
            pltpu.VMEM((2 * R * 8, C), f32),
            pltpu.SemaphoreType.DMA((2,)),
        ],
        compiler_params=SMALL,
        name="sides",
    )(field)


def join_body(CW, width, flip, place, near, far, blk_b, lc, rc, south, north, lp, rp, cat, scr):
    odd = lax.axis_index("lat") % 2 == 1
    top = on_top()
    rem = place[1]
    at = lax.broadcasted_iota(jnp.int32, (CW, CW), 0)
    turn = (at + lax.broadcasted_iota(jnp.int32, (CW, CW), 1) == CW - 1).astype(f32).astype(bf16)
    for k in range(3):
        cat[0:CW, :] = blk_b[k].astype(f32)
        cat[CW : 2 * CW, :] = far[k].astype(f32)
        win = cat[pl.ds(rem + 1, CW), :].astype(bf16)
        scr[k * CW : (k + 1) * CW, :] = dot(turn, win)
    for k in range(3):
        m = 2 - k if flip else k
        beyond = scr[m * CW : (m + 1) * CW, :]
        above = jnp.where(odd, far[k].astype(f32), near[k].astype(f32))
        below = jnp.where(odd, near[k].astype(f32), far[k].astype(f32))
        above = jnp.where(top, beyond, above)
        south[k] = below.astype(bf16)
        north[k] = above.astype(bf16)
        scr[(3 + k) * CW : (4 + k) * CW, :] = below
        scr[(6 + k) * CW : (7 + k) * CW, :] = above
    for pay, core, lo in ((lp, lc, 0), (rp, rc, CW - 3)):
        if flip:
            for j in range(3):
                for k in range(3):
                    cat[k : k + 1, :] = scr[(3 + k) * CW + lo + j : (3 + k) * CW + lo + j + 1, :]
                    cat[3 + width + k : 4 + width + k, :] = scr[(6 + k) * CW + lo + j : (6 + k) * CW + lo + j + 1, :]
                cat[3 : 3 + width, :] = core[j].astype(f32)
                pay[j] = cat[0 : width + 6, :].astype(bf16)
        else:
            pay[0:width, :] = core[...]
            for end in range(2):
                for k in range(3):
                    src = (3 + 3 * end + k) * CW + lo
                    cat[end * 9 + k * 3 : end * 9 + k * 3 + 3, :] = scr[src : src + 3, :]
            pay[width : width + 32, :] = cat[0:32, :].astype(bf16)


def join(place, near, far, blk_b, lc, rc, flip):
    CW, C = near.shape[1:]
    width = lc.shape[1] if flip else lc.shape[0]
    sd = jax.ShapeDtypeStruct
    pay = sd((3, width + 6, C) if flip else (width + 32, C), bf16)
    return pl.pallas_call(
        functools.partial(join_body, CW, width, flip),
        out_shape=(sd((3, CW, C), bf16),) * 2 + (pay, pay),
        in_specs=[SMEM] + [VMEM] * 5,
        out_specs=[VMEM] * 4,
        scratch_shapes=[pltpu.VMEM((max(2 * CW + 8, width + 8), C), f32), pltpu.VMEM((9 * CW, C), f32)],
        compiler_params=SMALL,
        name="join",
    )(place, near, far, blk_b, lc, rc)


def far_rows(send, last, quot, work=lambda: ()):
    nl = lax.axis_size("lon")
    nt = lax.axis_size("lat")
    top = (nt - 1) * nl
    axes = ("lat", "lon")
    swap = [(a * nl + e, (a + 1) * nl + e) for a in range(1, nt - 1, 2) for e in range(nl)]
    swap += [(j, i) for i, j in swap]

    def branch(q):
        def run():
            fa = [(top + e, top + (q - e) % nl) for e in range(nl)]
            fb = [(top + e, top + (q - 1 - e) % nl) for e in range(nl)]
            return lax.ppermute(send, axes, swap + fa), lax.ppermute(last, axes, fb), work()

        return run

    return lax.switch(quot, [branch(q) for q in range(nl)])


def shift_pairs(axis, by):
    n = lax.axis_size(axis)
    return [(i, (i + by) % n) for i in range(n)]


def on_device(
    field, land, mirror, depth_weight, norm_gain, up_weight, up_bias, down_proj, layer_scale,
    section_gain, section_weight, section_bias, cotangent,
):
    R, CW, C = field.shape
    total = R * CW * lax.axis_size("lat") * lax.axis_size("lon")
    factor = 1.0 / math.sqrt(total / 64.0)
    near, send, last, shift = rim(field, mirror)
    near = lax.ppermute(near, "lat", flip_pairs("lat", 1))
    far, blk_b, (lc, rc) = far_rows(send, last, shift[0], lambda: sides(field))
    south_f, north_f, lpay, rpay = join(shift, near, far, blk_b, lc, rc, True)
    right_f = lax.ppermute(lpay, "lon", shift_pairs("lon", -1))
    left_f = lax.ppermute(rpay, "lon", shift_pairs("lon", 1))
    level, g, direct, send, last, lcol, rcol, keep, away = block_pass(
        field, south_f, north_f, left_f, right_f, land.T, depth_weight, norm_gain, up_weight, up_bias, down_proj,
        layer_scale, section_gain, section_weight, section_bias, cotangent,
    )

    place = (lax.axis_index("lat") // 2) * 2 + lax.axis_index("lon") % 2
    got = lax.ppermute(away, "lat", flip_pairs("lat", 1))
    near = got[HALF:].reshape(3, CW, C)
    held = add_bf(keep, got[:HALF]).reshape(4, HALF // 4, C)
    send, held = lax.optimization_barrier((send, held))
    chunk = square_sum(held, place)
    far, blk_b, base = far_rows(
        send, last, shift[0], lambda: conv_back(g, direct, depth_weight, R, CW)
    )
    chunk, far = lax.optimization_barrier((chunk, far))
    south_g, north_g, lpay, rpay = join(shift, near, far, blk_b, lcol, rcol, False)
    chunk, lpay = lax.optimization_barrier((chunk, lpay))
    gr = lax.ppermute(lpay, "lon", shift_pairs("lon", -1))
    gl = lax.ppermute(rpay, "lon", shift_pairs("lon", 1))
    chunk = line_sum(chunk)
    grad_field = edges(base, south_g, north_g, gl, gr, depth_weight, R, CW)
    axes = ("lat", "lon")
    back = [lax.ppermute(chunk, axes, square_pairs(k)) for k in (1, 2, 3)]
    back[0], grad_field = lax.optimization_barrier((back[0], grad_field))
    mine = jnp.stack([chunk] + back)
    other = lax.ppermute(mine, "lat", flip_pairs("lat", 1))
    g_depth, g_up, g_down, g_sec = finish(mine, other, factor)
    return level, grad_field, g_depth, g_up, g_down, g_sec


def solution(mesh):
    cells = P("lat", "lon", None)
    in_specs = (cells, P("lat", "lon")) + (P(),) * 10 + (cells,)
    out_specs = (cells, cells, P(), P(), P(), P())
    return jax.shard_map(on_device, mesh=mesh, in_specs=in_specs, out_specs=out_specs, check_vma=False)
```

```python
import functools
import math

import jax
import jax.numpy as jnp
from jax import lax
from jax.experimental import pallas as pl
from jax.experimental.pallas import tpu as pltpu
from jax.sharding import PartitionSpec as P

SECTIONS = 3
EPS = 1e-6
f32, bf16 = jnp.float32, jnp.bfloat16
S = 16
LOG2E = 1.4426950408889634
LOG2_DENS = -0.3257480647361593
HALF = 1344
VMEM = pl.BlockSpec(memory_space=pltpu.VMEM)
SMEM = pl.BlockSpec(memory_space=pltpu.SMEM)
PARAMS = pltpu.CompilerParams(vmem_limit_bytes=44 * 2**20)
WHOLE = pltpu.CompilerParams(vmem_limit_bytes=63 * 2**20 + 2**19)
SMALL = pltpu.CompilerParams(vmem_limit_bytes=24 * 2**20)


def dot(a, b):
    return jnp.dot(a, b, preferred_element_type=f32)


def dot_t(a, b):
    return lax.dot_general(a, b, (((0,), (0,)), ((), ())), preferred_element_type=f32)


def dot_r(a, b):
    return lax.dot_general(a, b, (((1,), (1,)), ((), ())), preferred_element_type=f32)


def ones_mean(n):
    return jnp.full((n, 128), 1.0 / 128, bf16)


def pair_mean():
    r = lax.broadcasted_iota(jnp.int32, (256, 256), 0) // 128
    c = lax.broadcasted_iota(jnp.int32, (256, 256), 1) // 128
    return jnp.where(r == c, 1.0 / 128, 0.0).astype(bf16)


def split2(x):
    hi = x.astype(bf16)
    lo = (x - hi.astype(f32)).astype(bf16)
    return jnp.concatenate([hi, lo], axis=1)


def norm_bwd(u, hat, rstd, pm):
    m = dot(jnp.concatenate([u.astype(bf16), (u * hat).astype(bf16)], axis=1), pm)
    return rstd * (u - m[:, :128] - hat * m[:, 128:])


def gelu2(h):
    g = h * 0.7071067811865476
    c = 1.0 + lax.erf(g)
    e = jnp.exp2(g * g * (-LOG2E) + LOG2_DENS)
    return h * c, c + h * e


def weights_table(dw, w49, flip):
    for t in range(49):
        w49[48 - t if flip else t] = jnp.broadcast_to(dw[t : t + 1, :].astype(f32), (S, 128)).astype(w49.dtype)


def conv49(el, w49, emit, I, CW):
    CE = CW + 6
    CG = 4

    def step(n, _):
        i = n // (CW // CG)
        c0 = (n % (CW // CG)) * CG
        acc = [None] * CG
        for a in range(7):
            row = [el[(i + a) * CE + c0 + m].astype(f32) for m in range(CG + 6)]
            for b in range(7):
                w = w49[a * 7 + b].astype(f32)
                for k in range(CG):
                    pr = row[k + b] * w
                    acc[k] = pr if acc[k] is None else acc[k] + pr
        for k in range(CG):
            emit(i, c0 + k, acc[k])
        return 0

    lax.fori_loop(0, I * (CW // CG), step, 0)


def block_body(
    R, CW,
    field, south, north, left, right, land, dw, gain, upw, bias, down, scale, sgain, sw, sbias, cot,
    bott, gout, dirout, send, last, lcol, rcol, keep, away,
    x2d, el, w49, dep, hat, rst, nrm, act, slp, shat, srst, p1, back, tacc, downs, ups, mgs, landb, up, dn, sums,
):
    I = R // S
    CE = CW + 6
    XW = 40
    n0 = R * CW

    def asm(r, _):
        x2d[pl.ds((r + 3) * XW + (r + 3) // I + 3, CW), :] = field[r].astype(f32)
        return 0

    lax.fori_loop(0, R, asm, 0, unroll=4)
    PB = I * XW + 1
    for k in range(3):
        x2d[pl.ds(k * XW + 3, CW), :] = south[k].astype(f32)
        x2d[pl.ds((R + 3 + k) * XW + (R + 3 + k) // I + 3, CW), :] = north[k].astype(f32)
        for m in range((R + 6 + I - 1) // I):
            rows = min(I, R + 6 - m * I)
            x2d[pl.ds(m * PB + k, rows, stride=XW), :] = left[k, m * I : m * I + rows, :].astype(f32)
            x2d[pl.ds(m * PB + CW + 3 + k, rows, stride=XW), :] = right[k, m * I : m * I + rows, :].astype(f32)

    def tr(i, _):
        for c in range(CE):
            el[i * CE + c] = x2d[pl.ds(i * XW + i // I + c, S, stride=PB), :].astype(bf16)
        return 0

    lax.fori_loop(0, I + 6, tr, 0)
    weights_table(dw, w49, False)
    p_at = lax.broadcasted_iota(jnp.int32, (R, R), 0)
    p_row = lax.broadcasted_iota(jnp.int32, (R, R), 1)
    order = (p_row == (p_at % S) * I + p_at // S).astype(f32).astype(bf16)
    land_p = dot_r(order, land[...].astype(f32).astype(bf16)).astype(bf16)
    spread = (
        lax.broadcasted_iota(jnp.int32, (CW, CW * 128), 1) // 128
        == lax.broadcasted_iota(jnp.int32, (CW, CW * 128), 0)
    )
    land_w = dot(land_p, spread.astype(f32).astype(bf16)).astype(bf16)
    for i in range(I):
        for c in range(CW):
            at = (i * CW + c) * S
            landb[at : at + S, :] = land_w[i * S : (i + 1) * S, c * 128 : (c + 1) * 128]
    dn[...] = (down[...].astype(f32) * 0.5).astype(bf16)
    up[0:128, :] = upw[...]
    up[128:256, :] = jnp.where(
        lax.broadcasted_iota(jnp.int32, (128, 512), 0) == 0, bias[...].astype(f32).reshape(1, 512), 0.0
    ).astype(bf16)

    def emit(i, c, v):
        dep[pl.ds((i * CW + c) * S, S), :] = v

    conv49(el, w49, emit, I, CW)

    jj, j1, pm = ones_mean(256), ones_mean(128), pair_mean()
    g_n = gain[...].astype(f32).reshape(1, 128)
    sc = scale[...].astype(f32).reshape(1, 128)
    sg0 = sgain[0:1, :].astype(f32)
    T1 = n0

    def nfwd(n, _):
        base = pl.multiple_of(n * T1, T1)
        x = dep[pl.ds(base, T1), :]
        cen = x - dot(split2(x), jj)
        rs = lax.rsqrt(dot((cen * cen).astype(bf16), j1) + EPS)
        ht = cen * rs
        hat[pl.ds(base, T1), :] = ht
        rst[pl.ds(base, T1), :] = rs
        nrm[pl.ds(base, T1), :] = (ht * g_n).astype(bf16)
        return 0

    lax.fori_loop(0, n0 // T1, nfwd, 0)

    T2 = n0 // 4
    onec = (lax.broadcasted_iota(jnp.int32, (T2, 128), 1) == 0).astype(f32).astype(bf16)

    def upf(n, _):
        base = pl.multiple_of(n * T2, T2)
        lhs = jnp.concatenate([nrm[pl.ds(base, T2), :], onec], axis=1)
        for q in range(2):
            hid = dot(lhs, up[:, q * 256 : (q + 1) * 256])
            ac, sl = gelu2(hid)
            act[pl.ds(base, T2), q * 256 : (q + 1) * 256] = ac.astype(bf16)
            slp[pl.ds(base, T2), q * 256 : (q + 1) * 256] = sl.astype(bf16)
        return 0

    lax.fori_loop(0, n0 // T2, upf, 0)

    TP = 2 * CW * S

    def sect_norm(lv, s):
        cen = lv.astype(f32) - dot(lv, j1)
        rs1 = lax.rsqrt(dot((cen * cen).astype(bf16), j1) + EPS)
        h1 = cen * rs1
        return h1, rs1, (h1 * sgain[s : s + 1, :].astype(f32)).astype(bf16)

    def dnf(i2, _):
        base = pl.multiple_of(i2 * TP, TP)
        mixed = dot(act[pl.ds(base, TP), :], dn[...])
        xs = jnp.concatenate(
            [el[pl.ds((i2 * 2 + a + 3) * CE + 3, CW)].reshape(CW * S, 128) for a in range(2)], axis=0
        ).astype(f32)
        lv = (landb[pl.ds(base, TP), :].astype(f32) * (xs + sc * mixed)).astype(bf16)
        h1, rs1, sn = sect_norm(lv, 0)
        shat[pl.ds(base, TP), :] = h1
        srst[pl.ds(base, TP), :] = rs1
        sn = sn.reshape(2, CW // 2, 2, S, 128)
        pb = pl.multiple_of(i2 * (TP // 4), TP // 4)
        for a in range(2):
            for b in range(2):
                k = 2 * a + b
                p1[pl.ds(pb, TP // 4), k * 128 : (k + 1) * 128] = sn[a, :, b].reshape(TP // 4, 128)
        return 0

    lax.fori_loop(0, I // 2, dnf, 0)

    def to_patches(sn, ii, cc):
        v = sn.reshape(ii // 2, 2, cc // 2, 2, S, 128)
        return jnp.concatenate(
            [v[:, a, :, b].reshape(ii * cc * S // 4, 128) for a in range(2) for b in range(2)], axis=1
        )

    def from_patches(sp, ii, cc):
        ps = [sp[:, k * 128 : (k + 1) * 128].reshape(ii // 2, cc // 2, S, 128) for k in range(4)]
        rows = [jnp.stack([ps[2 * a], ps[2 * a + 1]], axis=2).reshape(ii // 2, cc, S, 128) for a in range(2)]
        return jnp.stack(rows, axis=1).reshape(ii * cc * S, 128)

    def put(at, value, blocks):
        for q in range(blocks):
            sums[at + q * 128 : at + (q + 1) * 128, :] = value[:, q * 128 : (q + 1) * 128].astype(bf16)

    l1 = (dot(p1[...], sw[0]) + sbias[0:1, :].astype(f32)).astype(bf16)
    h1, r1, sn1 = sect_norm(l1, 1)
    P2 = to_patches(sn1, I // 2, CW // 2)
    l2 = (dot(P2, sw[1]) + sbias[1:2, :].astype(f32)).astype(bf16)
    h2, r2, sn2 = sect_norm(l2, 2)
    P3 = to_patches(sn2, I // 4, CW // 4)
    l3 = (dot(P3, sw[2]) + sbias[2:3, :].astype(f32)).astype(bf16)
    Q = CW // 8
    for c in range(Q):
        x2d[pl.ds(c, S, stride=Q), :] = l3[c * S : (c + 1) * S, :].astype(f32)
    for r in range(S):
        bott[r] = x2d[r * Q : (r + 1) * Q, :].astype(bf16)
        x2d[128 + r * Q : 128 + (r + 1) * Q, :] = cot[r].astype(f32)
    b3 = jnp.concatenate([x2d[pl.ds(128 + c, S, stride=Q), :] for c in range(Q)], axis=0).astype(bf16)
    put(1024, dot_t(b3, P3), 4)
    u2 = from_patches(dot_r(b3, sw[2]), I // 4, CW // 4) * sgain[2:3, :].astype(f32)
    b2 = norm_bwd(u2, h2, r2, pm).astype(bf16)
    put(512, dot_t(b2, P2), 4)
    u1 = from_patches(dot_r(b2, sw[1]), I // 2, CW // 2) * sgain[1:2, :].astype(f32)
    b1 = norm_bwd(u1, h1, r1, pm).astype(bf16)
    put(0, dot_t(b1, p1[...]), 4)
    back[...] = b1

    QP = TP // 4

    def bk1(i2, _):
        pb = pl.multiple_of(i2 * QP, QP)
        bk = back[pl.ds(pb, QP), :]
        base = pl.multiple_of(i2 * TP, TP)
        us = []
        for a in range(2):
            sp = dot_r(bk, sw[0, a * 256 : (a + 1) * 256, :])
            us.append(
                jnp.stack(
                    [sp[:, :128].reshape(CW // 2, S, 128), sp[:, 128:].reshape(CW // 2, S, 128)], axis=1
                ).reshape(TP // 2, 128)
            )
        u = jnp.concatenate(us, axis=0) * sg0
        b0 = norm_bwd(u, shat[pl.ds(base, TP), :], srst[pl.ds(base, TP), :], pm).astype(bf16).astype(f32)
        dr = landb[pl.ds(base, TP), :].astype(f32) * b0
        dirout[pl.ds(base, TP), :] = dr.astype(bf16)
        mgs[pl.ds(base, TP), :] = (dr * sc).astype(bf16)
        return 0

    lax.fori_loop(0, I // 2, bk1, 0, unroll=4)

    def bk2(n, _):
        base = pl.multiple_of(n * T2, T2)
        mg = mgs[pl.ds(base, T2), :]
        for q in range(2):
            ag = dot_r(mg, dn[q * 256 : (q + 1) * 256, :])
            sl = slp[pl.ds(base, T2), q * 256 : (q + 1) * 256].astype(f32)
            slp[pl.ds(base, T2), q * 256 : (q + 1) * 256] = (ag * sl).astype(bf16)
        return 0

    lax.fori_loop(0, n0 // T2, bk2, 0)

    def bk3(n, _):
        base = pl.multiple_of(n * T1, T1)
        ng = dot_r(slp[pl.ds(base, T1), :], up[0:128, :])
        dg = norm_bwd(ng * g_n, hat[pl.ds(base, T1), :], rst[pl.ds(base, T1), :], pm)
        gout[pl.ds(base, T1), :] = dg.astype(bf16)
        return 0

    lax.fori_loop(0, n0 // T1, bk3, 0)
    downs[...] = dot_t(mgs[...], act[...]) * 0.5
    ups[...] = dot_t(nrm[...], slp[...])
    put(1536, downs[...], 4)
    put(2048, ups[...], 4)

    tacc[...] = jnp.zeros_like(tacc)

    def tap(n, _):
        i = n // (CW // 8)
        c0 = (n % (CW // 8)) * 8
        g = [gout[pl.ds((i * CW + c0 + k) * S, S), :].astype(f32) for k in range(8)]
        for a in range(7):
            row = [el[(i + a) * CE + c0 + m].astype(f32) for m in range(14)]
            for b in range(7):
                s = None
                for k in range(8):
                    pr = row[k + b] * g[k]
                    s = pr if s is None else s + pr
                tacc[a * 7 + b] += s[:8] + s[8:]
        return 0

    lax.fori_loop(0, I * (CW // 8), tap, 0)
    ts = [jnp.sum(tacc[t], axis=0, keepdims=True) for t in range(49)]
    ts = jnp.concatenate(ts + [jnp.zeros((15, 128), f32)], axis=0)
    sums[2560:2624, :] = ts.astype(bf16)
    sums[2624:2688, :] = jnp.zeros((64, 128), bf16)

    odd = lax.axis_index("lat") % 2
    keep[...] = sums[pl.ds(pl.multiple_of(odd * HALF, 64), HALF), :]
    away[0:HALF, :] = sums[pl.ds(pl.multiple_of((1 - odd) * HALF, 64), HALF), :]
    x2d[0:n0, :] = gout[...].astype(f32)
    for k in range(3):
        lo = x2d[pl.ds(k * CW * S, CW, stride=S), :].astype(bf16)
        hi = x2d[pl.ds((I - 3 + k) * CW * S + S - 1, CW, stride=S), :].astype(bf16)
        last[k] = hi
        send[k] = jnp.where(odd == 1, hi, lo)
        away[HALF + k * CW : HALF + (k + 1) * CW, :] = jnp.where(odd == 1, lo, hi)
    for i in range(I):
        lcol[i * 3 * S : (i + 1) * 3 * S, :] = gout[i * CW * S : (i * CW + 3) * S, :]
        rcol[i * 3 * S : (i + 1) * 3 * S, :] = gout[((i + 1) * CW - 3) * S : (i + 1) * CW * S, :]


def block_pass(field, south, north, left, right, land, dw, gain, upw, bias, down, scale, sgain, sw, sbias, cot):
    R, CW, C = field.shape
    n = R * CW
    I = R // S
    sd = jax.ShapeDtypeStruct
    out_shape = (
        sd((S, CW // 8, C), bf16),
        sd((n, C), bf16),
        sd((n, C), bf16),
        sd((3, CW, C), bf16),
        sd((3, CW, C), bf16),
        sd((I * 3 * S, C), bf16),
        sd((I * 3 * S, C), bf16),
        sd((HALF, C), bf16),
        sd((HALF + 3 * CW, C), bf16),
    )
    V = pltpu.VMEM
    scratch = [
        V(((R + 6) * 40 + (R + 6) // I + 16, C), f32),
        V(((I + 6) * (CW + 6), S, C), bf16),
        V((49, S, C), bf16),
        V((n, C), f32),
        V((n, C), f32),
        V((n, C), f32),
        V((n, C), bf16),
        V((n, 512), bf16),
        V((n, 512), bf16),
        V((n, C), f32),
        V((n, C), f32),
        V((n // 4, 512), bf16),
        V((n // 4, C), bf16),
        V((49, 8, C), f32),
        V((C, 512), f32),
        V((C, 512), f32),
        V((n, C), bf16),
        V((n, C), bf16),
        V((256, 512), bf16),
        V((512, 128), bf16),
        V((2 * HALF, C), bf16),
    ]
    return pl.pallas_call(
        functools.partial(block_body, R, CW),
        out_shape=out_shape,
        in_specs=[VMEM] * 16,
        out_specs=[VMEM] * 9,
        scratch_shapes=scratch,
        compiler_params=PARAMS,
        name="block_pass",
    )(field, south, north, left, right, land, dw, gain, upw, bias, down, scale, sgain, sw, sbias, cot)


def conv_back_body(R, CW, g, dirin, dw, out, gx, gext, w49):
    I = R // S
    CE = CW + 6
    row = lax.broadcasted_iota(jnp.int32, (S, 128), 0)
    zero = jnp.zeros((3, S, 128), bf16)

    def cpy(i, _):
        gext[pl.ds((i + 3) * CE, 3)] = zero
        gext[pl.ds((i + 3) * CE + 3, CW)] = g[pl.ds(pl.multiple_of(i * CW * S, CW * S), CW * S), :].reshape(CW, S, 128)
        gext[pl.ds((i + 3) * CE + 3 + CW, 3)] = zero
        return 0

    lax.fori_loop(0, I, cpy, 0)
    for k in range(3):

        def shift(c, _, k=k):
            v = pltpu.roll(gext[(I + k) * CE + c].astype(f32), 1, 0)
            gext[k * CE + c] = jnp.where(row == 0, 0.0, v).astype(bf16)
            v = pltpu.roll(gext[(3 + k) * CE + c].astype(f32), S - 1, 0)
            gext[(I + 3 + k) * CE + c] = jnp.where(row == S - 1, 0.0, v).astype(bf16)
            return 0

        lax.fori_loop(0, CE, shift, 0, unroll=2)
    weights_table(dw, w49, True)

    def emit(i, c, v):
        at = pl.multiple_of((i * CW + c) * S, S)
        out[pl.ds(at, S), :] = (v + dirin[pl.ds(at, S), :].astype(f32)).astype(bf16)

    conv49(gext, w49, emit, I, CW)


def conv_back(g, dirin, dw, R, CW):
    C = g.shape[1]
    I = R // S
    return pl.pallas_call(
        functools.partial(conv_back_body, R, CW),
        out_shape=jax.ShapeDtypeStruct((R * CW, C), bf16),
        in_specs=[VMEM] * 3,
        out_specs=VMEM,
        scratch_shapes=[
            pltpu.VMEM((8, C), f32),
            pltpu.VMEM(((I + 6) * (CW + 6), S, C), bf16),
            pltpu.VMEM((49, S, C), bf16),
        ],
        compiler_params=SMALL,
        cost_estimate=pl.CostEstimate(flops=10**8, bytes_accessed=30 * 2**20, transcendentals=0),
        name="conv_back",
    )(g, dirin, dw)


def edges_body(R, CW, base, south, north, gl, gr, dw, out, acc, rows, cols, w49):
    I = R // S
    CE = CW + 6
    isn = on_top().astype(f32)
    nots = 1.0 - isn
    core = I * 3 * S
    row = lax.broadcasted_iota(jnp.int32, (S, 128), 0)
    for t in range(49):
        w49[t] = jnp.broadcast_to(dw[t : t + 1, :].astype(f32), (S, 128))
    for side in range(2):
        for k in range(3):
            at = core + side * 9 + k * 3
            mid = (north if side else south)[k]
            rows[pl.ds((side * 3 + k) * 40, CE), :] = jnp.concatenate(
                [gl[at : at + 3, :], mid, gr[at : at + 3, :]], axis=0
            ).astype(f32)

    def taps(k, a, flip):
        s = None
        for b in range(7):
            o = 6 - b if flip else b
            pr = rows[pl.ds(k * 40 + o, CW), :] * w49[7 * a + b, 0:1, :]
            s = pr if s is None else s + pr
        return s

    low = []
    for r in range(3):
        low.append(sum(taps(k, r + 6 - k, True) for k in range(r, 3)))
    high = []
    for t in range(3):
        v = sum(taps(3 + k, 2 - t - k, True) for k in range(3 - t)) * nots
        k1 = t + 1
        f = sum(taps(3 + rho, 5 + k1 - rho, False) for rho in range(k1 - 1, 3)) * isn
        high.append(v + f)
    for side in range(2):
        src = gr if side else gl

        def fill(i, _, src=src, side=side):
            for j in range(3):
                at = pl.multiple_of((i * 3 + j) * S, S)
                cols[side * (I + 6) * 3 + (i + 3) * 3 + j] = src[pl.ds(at, S), :].astype(f32)
            return 0

        lax.fori_loop(0, I, fill, 0)
        for k in range(3):
            for j in range(3):
                at = side * (I + 6) * 3
                v = pltpu.roll(cols[at + (I + k) * 3 + j], 1, 0)
                cols[at + k * 3 + j] = jnp.where(row == 0, 0.0, v)
                v = pltpu.roll(cols[at + (3 + k) * 3 + j], S - 1, 0)
                cols[at + (I + 3 + k) * 3 + j] = jnp.where(row == S - 1, 0.0, v)

    PITCH = CW * S

    def step(i, _):
        at = pl.multiple_of(i * PITCH, PITCH)
        acc[pl.ds(at, PITCH), :] = base[pl.ds(at, PITCH), :].astype(f32)
        for side in range(2):
            for t in range(3):
                s = None
                for j in range(3):
                    b = 2 - t - j if side else t + 6 - j
                    if b < 0 or b > 6:
                        continue
                    for a in range(7):
                        pr = cols[side * (I + 6) * 3 + (i + 6 - a) * 3 + j] * w49[7 * a + b]
                        s = pr if s is None else s + pr
                c = CW - 1 - t if side else t
                at = pl.multiple_of(i * PITCH + c * S, S)
                acc[pl.ds(at, S), :] += s
        return 0

    lax.fori_loop(0, I, step, 0)

    def unt(r, _):
        s = r // I
        i = r % I
        out[r] = acc[pl.ds(i * PITCH + s, CW, stride=S), :].astype(bf16)
        return 0

    lax.fori_loop(3, R - 3, unt, 0, unroll=2)
    for r in list(range(3)) + list(range(R - 3, R)):
        v = acc[pl.ds((r % I) * PITCH + r // I, CW, stride=S), :]
        v = v + (low[r] if r < 3 else high[R - 1 - r])
        out[r] = v.astype(bf16)


def edges(base, south, north, gl, gr, dw, R, CW):
    C = base.shape[1]
    I = R // S
    return pl.pallas_call(
        functools.partial(edges_body, R, CW),
        out_shape=jax.ShapeDtypeStruct((R, CW, C), bf16),
        in_specs=[VMEM] * 6,
        out_specs=VMEM,
        scratch_shapes=[
            pltpu.VMEM((R * CW, C), f32),
            pltpu.VMEM((240, C), f32),
            pltpu.VMEM((2 * (I + 6) * 3, S, C), f32),
            pltpu.VMEM((49, S, C), f32),
        ],
        compiler_params=SMALL,
        cost_estimate=pl.CostEstimate(flops=10**8, bytes_accessed=10 * 2**20, transcendentals=0),
        name="edges",
    )(base, south, north, gl, gr, dw)


def finish_body(factor, chunk, mine, other, o_depth, o_up, o_down, o_sec, full):
    core = lax.axis_index("lat") % 2
    place = (lax.axis_index("lat") // 2) * 2 + lax.axis_index("lon") % 2
    half = 4 * chunk
    for j in range(4):
        src = lax.bitwise_xor(place, j)
        at = pl.multiple_of(core * half + j * chunk, 16)
        full[pl.ds(at, chunk), :] = mine[src]
        at = pl.multiple_of((1 - core) * half + j * chunk, 16)
        full[pl.ds(at, chunk), :] = other[src]

    def block(n):
        return full[n * 128 : (n + 1) * 128, :].astype(f32) * factor

    for s in range(3):
        for q in range(4):
            o_sec[s, q * 128 : (q + 1) * 128, :] = block(s * 4 + q).T
    for q in range(4):
        o_down[q * 128 : (q + 1) * 128, :] = block(12 + q).T
        o_up[:, q * 128 : (q + 1) * 128] = block(16 + q)
    o_depth[...] = block(20)[:49, :]


def finish(mine, other, factor):
    chunk = mine.shape[1]
    sd = jax.ShapeDtypeStruct
    return pl.pallas_call(
        functools.partial(finish_body, factor, chunk),
        out_shape=(sd((49, 128), f32), sd((128, 512), f32), sd((512, 128), f32), sd((3, 512, 128), f32)),
        in_specs=[VMEM, VMEM],
        out_specs=[VMEM] * 4,
        scratch_shapes=[pltpu.VMEM((8 * chunk, 128), bf16)],
        compiler_params=SMALL,
        name="finish_sums",
    )(mine, other)


def add_bf(*vals):
    vals = [v.astype(f32) for v in vals]
    while len(vals) > 1:
        vals = [vals[i] + vals[i + 1] for i in range(0, len(vals), 2)]
    return vals[0].astype(bf16)


def flip_pairs(axis, bits):
    return [(i, i ^ bits) for i in range(lax.axis_size(axis))]


def both_pairs(lat_bits, lon_bits):
    nl = lax.axis_size("lon")
    return [
        (a * nl + b, (a ^ lat_bits) * nl + (b ^ lon_bits))
        for a in range(lax.axis_size("lat"))
        for b in range(nl)
    ]


def square_pairs(k):
    return both_pairs((k // 2) * 2, k % 2)


def square_sum(held, place):
    own = lax.dynamic_index_in_dim(held, place, 0, keepdims=False)
    came = []
    for k in (1, 2, 3):
        part = lax.dynamic_index_in_dim(held, lax.bitwise_xor(place, k), 0, keepdims=False)
        came.append(lax.ppermute(part, ("lat", "lon"), square_pairs(k)))
    return add_bf(own, *came)


def line_sum(total):
    left = lax.axis_size("lon") // 2
    bit = 2
    while left > 1:
        if left % 4 == 0:
            total = add_bf(total, *[lax.ppermute(total, "lon", flip_pairs("lon", bit * k)) for k in (1, 2, 3)])
            left //= 4
            bit *= 4
        else:
            total = add_bf(total, lax.ppermute(total, "lon", flip_pairs("lon", bit)))
            left //= 2
            bit *= 2
    return total


def on_top():
    return lax.axis_index("lat") == lax.axis_size("lat") - 1


def rim_body(R, CW, field, mirror, near, send, last, place, low, high, mir, sems):
    odd = lax.axis_index("lat") % 2
    copies = [
        pltpu.make_async_copy(mirror, mir, sems.at[0]),
        pltpu.make_async_copy(field.at[0:3], low, sems.at[1]),
        pltpu.make_async_copy(field.at[R - 3 : R], high, sems.at[2]),
    ]
    for c in copies:
        c.start()
    for c in copies:
        c.wait()
    for k in range(3):
        lo = low[k]
        hi = high[k]
        last[k] = hi
        send[k] = jnp.where(odd == 1, hi, lo)
        near[k] = jnp.where(odd == 1, lo, hi)
    place[0] = mir[0] // CW
    place[1] = mir[0] % CW


def rim(field, mirror):
    R, CW, C = field.shape
    sd = jax.ShapeDtypeStruct
    hbm = pl.BlockSpec(memory_space=pltpu.HBM)
    return pl.pallas_call(
        functools.partial(rim_body, R, CW),
        out_shape=(sd((3, CW, C), bf16),) * 3 + (sd((2,), jnp.int32),),
        in_specs=[hbm, hbm],
        out_specs=[VMEM] * 3 + [SMEM],
        scratch_shapes=[
            pltpu.VMEM((3, CW, C), bf16),
            pltpu.VMEM((3, CW, C), bf16),
            pltpu.SMEM(mirror.shape, jnp.int32),
            pltpu.SemaphoreType.DMA((3,)),
        ],
        compiler_params=WHOLE,
        name="rim",
    )(field, mirror)


def sides_body(R, CW, field, lc, rc, low, high, cols, sems):
    copies = [
        pltpu.make_async_copy(field.at[:, 0:16], low, sems.at[0]),
        pltpu.make_async_copy(field.at[:, CW - 16 : CW], high, sems.at[1]),
    ]
    for c in copies:
        c.start()
    for c in copies:
        c.wait()
    cols[0 : R * 8, :] = low[:, 0:8, :].astype(f32).reshape(R * 8, 128)
    cols[R * 8 :, :] = high[:, 8:16, :].astype(f32).reshape(R * 8, 128)
    for k in range(3):
        lc[k] = cols[pl.ds(k, R, stride=8), :].astype(bf16)
        rc[k] = cols[pl.ds(R * 8 + 5 + k, R, stride=8), :].astype(bf16)


def sides(field):
    R, CW, C = field.shape
    sd = jax.ShapeDtypeStruct
    return pl.pallas_call(
        functools.partial(sides_body, R, CW),
        out_shape=(sd((3, R, C), bf16),) * 2,
        in_specs=[pl.BlockSpec(memory_space=pltpu.HBM)],
        out_specs=[VMEM] * 2,
        scratch_shapes=[
            pltpu.VMEM((R, 16, C), bf16),
            pltpu.VMEM((R, 16, C), bf16),
            pltpu.VMEM((2 * R * 8, C), f32),
            pltpu.SemaphoreType.DMA((2,)),
        ],
        compiler_params=SMALL,
        name="sides",
    )(field)


def join_body(CW, width, flip, place, near, far, blk_b, lc, rc, south, north, lp, rp, cat, scr):
    odd = lax.axis_index("lat") % 2 == 1
    top = on_top()
    rem = place[1]
    at = lax.broadcasted_iota(jnp.int32, (CW, CW), 0)
    turn = (at + lax.broadcasted_iota(jnp.int32, (CW, CW), 1) == CW - 1).astype(f32).astype(bf16)
    for k in range(3):
        cat[0:CW, :] = blk_b[k].astype(f32)
        cat[CW : 2 * CW, :] = far[k].astype(f32)
        win = cat[pl.ds(rem + 1, CW), :].astype(bf16)
        scr[k * CW : (k + 1) * CW, :] = dot(turn, win)
    for k in range(3):
        m = 2 - k if flip else k
        beyond = scr[m * CW : (m + 1) * CW, :]
        close = (near[k] if flip else near[HALF + k * CW : HALF + (k + 1) * CW, :]).astype(f32)
        above = jnp.where(odd, far[k].astype(f32), close)
        below = jnp.where(odd, close, far[k].astype(f32))
        above = jnp.where(top, beyond, above)
        south[k] = below.astype(bf16)
        north[k] = above.astype(bf16)
        scr[(3 + k) * CW : (4 + k) * CW, :] = below
        scr[(6 + k) * CW : (7 + k) * CW, :] = above
    for pay, core, lo in ((lp, lc, 0), (rp, rc, CW - 3)):
        if flip:
            for j in range(3):
                for k in range(3):
                    cat[k : k + 1, :] = scr[(3 + k) * CW + lo + j : (3 + k) * CW + lo + j + 1, :]
                    cat[3 + width + k : 4 + width + k, :] = scr[(6 + k) * CW + lo + j : (6 + k) * CW + lo + j + 1, :]
                cat[3 : 3 + width, :] = core[j].astype(f32)
                pay[j] = cat[0 : width + 6, :].astype(bf16)
        else:
            pay[0:width, :] = core[...]
            for end in range(2):
                for k in range(3):
                    src = (3 + 3 * end + k) * CW + lo
                    cat[end * 9 + k * 3 : end * 9 + k * 3 + 3, :] = scr[src : src + 3, :]
            pay[width : width + 32, :] = cat[0:32, :].astype(bf16)


def join(place, near, far, blk_b, lc, rc, flip):
    CW, C = far.shape[1:]
    width = lc.shape[1] if flip else lc.shape[0]
    sd = jax.ShapeDtypeStruct
    pay = sd((3, width + 6, C) if flip else (width + 32, C), bf16)
    return pl.pallas_call(
        functools.partial(join_body, CW, width, flip),
        out_shape=(sd((3, CW, C), bf16),) * 2 + (pay, pay),
        in_specs=[SMEM] + [VMEM] * 5,
        out_specs=[VMEM] * 4,
        scratch_shapes=[pltpu.VMEM((max(2 * CW + 8, width + 8), C), f32), pltpu.VMEM((9 * CW, C), f32)],
        compiler_params=SMALL,
        name="join",
    )(place, near, far, blk_b, lc, rc)


def far_rows(send, last, quot, work=lambda: ()):
    nl = lax.axis_size("lon")
    nt = lax.axis_size("lat")
    top = (nt - 1) * nl
    axes = ("lat", "lon")
    swap = [(a * nl + e, (a + 1) * nl + e) for a in range(1, nt - 1, 2) for e in range(nl)]
    swap += [(j, i) for i, j in swap]

    def branch(q):
        def run():
            fa = [(top + e, top + (q - e) % nl) for e in range(nl)]
            fb = [(top + e, top + (q - 1 - e) % nl) for e in range(nl)]
            return lax.ppermute(send, axes, swap + fa), lax.ppermute(last, axes, fb), work()

        return run

    return lax.switch(quot, [branch(q) for q in range(nl)])


def shift_pairs(axis, by):
    n = lax.axis_size(axis)
    return [(i, (i + by) % n) for i in range(n)]


def on_device(
    field, land, mirror, depth_weight, norm_gain, up_weight, up_bias, down_proj, layer_scale,
    section_gain, section_weight, section_bias, cotangent,
):
    R, CW, C = field.shape
    total = R * CW * lax.axis_size("lat") * lax.axis_size("lon")
    factor = 1.0 / math.sqrt(total / 64.0)
    near, send, last, shift = rim(field, mirror)
    near = lax.ppermute(near, "lat", flip_pairs("lat", 1))
    far, blk_b, (lc, rc) = far_rows(send, last, shift[0], lambda: sides(field))
    south_f, north_f, lpay, rpay = join(shift, near, far, blk_b, lc, rc, True)
    right_f = lax.ppermute(lpay, "lon", shift_pairs("lon", -1))
    left_f = lax.ppermute(rpay, "lon", shift_pairs("lon", 1))
    level, g, direct, send, last, lcol, rcol, keep, away = block_pass(
        field, south_f, north_f, left_f, right_f, land.T, depth_weight, norm_gain, up_weight, up_bias, down_proj,
        layer_scale, section_gain, section_weight, section_bias, cotangent,
    )

    place = (lax.axis_index("lat") // 2) * 2 + lax.axis_index("lon") % 2
    got = lax.ppermute(away, "lat", flip_pairs("lat", 1))
    held = add_bf(keep, got[:HALF]).reshape(4, HALF // 4, C)
    send, held = lax.optimization_barrier((send, held))
    chunk = square_sum(held, place)
    far, blk_b, base = far_rows(
        send, last, shift[0], lambda: conv_back(g, direct, depth_weight, R, CW)
    )
    chunk, far = lax.optimization_barrier((chunk, far))
    south_g, north_g, lpay, rpay = join(shift, got, far, blk_b, lcol, rcol, False)
    chunk, lpay = lax.optimization_barrier((chunk, lpay))
    gr = lax.ppermute(lpay, "lon", shift_pairs("lon", -1))
    gl = lax.ppermute(rpay, "lon", shift_pairs("lon", 1))
    chunk = line_sum(chunk)
    grad_field = edges(base, south_g, north_g, gl, gr, depth_weight, R, CW)
    axes = ("lat", "lon")
    back = [lax.ppermute(chunk, axes, square_pairs(k)) for k in (1, 2, 3)]
    back[0], grad_field = lax.optimization_barrier((back[0], grad_field))
    mine = jnp.stack([chunk] + back)
    other = lax.ppermute(mine, "lat", flip_pairs("lat", 1))
    g_depth, g_up, g_down, g_sec = finish(mine, other, factor)
    return level, grad_field, g_depth, g_up, g_down, g_sec


def solution(mesh):
    cells = P("lat", "lon", None)
    in_specs = (cells, P("lat", "lon")) + (P(),) * 10 + (cells,)
    out_specs = (cells, cells, P(), P(), P(), P())
    return jax.shard_map(on_device, mesh=mesh, in_specs=in_specs, out_specs=out_specs, check_vma=False)
```

```python
import functools
import math

import jax
import jax.numpy as jnp
from jax import lax
from jax.experimental import pallas as pl
from jax.experimental.pallas import tpu as pltpu
from jax.sharding import PartitionSpec as P

SECTIONS = 3
EPS = 1e-6
f32, bf16 = jnp.float32, jnp.bfloat16
S = 16
LOG2E = 1.4426950408889634
LOG2_DENS = -0.3257480647361593
HALF = 1344
VMEM = pl.BlockSpec(memory_space=pltpu.VMEM)
SMEM = pl.BlockSpec(memory_space=pltpu.SMEM)
PARAMS = pltpu.CompilerParams(vmem_limit_bytes=44 * 2**20)
WHOLE = pltpu.CompilerParams(vmem_limit_bytes=63 * 2**20 + 2**19)
SMALL = pltpu.CompilerParams(vmem_limit_bytes=24 * 2**20)


def dot(a, b):
    return jnp.dot(a, b, preferred_element_type=f32)


def dot_t(a, b):
    return lax.dot_general(a, b, (((0,), (0,)), ((), ())), preferred_element_type=f32)


def dot_r(a, b):
    return lax.dot_general(a, b, (((1,), (1,)), ((), ())), preferred_element_type=f32)


def ones_mean(n):
    return jnp.full((n, 128), 1.0 / 128, bf16)


def pair_mean():
    r = lax.broadcasted_iota(jnp.int32, (256, 256), 0) // 128
    c = lax.broadcasted_iota(jnp.int32, (256, 256), 1) // 128
    return jnp.where(r == c, 1.0 / 128, 0.0).astype(bf16)


def split2(x):
    hi = x.astype(bf16)
    lo = (x - hi.astype(f32)).astype(bf16)
    return jnp.concatenate([hi, lo], axis=1)


def norm_bwd(u, hat, rstd, pm):
    m = dot(jnp.concatenate([u.astype(bf16), (u * hat).astype(bf16)], axis=1), pm)
    return rstd * (u - m[:, :128] - hat * m[:, 128:])


def gelu2(h):
    g = h * 0.7071067811865476
    c = 1.0 + lax.erf(g)
    e = jnp.exp2(g * g * (-LOG2E) + LOG2_DENS)
    return h * c, c + h * e


def weights_table(dw, w49, flip):
    for t in range(49):
        w49[48 - t if flip else t] = jnp.broadcast_to(dw[t : t + 1, :].astype(f32), (S, 128)).astype(w49.dtype)


def conv49(el, w49, emit, I, CW):
    CE = CW + 6
    CG = 4

    def step(n, _):
        i = n // (CW // CG)
        c0 = (n % (CW // CG)) * CG
        acc = [None] * CG
        for a in range(7):
            row = [el[(i + a) * CE + c0 + m].astype(f32) for m in range(CG + 6)]
            for b in range(7):
                w = w49[a * 7 + b].astype(f32)
                for k in range(CG):
                    pr = row[k + b] * w
                    acc[k] = pr if acc[k] is None else acc[k] + pr
        for k in range(CG):
            emit(i, c0 + k, acc[k])
        return 0

    lax.fori_loop(0, I * (CW // CG), step, 0)


def block_body(
    R, CW,
    field, south, north, left, right, land, dw, gain, upw, bias, down, scale, sgain, sw, sbias, cot,
    bott, gout, dirout, send, last, lcol, rcol, keep, away,
    x2d, el, w49, dep, hat, rst, nrm, act, slp, shat, srst, p1, back, tacc, downs, ups, mgs, landb, up, dn, sums,
):
    I = R // S
    CE = CW + 6
    XW = 40
    n0 = R * CW

    def asm(r, _):
        x2d[pl.ds((r + 3) * XW + (r + 3) // I + 3, CW), :] = field[r].astype(f32)
        return 0

    lax.fori_loop(0, R, asm, 0, unroll=4)
    PB = I * XW + 1
    for k in range(3):
        x2d[pl.ds(k * XW + 3, CW), :] = south[k].astype(f32)
        x2d[pl.ds((R + 3 + k) * XW + (R + 3 + k) // I + 3, CW), :] = north[k].astype(f32)
        for m in range((R + 6 + I - 1) // I):
            rows = min(I, R + 6 - m * I)
            x2d[pl.ds(m * PB + k, rows, stride=XW), :] = left[k, m * I : m * I + rows, :].astype(f32)
            x2d[pl.ds(m * PB + CW + 3 + k, rows, stride=XW), :] = right[k, m * I : m * I + rows, :].astype(f32)

    def tr(i, _):
        for c in range(CE):
            el[i * CE + c] = x2d[pl.ds(i * XW + i // I + c, S, stride=PB), :].astype(bf16)
        return 0

    lax.fori_loop(0, I + 6, tr, 0)
    weights_table(dw, w49, False)
    p_at = lax.broadcasted_iota(jnp.int32, (R, R), 0)
    p_row = lax.broadcasted_iota(jnp.int32, (R, R), 1)
    order = (p_row == (p_at % S) * I + p_at // S).astype(f32).astype(bf16)
    land_p = dot_r(order, land[...].astype(f32).astype(bf16)).astype(bf16)
    spread = (
        lax.broadcasted_iota(jnp.int32, (CW, CW * 128), 1) // 128
        == lax.broadcasted_iota(jnp.int32, (CW, CW * 128), 0)
    )
    land_w = dot(land_p, spread.astype(f32).astype(bf16)).astype(bf16)
    for i in range(I):
        for c in range(CW):
            at = (i * CW + c) * S
            landb[at : at + S, :] = land_w[i * S : (i + 1) * S, c * 128 : (c + 1) * 128]
    dn[...] = (down[...].astype(f32) * 0.5).astype(bf16)
    up[0:128, :] = upw[...]
    up[128:256, :] = jnp.where(
        lax.broadcasted_iota(jnp.int32, (128, 512), 0) == 0, bias[...].astype(f32).reshape(1, 512), 0.0
    ).astype(bf16)

    def emit(i, c, v):
        dep[pl.ds((i * CW + c) * S, S), :] = v

    conv49(el, w49, emit, I, CW)

    jj, j1, pm = ones_mean(256), ones_mean(128), pair_mean()
    g_n = gain[...].astype(f32).reshape(1, 128)
    sc = scale[...].astype(f32).reshape(1, 128)
    sg0 = sgain[0:1, :].astype(f32)
    T1 = n0

    def nfwd(n, _):
        base = pl.multiple_of(n * T1, T1)
        x = dep[pl.ds(base, T1), :]
        cen = x - dot(split2(x), jj)
        rs = lax.rsqrt(dot((cen * cen).astype(bf16), j1) + EPS)
        ht = cen * rs
        hat[pl.ds(base, T1), :] = ht
        rst[pl.ds(base, T1), :] = rs
        nrm[pl.ds(base, T1), :] = (ht * g_n).astype(bf16)
        return 0

    lax.fori_loop(0, n0 // T1, nfwd, 0)

    T2 = n0 // 2
    onec = (lax.broadcasted_iota(jnp.int32, (T2, 128), 1) == 0).astype(f32).astype(bf16)

    def upf(n, _):
        base = pl.multiple_of(n * T2, T2)
        lhs = jnp.concatenate([nrm[pl.ds(base, T2), :], onec], axis=1)
        for q in range(2):
            hid = dot(lhs, up[:, q * 256 : (q + 1) * 256])
            ac, sl = gelu2(hid)
            act[pl.ds(base, T2), q * 256 : (q + 1) * 256] = ac.astype(bf16)
            slp[pl.ds(base, T2), q * 256 : (q + 1) * 256] = sl.astype(bf16)
        return 0

    lax.fori_loop(0, n0 // T2, upf, 0)

    TP = 2 * CW * S

    def sect_norm(lv, s):
        cen = lv.astype(f32) - dot(lv, j1)
        rs1 = lax.rsqrt(dot((cen * cen).astype(bf16), j1) + EPS)
        h1 = cen * rs1
        return h1, rs1, (h1 * sgain[s : s + 1, :].astype(f32)).astype(bf16)

    def dnf(i2, _):
        base = pl.multiple_of(i2 * TP, TP)
        mixed = dot(act[pl.ds(base, TP), :], dn[...])
        xs = jnp.concatenate(
            [el[pl.ds((i2 * 2 + a + 3) * CE + 3, CW)].reshape(CW * S, 128) for a in range(2)], axis=0
        ).astype(f32)
        lv = (landb[pl.ds(base, TP), :].astype(f32) * (xs + sc * mixed)).astype(bf16)
        h1, rs1, sn = sect_norm(lv, 0)
        shat[pl.ds(base, TP), :] = h1
        srst[pl.ds(base, TP), :] = rs1
        sn = sn.reshape(2, CW // 2, 2, S, 128)
        pb = pl.multiple_of(i2 * (TP // 4), TP // 4)
        for a in range(2):
            for b in range(2):
                k = 2 * a + b
                p1[pl.ds(pb, TP // 4), k * 128 : (k + 1) * 128] = sn[a, :, b].reshape(TP // 4, 128)
        return 0

    lax.fori_loop(0, I // 2, dnf, 0, unroll=2)

    def to_patches(sn, ii, cc):
        v = sn.reshape(ii // 2, 2, cc // 2, 2, S, 128)
        return jnp.concatenate(
            [v[:, a, :, b].reshape(ii * cc * S // 4, 128) for a in range(2) for b in range(2)], axis=1
        )

    def from_patches(sp, ii, cc):
        ps = [sp[:, k * 128 : (k + 1) * 128].reshape(ii // 2, cc // 2, S, 128) for k in range(4)]
        rows = [jnp.stack([ps[2 * a], ps[2 * a + 1]], axis=2).reshape(ii // 2, cc, S, 128) for a in range(2)]
        return jnp.stack(rows, axis=1).reshape(ii * cc * S, 128)

    def put(at, value, blocks):
        for q in range(blocks):
            sums[at + q * 128 : at + (q + 1) * 128, :] = value[:, q * 128 : (q + 1) * 128].astype(bf16)

    l1 = (dot(p1[...], sw[0]) + sbias[0:1, :].astype(f32)).astype(bf16)
    h1, r1, sn1 = sect_norm(l1, 1)
    P2 = to_patches(sn1, I // 2, CW // 2)
    l2 = (dot(P2, sw[1]) + sbias[1:2, :].astype(f32)).astype(bf16)
    h2, r2, sn2 = sect_norm(l2, 2)
    P3 = to_patches(sn2, I // 4, CW // 4)
    l3 = (dot(P3, sw[2]) + sbias[2:3, :].astype(f32)).astype(bf16)
    Q = CW // 8
    for c in range(Q):
        x2d[pl.ds(c, S, stride=Q), :] = l3[c * S : (c + 1) * S, :].astype(f32)
    for r in range(S):
        bott[r] = x2d[r * Q : (r + 1) * Q, :].astype(bf16)
        x2d[128 + r * Q : 128 + (r + 1) * Q, :] = cot[r].astype(f32)
    b3 = jnp.concatenate([x2d[pl.ds(128 + c, S, stride=Q), :] for c in range(Q)], axis=0).astype(bf16)
    put(1024, dot_t(b3, P3), 4)
    u2 = from_patches(dot_r(b3, sw[2]), I // 4, CW // 4) * sgain[2:3, :].astype(f32)
    b2 = norm_bwd(u2, h2, r2, pm).astype(bf16)
    put(512, dot_t(b2, P2), 4)
    u1 = from_patches(dot_r(b2, sw[1]), I // 2, CW // 2) * sgain[1:2, :].astype(f32)
    b1 = norm_bwd(u1, h1, r1, pm).astype(bf16)
    put(0, dot_t(b1, p1[...]), 4)
    back[...] = b1

    QP = TP // 4

    def bk1(i2, _):
        pb = pl.multiple_of(i2 * QP, QP)
        bk = back[pl.ds(pb, QP), :]
        base = pl.multiple_of(i2 * TP, TP)
        us = []
        for a in range(2):
            sp = dot_r(bk, sw[0, a * 256 : (a + 1) * 256, :])
            us.append(
                jnp.stack(
                    [sp[:, :128].reshape(CW // 2, S, 128), sp[:, 128:].reshape(CW // 2, S, 128)], axis=1
                ).reshape(TP // 2, 128)
            )
        u = jnp.concatenate(us, axis=0) * sg0
        b0 = norm_bwd(u, shat[pl.ds(base, TP), :], srst[pl.ds(base, TP), :], pm).astype(bf16).astype(f32)
        dr = landb[pl.ds(base, TP), :].astype(f32) * b0
        dirout[pl.ds(base, TP), :] = dr.astype(bf16)
        mgs[pl.ds(base, TP), :] = (dr * sc).astype(bf16)
        return 0

    lax.fori_loop(0, I // 2, bk1, 0, unroll=4)

    def bk2(n, _):
        base = pl.multiple_of(n * T2, T2)
        mg = mgs[pl.ds(base, T2), :]
        for q in range(2):
            ag = dot_r(mg, dn[q * 256 : (q + 1) * 256, :])
            sl = slp[pl.ds(base, T2), q * 256 : (q + 1) * 256].astype(f32)
            slp[pl.ds(base, T2), q * 256 : (q + 1) * 256] = (ag * sl).astype(bf16)
        return 0

    lax.fori_loop(0, n0 // T2, bk2, 0)

    def bk3(n, _):
        base = pl.multiple_of(n * T1, T1)
        ng = dot_r(slp[pl.ds(base, T1), :], up[0:128, :])
        dg = norm_bwd(ng * g_n, hat[pl.ds(base, T1), :], rst[pl.ds(base, T1), :], pm)
        gout[pl.ds(base, T1), :] = dg.astype(bf16)
        return 0

    lax.fori_loop(0, n0 // T1, bk3, 0)
    downs[...] = dot_t(mgs[...], act[...]) * 0.5
    ups[...] = dot_t(nrm[...], slp[...])
    put(1536, downs[...], 4)
    put(2048, ups[...], 4)

    tacc[...] = jnp.zeros_like(tacc)

    def tap(n, _):
        i = n // (CW // 8)
        c0 = (n % (CW // 8)) * 8
        g = [gout[pl.ds((i * CW + c0 + k) * S, S), :].astype(f32) for k in range(8)]
        for a in range(7):
            row = [el[(i + a) * CE + c0 + m].astype(f32) for m in range(14)]
            for b in range(7):
                s = None
                for k in range(8):
                    pr = row[k + b] * g[k]
                    s = pr if s is None else s + pr
                tacc[a * 7 + b] += s[:8] + s[8:]
        return 0

    lax.fori_loop(0, I * (CW // 8), tap, 0)
    ts = [jnp.sum(tacc[t], axis=0, keepdims=True) for t in range(49)]
    ts = jnp.concatenate(ts + [jnp.zeros((15, 128), f32)], axis=0)
    sums[2560:2624, :] = ts.astype(bf16)
    sums[2624:2688, :] = jnp.zeros((64, 128), bf16)

    odd = lax.axis_index("lat") % 2
    keep[...] = sums[pl.ds(pl.multiple_of(odd * HALF, 64), HALF), :]
    away[0:HALF, :] = sums[pl.ds(pl.multiple_of((1 - odd) * HALF, 64), HALF), :]
    x2d[0:n0, :] = gout[...].astype(f32)
    for k in range(3):
        lo = x2d[pl.ds(k * CW * S, CW, stride=S), :].astype(bf16)
        hi = x2d[pl.ds((I - 3 + k) * CW * S + S - 1, CW, stride=S), :].astype(bf16)
        last[k] = hi
        send[k] = jnp.where(odd == 1, hi, lo)
        away[HALF + k * CW : HALF + (k + 1) * CW, :] = jnp.where(odd == 1, lo, hi)
    for i in range(I):
        lcol[i * 3 * S : (i + 1) * 3 * S, :] = gout[i * CW * S : (i * CW + 3) * S, :]
        rcol[i * 3 * S : (i + 1) * 3 * S, :] = gout[((i + 1) * CW - 3) * S : (i + 1) * CW * S, :]


def block_pass(field, south, north, left, right, land, dw, gain, upw, bias, down, scale, sgain, sw, sbias, cot):
    R, CW, C = field.shape
    n = R * CW
    I = R // S
    sd = jax.ShapeDtypeStruct
    out_shape = (
        sd((S, CW // 8, C), bf16),
        sd((n, C), bf16),
        sd((n, C), bf16),
        sd((3, CW, C), bf16),
        sd((3, CW, C), bf16),
        sd((I * 3 * S, C), bf16),
        sd((I * 3 * S, C), bf16),
        sd((HALF, C), bf16),
        sd((HALF + 3 * CW, C), bf16),
    )
    V = pltpu.VMEM
    scratch = [
        V(((R + 6) * 40 + (R + 6) // I + 16, C), f32),
        V(((I + 6) * (CW + 6), S, C), bf16),
        V((49, S, C), bf16),
        V((n, C), f32),
        V((n, C), f32),
        V((n, C), f32),
        V((n, C), bf16),
        V((n, 512), bf16),
        V((n, 512), bf16),
        V((n, C), f32),
        V((n, C), f32),
        V((n // 4, 512), bf16),
        V((n // 4, C), bf16),
        V((49, 8, C), f32),
        V((C, 512), f32),
        V((C, 512), f32),
        V((n, C), bf16),
        V((n, C), bf16),
        V((256, 512), bf16),
        V((512, 128), bf16),
        V((2 * HALF, C), bf16),
    ]
    return pl.pallas_call(
        functools.partial(block_body, R, CW),
        out_shape=out_shape,
        in_specs=[VMEM] * 16,
        out_specs=[VMEM] * 9,
        scratch_shapes=scratch,
        compiler_params=PARAMS,
        name="block_pass",
    )(field, south, north, left, right, land, dw, gain, upw, bias, down, scale, sgain, sw, sbias, cot)


def conv_back_body(R, CW, g, dirin, dw, out, gx, gext, w49):
    I = R // S
    CE = CW + 6
    row = lax.broadcasted_iota(jnp.int32, (S, 128), 0)
    zero = jnp.zeros((3, S, 128), bf16)

    def cpy(i, _):
        gext[pl.ds((i + 3) * CE, 3)] = zero
        gext[pl.ds((i + 3) * CE + 3, CW)] = g[pl.ds(pl.multiple_of(i * CW * S, CW * S), CW * S), :].reshape(CW, S, 128)
        gext[pl.ds((i + 3) * CE + 3 + CW, 3)] = zero
        return 0

    lax.fori_loop(0, I, cpy, 0)
    for k in range(3):

        def shift(c, _, k=k):
            v = pltpu.roll(gext[(I + k) * CE + c].astype(f32), 1, 0)
            gext[k * CE + c] = jnp.where(row == 0, 0.0, v).astype(bf16)
            v = pltpu.roll(gext[(3 + k) * CE + c].astype(f32), S - 1, 0)
            gext[(I + 3 + k) * CE + c] = jnp.where(row == S - 1, 0.0, v).astype(bf16)
            return 0

        lax.fori_loop(0, CE, shift, 0, unroll=2)
    weights_table(dw, w49, True)

    def emit(i, c, v):
        at = pl.multiple_of((i * CW + c) * S, S)
        out[pl.ds(at, S), :] = (v + dirin[pl.ds(at, S), :].astype(f32)).astype(bf16)

    conv49(gext, w49, emit, I, CW)


def conv_back(g, dirin, dw, R, CW):
    C = g.shape[1]
    I = R // S
    return pl.pallas_call(
        functools.partial(conv_back_body, R, CW),
        out_shape=jax.ShapeDtypeStruct((R * CW, C), bf16),
        in_specs=[VMEM] * 3,
        out_specs=VMEM,
        scratch_shapes=[
            pltpu.VMEM((8, C), f32),
            pltpu.VMEM(((I + 6) * (CW + 6), S, C), bf16),
            pltpu.VMEM((49, S, C), bf16),
        ],
        compiler_params=SMALL,
        cost_estimate=pl.CostEstimate(flops=10**8, bytes_accessed=30 * 2**20, transcendentals=0),
        name="conv_back",
    )(g, dirin, dw)


def edges_body(R, CW, base, south, north, gl, gr, dw, out, acc, rows, cols, w49):
    I = R // S
    CE = CW + 6
    isn = on_top().astype(f32)
    nots = 1.0 - isn
    core = I * 3 * S
    row = lax.broadcasted_iota(jnp.int32, (S, 128), 0)
    for t in range(49):
        w49[t] = jnp.broadcast_to(dw[t : t + 1, :].astype(f32), (S, 128))
    for side in range(2):
        for k in range(3):
            at = core + side * 9 + k * 3
            mid = (north if side else south)[k]
            rows[pl.ds((side * 3 + k) * 40, CE), :] = jnp.concatenate(
                [gl[at : at + 3, :], mid, gr[at : at + 3, :]], axis=0
            ).astype(f32)

    def taps(k, a, flip):
        s = None
        for b in range(7):
            o = 6 - b if flip else b
            pr = rows[pl.ds(k * 40 + o, CW), :] * w49[7 * a + b, 0:1, :]
            s = pr if s is None else s + pr
        return s

    low = []
    for r in range(3):
        low.append(sum(taps(k, r + 6 - k, True) for k in range(r, 3)))
    high = []
    for t in range(3):
        v = sum(taps(3 + k, 2 - t - k, True) for k in range(3 - t)) * nots
        k1 = t + 1
        f = sum(taps(3 + rho, 5 + k1 - rho, False) for rho in range(k1 - 1, 3)) * isn
        high.append(v + f)
    for side in range(2):
        src = gr if side else gl

        def fill(i, _, src=src, side=side):
            for j in range(3):
                at = pl.multiple_of((i * 3 + j) * S, S)
                cols[side * (I + 6) * 3 + (i + 3) * 3 + j] = src[pl.ds(at, S), :].astype(f32)
            return 0

        lax.fori_loop(0, I, fill, 0)
        for k in range(3):
            for j in range(3):
                at = side * (I + 6) * 3
                v = pltpu.roll(cols[at + (I + k) * 3 + j], 1, 0)
                cols[at + k * 3 + j] = jnp.where(row == 0, 0.0, v)
                v = pltpu.roll(cols[at + (3 + k) * 3 + j], S - 1, 0)
                cols[at + (I + 3 + k) * 3 + j] = jnp.where(row == S - 1, 0.0, v)

    PITCH = CW * S

    def step(i, _):
        at = pl.multiple_of(i * PITCH, PITCH)
        acc[pl.ds(at, PITCH), :] = base[pl.ds(at, PITCH), :].astype(f32)
        for side in range(2):
            for t in range(3):
                s = None
                for j in range(3):
                    b = 2 - t - j if side else t + 6 - j
                    if b < 0 or b > 6:
                        continue
                    for a in range(7):
                        pr = cols[side * (I + 6) * 3 + (i + 6 - a) * 3 + j] * w49[7 * a + b]
                        s = pr if s is None else s + pr
                c = CW - 1 - t if side else t
                at = pl.multiple_of(i * PITCH + c * S, S)
                acc[pl.ds(at, S), :] += s
        return 0

    lax.fori_loop(0, I, step, 0)

    def unt(r, _):
        s = r // I
        i = r % I
        out[r] = acc[pl.ds(i * PITCH + s, CW, stride=S), :].astype(bf16)
        return 0

    lax.fori_loop(3, R - 3, unt, 0, unroll=2)
    for r in list(range(3)) + list(range(R - 3, R)):
        v = acc[pl.ds((r % I) * PITCH + r // I, CW, stride=S), :]
        v = v + (low[r] if r < 3 else high[R - 1 - r])
        out[r] = v.astype(bf16)


def edges(base, south, north, gl, gr, dw, R, CW):
    C = base.shape[1]
    I = R // S
    return pl.pallas_call(
        functools.partial(edges_body, R, CW),
        out_shape=jax.ShapeDtypeStruct((R, CW, C), bf16),
        in_specs=[VMEM] * 6,
        out_specs=VMEM,
        scratch_shapes=[
            pltpu.VMEM((R * CW, C), f32),
            pltpu.VMEM((240, C), f32),
            pltpu.VMEM((2 * (I + 6) * 3, S, C), f32),
            pltpu.VMEM((49, S, C), f32),
        ],
        compiler_params=SMALL,
        cost_estimate=pl.CostEstimate(flops=10**8, bytes_accessed=10 * 2**20, transcendentals=0),
        name="edges",
    )(base, south, north, gl, gr, dw)


def finish_body(factor, chunk, mine, other, o_depth, o_up, o_down, o_sec, full):
    core = lax.axis_index("lat") % 2
    place = (lax.axis_index("lat") // 2) * 2 + lax.axis_index("lon") % 2
    half = 4 * chunk
    for j in range(4):
        src = lax.bitwise_xor(place, j)
        at = pl.multiple_of(core * half + j * chunk, 16)
        full[pl.ds(at, chunk), :] = mine[src]
        at = pl.multiple_of((1 - core) * half + j * chunk, 16)
        full[pl.ds(at, chunk), :] = other[src]

    def block(n):
        return full[n * 128 : (n + 1) * 128, :].astype(f32) * factor

    for s in range(3):
        for q in range(4):
            o_sec[s, q * 128 : (q + 1) * 128, :] = block(s * 4 + q).T
    for q in range(4):
        o_down[q * 128 : (q + 1) * 128, :] = block(12 + q).T
        o_up[:, q * 128 : (q + 1) * 128] = block(16 + q)
    o_depth[...] = block(20)[:49, :]


def finish(mine, other, factor):
    chunk = mine.shape[1]
    sd = jax.ShapeDtypeStruct
    return pl.pallas_call(
        functools.partial(finish_body, factor, chunk),
        out_shape=(sd((49, 128), f32), sd((128, 512), f32), sd((512, 128), f32), sd((3, 512, 128), f32)),
        in_specs=[VMEM, VMEM],
        out_specs=[VMEM] * 4,
        scratch_shapes=[pltpu.VMEM((8 * chunk, 128), bf16)],
        compiler_params=SMALL,
        name="finish_sums",
    )(mine, other)


def add_bf(*vals):
    vals = [v.astype(f32) for v in vals]
    while len(vals) > 1:
        vals = [vals[i] + vals[i + 1] for i in range(0, len(vals), 2)]
    return vals[0].astype(bf16)


def flip_pairs(axis, bits):
    return [(i, i ^ bits) for i in range(lax.axis_size(axis))]


def both_pairs(lat_bits, lon_bits):
    nl = lax.axis_size("lon")
    return [
        (a * nl + b, (a ^ lat_bits) * nl + (b ^ lon_bits))
        for a in range(lax.axis_size("lat"))
        for b in range(nl)
    ]


def square_pairs(k):
    return both_pairs((k // 2) * 2, k % 2)


def square_sum(held, place):
    own = lax.dynamic_index_in_dim(held, place, 0, keepdims=False)
    came = []
    for k in (1, 2, 3):
        part = lax.dynamic_index_in_dim(held, lax.bitwise_xor(place, k), 0, keepdims=False)
        came.append(lax.ppermute(part, ("lat", "lon"), square_pairs(k)))
    return add_bf(own, *came)


def line_sum(total):
    left = lax.axis_size("lon") // 2
    bit = 2
    while left > 1:
        if left % 4 == 0:
            total = add_bf(total, *[lax.ppermute(total, "lon", flip_pairs("lon", bit * k)) for k in (1, 2, 3)])
            left //= 4
            bit *= 4
        else:
            total = add_bf(total, lax.ppermute(total, "lon", flip_pairs("lon", bit)))
            left //= 2
            bit *= 2
    return total


def on_top():
    return lax.axis_index("lat") == lax.axis_size("lat") - 1


def rim_body(R, CW, field, mirror, near, send, last, place, low, high, mir, sems):
    odd = lax.axis_index("lat") % 2
    copies = [
        pltpu.make_async_copy(mirror, mir, sems.at[0]),
        pltpu.make_async_copy(field.at[0:3], low, sems.at[1]),
        pltpu.make_async_copy(field.at[R - 3 : R], high, sems.at[2]),
    ]
    for c in copies:
        c.start()
    for c in copies:
        c.wait()
    for k in range(3):
        lo = low[k]
        hi = high[k]
        last[k] = hi
        send[k] = jnp.where(odd == 1, hi, lo)
        near[k] = jnp.where(odd == 1, lo, hi)
    place[0] = mir[0] // CW
    place[1] = mir[0] % CW


def rim(field, mirror):
    R, CW, C = field.shape
    sd = jax.ShapeDtypeStruct
    hbm = pl.BlockSpec(memory_space=pltpu.HBM)
    return pl.pallas_call(
        functools.partial(rim_body, R, CW),
        out_shape=(sd((3, CW, C), bf16),) * 3 + (sd((2,), jnp.int32),),
        in_specs=[hbm, hbm],
        out_specs=[VMEM] * 3 + [SMEM],
        scratch_shapes=[
            pltpu.VMEM((3, CW, C), bf16),
            pltpu.VMEM((3, CW, C), bf16),
            pltpu.SMEM(mirror.shape, jnp.int32),
            pltpu.SemaphoreType.DMA((3,)),
        ],
        compiler_params=WHOLE,
        name="rim",
    )(field, mirror)


def sides_body(R, CW, field, lc, rc, low, high, cols, sems):
    copies = [
        pltpu.make_async_copy(field.at[:, 0:16], low, sems.at[0]),
        pltpu.make_async_copy(field.at[:, CW - 16 : CW], high, sems.at[1]),
    ]
    for c in copies:
        c.start()
    for c in copies:
        c.wait()
    cols[0 : R * 8, :] = low[:, 0:8, :].astype(f32).reshape(R * 8, 128)
    cols[R * 8 :, :] = high[:, 8:16, :].astype(f32).reshape(R * 8, 128)
    for k in range(3):
        lc[k] = cols[pl.ds(k, R, stride=8), :].astype(bf16)
        rc[k] = cols[pl.ds(R * 8 + 5 + k, R, stride=8), :].astype(bf16)


def sides(field):
    R, CW, C = field.shape
    sd = jax.ShapeDtypeStruct
    return pl.pallas_call(
        functools.partial(sides_body, R, CW),
        out_shape=(sd((3, R, C), bf16),) * 2,
        in_specs=[pl.BlockSpec(memory_space=pltpu.HBM)],
        out_specs=[VMEM] * 2,
        scratch_shapes=[
            pltpu.VMEM((R, 16, C), bf16),
            pltpu.VMEM((R, 16, C), bf16),
            pltpu.VMEM((2 * R * 8, C), f32),
            pltpu.SemaphoreType.DMA((2,)),
        ],
        compiler_params=SMALL,
        name="sides",
    )(field)


def join_body(CW, width, flip, place, near, far, blk_b, lc, rc, south, north, lp, rp, cat, scr):
    odd = lax.axis_index("lat") % 2 == 1
    top = on_top()
    rem = place[1]
    at = lax.broadcasted_iota(jnp.int32, (CW, CW), 0)
    turn = (at + lax.broadcasted_iota(jnp.int32, (CW, CW), 1) == CW - 1).astype(f32).astype(bf16)
    for k in range(3):
        cat[0:CW, :] = blk_b[k].astype(f32)
        cat[CW : 2 * CW, :] = far[k].astype(f32)
        win = cat[pl.ds(rem + 1, CW), :].astype(bf16)
        scr[k * CW : (k + 1) * CW, :] = dot(turn, win)
    for k in range(3):
        m = 2 - k if flip else k
        beyond = scr[m * CW : (m + 1) * CW, :]
        close = (near[k] if flip else near[HALF + k * CW : HALF + (k + 1) * CW, :]).astype(f32)
        above = jnp.where(odd, far[k].astype(f32), close)
        below = jnp.where(odd, close, far[k].astype(f32))
        above = jnp.where(top, beyond, above)
        south[k] = below.astype(bf16)
        north[k] = above.astype(bf16)
        scr[(3 + k) * CW : (4 + k) * CW, :] = below
        scr[(6 + k) * CW : (7 + k) * CW, :] = above
    for pay, core, lo in ((lp, lc, 0), (rp, rc, CW - 3)):
        if flip:
            for j in range(3):
                for k in range(3):
                    cat[k : k + 1, :] = scr[(3 + k) * CW + lo + j : (3 + k) * CW + lo + j + 1, :]
                    cat[3 + width + k : 4 + width + k, :] = scr[(6 + k) * CW + lo + j : (6 + k) * CW + lo + j + 1, :]
                cat[3 : 3 + width, :] = core[j].astype(f32)
                pay[j] = cat[0 : width + 6, :].astype(bf16)
        else:
            pay[0:width, :] = core[...]
            for end in range(2):
                for k in range(3):
                    src = (3 + 3 * end + k) * CW + lo
                    cat[end * 9 + k * 3 : end * 9 + k * 3 + 3, :] = scr[src : src + 3, :]
            pay[width : width + 32, :] = cat[0:32, :].astype(bf16)


def join(place, near, far, blk_b, lc, rc, flip):
    CW, C = far.shape[1:]
    width = lc.shape[1] if flip else lc.shape[0]
    sd = jax.ShapeDtypeStruct
    pay = sd((3, width + 6, C) if flip else (width + 32, C), bf16)
    return pl.pallas_call(
        functools.partial(join_body, CW, width, flip),
        out_shape=(sd((3, CW, C), bf16),) * 2 + (pay, pay),
        in_specs=[SMEM] + [VMEM] * 5,
        out_specs=[VMEM] * 4,
        scratch_shapes=[pltpu.VMEM((max(2 * CW + 8, width + 8), C), f32), pltpu.VMEM((9 * CW, C), f32)],
        compiler_params=SMALL,
        name="join",
    )(place, near, far, blk_b, lc, rc)


def far_rows(send, last, quot, work=lambda: ()):
    nl = lax.axis_size("lon")
    nt = lax.axis_size("lat")
    top = (nt - 1) * nl
    axes = ("lat", "lon")
    swap = [(a * nl + e, (a + 1) * nl + e) for a in range(1, nt - 1, 2) for e in range(nl)]
    swap += [(j, i) for i, j in swap]

    def branch(q):
        def run():
            fa = [(top + e, top + (q - e) % nl) for e in range(nl)]
            fb = [(top + e, top + (q - 1 - e) % nl) for e in range(nl)]
            return lax.ppermute(send, axes, swap + fa), lax.ppermute(last, axes, fb), work()

        return run

    return lax.switch(quot, [branch(q) for q in range(nl)])


def shift_pairs(axis, by):
    n = lax.axis_size(axis)
    return [(i, (i + by) % n) for i in range(n)]


def on_device(
    field, land, mirror, depth_weight, norm_gain, up_weight, up_bias, down_proj, layer_scale,
    section_gain, section_weight, section_bias, cotangent,
):
    R, CW, C = field.shape
    total = R * CW * lax.axis_size("lat") * lax.axis_size("lon")
    factor = 1.0 / math.sqrt(total / 64.0)
    near, send, last, shift = rim(field, mirror)
    near = lax.ppermute(near, "lat", flip_pairs("lat", 1))
    far, blk_b, (lc, rc) = far_rows(send, last, shift[0], lambda: sides(field))
    south_f, north_f, lpay, rpay = join(shift, near, far, blk_b, lc, rc, True)
    right_f = lax.ppermute(lpay, "lon", shift_pairs("lon", -1))
    left_f = lax.ppermute(rpay, "lon", shift_pairs("lon", 1))
    level, g, direct, send, last, lcol, rcol, keep, away = block_pass(
        field, south_f, north_f, left_f, right_f, land.T, depth_weight, norm_gain, up_weight, up_bias, down_proj,
        layer_scale, section_gain, section_weight, section_bias, cotangent,
    )

    place = (lax.axis_index("lat") // 2) * 2 + lax.axis_index("lon") % 2
    got = lax.ppermute(away, "lat", flip_pairs("lat", 1))
    held = add_bf(keep, got[:HALF]).reshape(4, HALF // 4, C)
    send, held = lax.optimization_barrier((send, held))
    chunk = square_sum(held, place)
    far, blk_b, base = far_rows(
        send, last, shift[0], lambda: conv_back(g, direct, depth_weight, R, CW)
    )
    chunk, far = lax.optimization_barrier((chunk, far))
    south_g, north_g, lpay, rpay = join(shift, got, far, blk_b, lcol, rcol, False)
    chunk, lpay = lax.optimization_barrier((chunk, lpay))
    gr = lax.ppermute(lpay, "lon", shift_pairs("lon", -1))
    gl = lax.ppermute(rpay, "lon", shift_pairs("lon", 1))
    chunk = line_sum(chunk)
    grad_field = edges(base, south_g, north_g, gl, gr, depth_weight, R, CW)
    axes = ("lat", "lon")
    back = [lax.ppermute(chunk, axes, square_pairs(k)) for k in (1, 2, 3)]
    back[0], grad_field = lax.optimization_barrier((back[0], grad_field))
    mine = jnp.stack([chunk] + back)
    other = lax.ppermute(mine, "lat", flip_pairs("lat", 1))
    g_depth, g_up, g_down, g_sec = finish(mine, other, factor)
    return level, grad_field, g_depth, g_up, g_down, g_sec


def solution(mesh):
    cells = P("lat", "lon", None)
    in_specs = (cells, P("lat", "lon")) + (P(),) * 10 + (cells,)
    out_specs = (cells, cells, P(), P(), P(), P())
    return jax.shard_map(on_device, mesh=mesh, in_specs=in_specs, out_specs=out_specs, check_vma=False)
```

```python
import functools
import math

import jax
import jax.numpy as jnp
from jax import lax
from jax.experimental import pallas as pl
from jax.experimental.pallas import tpu as pltpu
from jax.sharding import PartitionSpec as P

SECTIONS = 3
EPS = 1e-6
f32, bf16 = jnp.float32, jnp.bfloat16
S = 16
LOG2E = 1.4426950408889634
LOG2_DENS = -0.3257480647361593
HALF = 1344
VMEM = pl.BlockSpec(memory_space=pltpu.VMEM)
SMEM = pl.BlockSpec(memory_space=pltpu.SMEM)
PARAMS = pltpu.CompilerParams(vmem_limit_bytes=44 * 2**20)
WHOLE = pltpu.CompilerParams(vmem_limit_bytes=63 * 2**20 + 2**19)
SMALL = pltpu.CompilerParams(vmem_limit_bytes=24 * 2**20)


def dot(a, b):
    return jnp.dot(a, b, preferred_element_type=f32)


def dot_t(a, b):
    return lax.dot_general(a, b, (((0,), (0,)), ((), ())), preferred_element_type=f32)


def dot_r(a, b):
    return lax.dot_general(a, b, (((1,), (1,)), ((), ())), preferred_element_type=f32)


def ones_mean(n):
    return jnp.full((n, 128), 1.0 / 128, bf16)


def pair_mean():
    r = lax.broadcasted_iota(jnp.int32, (256, 256), 0) // 128
    c = lax.broadcasted_iota(jnp.int32, (256, 256), 1) // 128
    return jnp.where(r == c, 1.0 / 128, 0.0).astype(bf16)


def split2(x):
    hi = x.astype(bf16)
    lo = (x - hi.astype(f32)).astype(bf16)
    return jnp.concatenate([hi, lo], axis=1)


def norm_bwd(u, hat, rstd, pm):
    m = dot(jnp.concatenate([u.astype(bf16), (u * hat).astype(bf16)], axis=1), pm)
    return rstd * (u - m[:, :128] - hat * m[:, 128:])


def gelu2(h):
    g = h * 0.7071067811865476
    c = 1.0 + lax.erf(g)
    e = jnp.exp2(g * g * (-LOG2E) + LOG2_DENS)
    return h * c, c + h * e


def weights_table(dw, w49, flip):
    for t in range(49):
        w49[48 - t if flip else t] = jnp.broadcast_to(dw[t : t + 1, :].astype(f32), (S, 128)).astype(w49.dtype)


def conv49(el, w49, emit, I, CW):
    CE = CW + 6
    CG = 4

    def step(n, _):
        i = n // (CW // CG)
        c0 = (n % (CW // CG)) * CG
        acc = [None] * CG
        for a in range(7):
            row = [el[(i + a) * CE + c0 + m].astype(f32) for m in range(CG + 6)]
            for b in range(7):
                w = w49[a * 7 + b].astype(f32)
                for k in range(CG):
                    pr = row[k + b] * w
                    acc[k] = pr if acc[k] is None else acc[k] + pr
        for k in range(CG):
            emit(i, c0 + k, acc[k])
        return 0

    lax.fori_loop(0, I * (CW // CG), step, 0)


def block_body(
    R, CW,
    field, south, north, left, right, land, dw, gain, upw, bias, down, scale, sgain, sw, sbias, cot,
    bott, gout, dirout, send, last, lcol, rcol, keep, away,
    x2d, el, w49, dep, hat, rst, nrm, act, slp, shat, srst, p1, back, tacc, downs, ups, mgs, landb, up, dn, sums,
):
    I = R // S
    CE = CW + 6
    XW = 40
    n0 = R * CW

    def asm(r, _):
        x2d[pl.ds((r + 3) * XW + (r + 3) // I + 3, CW), :] = field[r].astype(f32)
        return 0

    lax.fori_loop(0, R, asm, 0, unroll=4)
    PB = I * XW + 1
    for k in range(3):
        x2d[pl.ds(k * XW + 3, CW), :] = south[k].astype(f32)
        x2d[pl.ds((R + 3 + k) * XW + (R + 3 + k) // I + 3, CW), :] = north[k].astype(f32)
        for m in range((R + 6 + I - 1) // I):
            rows = min(I, R + 6 - m * I)
            x2d[pl.ds(m * PB + k, rows, stride=XW), :] = left[k, m * I : m * I + rows, :].astype(f32)
            x2d[pl.ds(m * PB + CW + 3 + k, rows, stride=XW), :] = right[k, m * I : m * I + rows, :].astype(f32)

    def tr(i, _):
        for c in range(CE):
            el[i * CE + c] = x2d[pl.ds(i * XW + i // I + c, S, stride=PB), :].astype(bf16)
        return 0

    lax.fori_loop(0, I + 6, tr, 0)
    weights_table(dw, w49, False)
    p_at = lax.broadcasted_iota(jnp.int32, (R, R), 0)
    p_row = lax.broadcasted_iota(jnp.int32, (R, R), 1)
    order = (p_row == (p_at % S) * I + p_at // S).astype(f32).astype(bf16)
    land_p = dot_r(order, land[...].astype(f32).astype(bf16)).astype(bf16)
    spread = (
        lax.broadcasted_iota(jnp.int32, (CW, CW * 128), 1) // 128
        == lax.broadcasted_iota(jnp.int32, (CW, CW * 128), 0)
    )
    land_w = dot(land_p, spread.astype(f32).astype(bf16)).astype(bf16)
    for i in range(I):
        for c in range(CW):
            at = (i * CW + c) * S
            landb[at : at + S, :] = land_w[i * S : (i + 1) * S, c * 128 : (c + 1) * 128]
    dn[...] = (down[...].astype(f32) * 0.5).astype(bf16)
    up[0:128, :] = upw[...]
    up[128:256, :] = jnp.where(
        lax.broadcasted_iota(jnp.int32, (128, 512), 0) == 0, bias[...].astype(f32).reshape(1, 512), 0.0
    ).astype(bf16)

    def emit(i, c, v):
        dep[pl.ds((i * CW + c) * S, S), :] = v

    conv49(el, w49, emit, I, CW)

    jj, j1, pm = ones_mean(256), ones_mean(128), pair_mean()
    g_n = gain[...].astype(f32).reshape(1, 128)
    sc = scale[...].astype(f32).reshape(1, 128)
    sg0 = sgain[0:1, :].astype(f32)
    T1 = n0

    def nfwd(n, _):
        base = pl.multiple_of(n * T1, T1)
        x = dep[pl.ds(base, T1), :]
        cen = x - dot(split2(x), jj)
        rs = lax.rsqrt(dot((cen * cen).astype(bf16), j1) + EPS)
        ht = cen * rs
        hat[pl.ds(base, T1), :] = ht
        rst[pl.ds(base, T1), :] = rs
        nrm[pl.ds(base, T1), :] = (ht * g_n).astype(bf16)
        return 0

    lax.fori_loop(0, n0 // T1, nfwd, 0)

    T2 = n0 // 2
    onec = (lax.broadcasted_iota(jnp.int32, (T2, 128), 1) == 0).astype(f32).astype(bf16)

    def upf(n, _):
        base = pl.multiple_of(n * T2, T2)
        lhs = jnp.concatenate([nrm[pl.ds(base, T2), :], onec], axis=1)
        for q in range(2):
            hid = dot(lhs, up[:, q * 256 : (q + 1) * 256])
            ac, sl = gelu2(hid)
            act[pl.ds(base, T2), q * 256 : (q + 1) * 256] = ac.astype(bf16)
            slp[pl.ds(base, T2), q * 256 : (q + 1) * 256] = sl.astype(bf16)
        return 0

    lax.fori_loop(0, n0 // T2, upf, 0)

    TP = 2 * CW * S

    def sect_norm(lv, s):
        cen = lv.astype(f32) - dot(lv, j1)
        rs1 = lax.rsqrt(dot((cen * cen).astype(bf16), j1) + EPS)
        h1 = cen * rs1
        return h1, rs1, (h1 * sgain[s : s + 1, :].astype(f32)).astype(bf16)

    def dnf(i2, _):
        base = pl.multiple_of(i2 * TP, TP)
        mixed = dot(act[pl.ds(base, TP), :], dn[...])
        xs = jnp.concatenate(
            [el[pl.ds((i2 * 2 + a + 3) * CE + 3, CW)].reshape(CW * S, 128) for a in range(2)], axis=0
        ).astype(f32)
        lv = (landb[pl.ds(base, TP), :].astype(f32) * (xs + sc * mixed)).astype(bf16)
        h1, rs1, sn = sect_norm(lv, 0)
        shat[pl.ds(base, TP), :] = h1
        srst[pl.ds(base, TP), :] = rs1
        sn = sn.reshape(2, CW // 2, 2, S, 128)
        pb = pl.multiple_of(i2 * (TP // 4), TP // 4)
        for a in range(2):
            for b in range(2):
                k = 2 * a + b
                p1[pl.ds(pb, TP // 4), k * 128 : (k + 1) * 128] = sn[a, :, b].reshape(TP // 4, 128)
        return 0

    lax.fori_loop(0, I // 2, dnf, 0, unroll=2)

    def to_patches(sn, ii, cc):
        v = sn.reshape(ii // 2, 2, cc // 2, 2, S, 128)
        return jnp.concatenate(
            [v[:, a, :, b].reshape(ii * cc * S // 4, 128) for a in range(2) for b in range(2)], axis=1
        )

    def from_patches(sp, ii, cc):
        ps = [sp[:, k * 128 : (k + 1) * 128].reshape(ii // 2, cc // 2, S, 128) for k in range(4)]
        rows = [jnp.stack([ps[2 * a], ps[2 * a + 1]], axis=2).reshape(ii // 2, cc, S, 128) for a in range(2)]
        return jnp.stack(rows, axis=1).reshape(ii * cc * S, 128)

    def put(at, value, blocks):
        for q in range(blocks):
            sums[at + q * 128 : at + (q + 1) * 128, :] = value[:, q * 128 : (q + 1) * 128].astype(bf16)

    l1 = (dot(p1[...], sw[0]) + sbias[0:1, :].astype(f32)).astype(bf16)
    h1, r1, sn1 = sect_norm(l1, 1)
    P2 = to_patches(sn1, I // 2, CW // 2)
    l2 = (dot(P2, sw[1]) + sbias[1:2, :].astype(f32)).astype(bf16)
    h2, r2, sn2 = sect_norm(l2, 2)
    P3 = to_patches(sn2, I // 4, CW // 4)
    l3 = (dot(P3, sw[2]) + sbias[2:3, :].astype(f32)).astype(bf16)
    Q = CW // 8
    for c in range(Q):
        x2d[pl.ds(c, S, stride=Q), :] = l3[c * S : (c + 1) * S, :].astype(f32)
    for r in range(S):
        bott[r] = x2d[r * Q : (r + 1) * Q, :].astype(bf16)
        x2d[128 + r * Q : 128 + (r + 1) * Q, :] = cot[r].astype(f32)
    b3 = jnp.concatenate([x2d[pl.ds(128 + c, S, stride=Q), :] for c in range(Q)], axis=0).astype(bf16)
    put(1024, dot_t(b3, P3), 4)
    u2 = from_patches(dot_r(b3, sw[2]), I // 4, CW // 4) * sgain[2:3, :].astype(f32)
    b2 = norm_bwd(u2, h2, r2, pm).astype(bf16)
    put(512, dot_t(b2, P2), 4)
    u1 = from_patches(dot_r(b2, sw[1]), I // 2, CW // 2) * sgain[1:2, :].astype(f32)
    b1 = norm_bwd(u1, h1, r1, pm).astype(bf16)
    put(0, dot_t(b1, p1[...]), 4)
    back[...] = b1

    QP = TP // 4

    def bk1(i2, _):
        pb = pl.multiple_of(i2 * QP, QP)
        bk = back[pl.ds(pb, QP), :]
        base = pl.multiple_of(i2 * TP, TP)
        us = []
        for a in range(2):
            sp = dot_r(bk, sw[0, a * 256 : (a + 1) * 256, :])
            us.append(
                jnp.stack(
                    [sp[:, :128].reshape(CW // 2, S, 128), sp[:, 128:].reshape(CW // 2, S, 128)], axis=1
                ).reshape(TP // 2, 128)
            )
        u = jnp.concatenate(us, axis=0) * sg0
        b0 = norm_bwd(u, shat[pl.ds(base, TP), :], srst[pl.ds(base, TP), :], pm).astype(bf16).astype(f32)
        dr = landb[pl.ds(base, TP), :].astype(f32) * b0
        dirout[pl.ds(base, TP), :] = dr.astype(bf16)
        mgs[pl.ds(base, TP), :] = (dr * sc).astype(bf16)
        return 0

    lax.fori_loop(0, I // 2, bk1, 0, unroll=4)

    def bk2(n, _):
        base = pl.multiple_of(n * T2, T2)
        mg = mgs[pl.ds(base, T2), :]
        for q in range(2):
            ag = dot_r(mg, dn[q * 256 : (q + 1) * 256, :])
            sl = slp[pl.ds(base, T2), q * 256 : (q + 1) * 256].astype(f32)
            slp[pl.ds(base, T2), q * 256 : (q + 1) * 256] = (ag * sl).astype(bf16)
        return 0

    lax.fori_loop(0, n0 // T2, bk2, 0)

    def bk3(n, _):
        base = pl.multiple_of(n * T1, T1)
        ng = dot_r(slp[pl.ds(base, T1), :], up[0:128, :])
        dg = norm_bwd(ng * g_n, hat[pl.ds(base, T1), :], rst[pl.ds(base, T1), :], pm)
        gout[pl.ds(base, T1), :] = dg.astype(bf16)
        return 0

    lax.fori_loop(0, n0 // T1, bk3, 0)
    downs[...] = dot_t(mgs[...], act[...]) * 0.5
    ups[...] = dot_t(nrm[...], slp[...])
    put(1536, downs[...], 4)
    put(2048, ups[...], 4)

    tacc[...] = jnp.zeros_like(tacc)

    def tap(n, _):
        i = n // (CW // 8)
        c0 = (n % (CW // 8)) * 8
        g = [gout[pl.ds((i * CW + c0 + k) * S, S), :].astype(f32) for k in range(8)]
        for a in range(7):
            row = [el[(i + a) * CE + c0 + m].astype(f32) for m in range(14)]
            for b in range(7):
                s = None
                for k in range(8):
                    pr = row[k + b] * g[k]
                    s = pr if s is None else s + pr
                tacc[a * 7 + b] += s[:8] + s[8:]
        return 0

    lax.fori_loop(0, I * (CW // 8), tap, 0, unroll=2)
    ts = [jnp.sum(tacc[t], axis=0, keepdims=True) for t in range(49)]
    ts = jnp.concatenate(ts + [jnp.zeros((15, 128), f32)], axis=0)
    sums[2560:2624, :] = ts.astype(bf16)
    sums[2624:2688, :] = jnp.zeros((64, 128), bf16)

    odd = lax.axis_index("lat") % 2
    keep[...] = sums[pl.ds(pl.multiple_of(odd * HALF, 64), HALF), :]
    away[0:HALF, :] = sums[pl.ds(pl.multiple_of((1 - odd) * HALF, 64), HALF), :]
    x2d[0:n0, :] = gout[...].astype(f32)
    for k in range(3):
        lo = x2d[pl.ds(k * CW * S, CW, stride=S), :].astype(bf16)
        hi = x2d[pl.ds((I - 3 + k) * CW * S + S - 1, CW, stride=S), :].astype(bf16)
        last[k] = hi
        send[k] = jnp.where(odd == 1, hi, lo)
        away[HALF + k * CW : HALF + (k + 1) * CW, :] = jnp.where(odd == 1, lo, hi)
    for i in range(I):
        lcol[i * 3 * S : (i + 1) * 3 * S, :] = gout[i * CW * S : (i * CW + 3) * S, :]
        rcol[i * 3 * S : (i + 1) * 3 * S, :] = gout[((i + 1) * CW - 3) * S : (i + 1) * CW * S, :]


def block_pass(field, south, north, left, right, land, dw, gain, upw, bias, down, scale, sgain, sw, sbias, cot):
    R, CW, C = field.shape
    n = R * CW
    I = R // S
    sd = jax.ShapeDtypeStruct
    out_shape = (
        sd((S, CW // 8, C), bf16),
        sd((n, C), bf16),
        sd((n, C), bf16),
        sd((3, CW, C), bf16),
        sd((3, CW, C), bf16),
        sd((I * 3 * S, C), bf16),
        sd((I * 3 * S, C), bf16),
        sd((HALF, C), bf16),
        sd((HALF + 3 * CW, C), bf16),
    )
    V = pltpu.VMEM
    scratch = [
        V(((R + 6) * 40 + (R + 6) // I + 16, C), f32),
        V(((I + 6) * (CW + 6), S, C), bf16),
        V((49, S, C), bf16),
        V((n, C), f32),
        V((n, C), f32),
        V((n, C), f32),
        V((n, C), bf16),
        V((n, 512), bf16),
        V((n, 512), bf16),
        V((n, C), f32),
        V((n, C), f32),
        V((n // 4, 512), bf16),
        V((n // 4, C), bf16),
        V((49, 8, C), f32),
        V((C, 512), f32),
        V((C, 512), f32),
        V((n, C), bf16),
        V((n, C), bf16),
        V((256, 512), bf16),
        V((512, 128), bf16),
        V((2 * HALF, C), bf16),
    ]
    return pl.pallas_call(
        functools.partial(block_body, R, CW),
        out_shape=out_shape,
        in_specs=[VMEM] * 16,
        out_specs=[VMEM] * 9,
        scratch_shapes=scratch,
        compiler_params=PARAMS,
        name="block_pass",
    )(field, south, north, left, right, land, dw, gain, upw, bias, down, scale, sgain, sw, sbias, cot)


def conv_back_body(R, CW, g, dirin, dw, out, gx, gext, w49):
    I = R // S
    CE = CW + 6
    row = lax.broadcasted_iota(jnp.int32, (S, 128), 0)
    zero = jnp.zeros((3, S, 128), bf16)

    def cpy(i, _):
        gext[pl.ds((i + 3) * CE, 3)] = zero
        gext[pl.ds((i + 3) * CE + 3, CW)] = g[pl.ds(pl.multiple_of(i * CW * S, CW * S), CW * S), :].reshape(CW, S, 128)
        gext[pl.ds((i + 3) * CE + 3 + CW, 3)] = zero
        return 0

    lax.fori_loop(0, I, cpy, 0)
    for k in range(3):

        def shift(c, _, k=k):
            v = pltpu.roll(gext[(I + k) * CE + c].astype(f32), 1, 0)
            gext[k * CE + c] = jnp.where(row == 0, 0.0, v).astype(bf16)
            v = pltpu.roll(gext[(3 + k) * CE + c].astype(f32), S - 1, 0)
            gext[(I + 3 + k) * CE + c] = jnp.where(row == S - 1, 0.0, v).astype(bf16)
            return 0

        lax.fori_loop(0, CE, shift, 0, unroll=2)
    weights_table(dw, w49, True)

    def emit(i, c, v):
        at = pl.multiple_of((i * CW + c) * S, S)
        out[pl.ds(at, S), :] = (v + dirin[pl.ds(at, S), :].astype(f32)).astype(bf16)

    conv49(gext, w49, emit, I, CW)


def conv_back(g, dirin, dw, R, CW):
    C = g.shape[1]
    I = R // S
    return pl.pallas_call(
        functools.partial(conv_back_body, R, CW),
        out_shape=jax.ShapeDtypeStruct((R * CW, C), bf16),
        in_specs=[VMEM] * 3,
        out_specs=VMEM,
        scratch_shapes=[
            pltpu.VMEM((8, C), f32),
            pltpu.VMEM(((I + 6) * (CW + 6), S, C), bf16),
            pltpu.VMEM((49, S, C), bf16),
        ],
        compiler_params=SMALL,
        cost_estimate=pl.CostEstimate(flops=10**8, bytes_accessed=30 * 2**20, transcendentals=0),
        name="conv_back",
    )(g, dirin, dw)


def edges_body(R, CW, base, south, north, gl, gr, dw, out, acc, rows, cols, w49):
    I = R // S
    CE = CW + 6
    isn = on_top().astype(f32)
    nots = 1.0 - isn
    core = I * 3 * S
    row = lax.broadcasted_iota(jnp.int32, (S, 128), 0)
    for t in range(49):
        w49[t] = jnp.broadcast_to(dw[t : t + 1, :].astype(f32), (S, 128))
    for side in range(2):
        for k in range(3):
            at = core + side * 9 + k * 3
            mid = (north if side else south)[k]
            rows[pl.ds((side * 3 + k) * 40, CE), :] = jnp.concatenate(
                [gl[at : at + 3, :], mid, gr[at : at + 3, :]], axis=0
            ).astype(f32)

    def taps(k, a, flip):
        s = None
        for b in range(7):
            o = 6 - b if flip else b
            pr = rows[pl.ds(k * 40 + o, CW), :] * w49[7 * a + b, 0:1, :]
            s = pr if s is None else s + pr
        return s

    low = []
    for r in range(3):
        low.append(sum(taps(k, r + 6 - k, True) for k in range(r, 3)))
    high = []
    for t in range(3):
        v = sum(taps(3 + k, 2 - t - k, True) for k in range(3 - t)) * nots
        k1 = t + 1
        f = sum(taps(3 + rho, 5 + k1 - rho, False) for rho in range(k1 - 1, 3)) * isn
        high.append(v + f)
    for side in range(2):
        src = gr if side else gl

        def fill(i, _, src=src, side=side):
            for j in range(3):
                at = pl.multiple_of((i * 3 + j) * S, S)
                cols[side * (I + 6) * 3 + (i + 3) * 3 + j] = src[pl.ds(at, S), :].astype(f32)
            return 0

        lax.fori_loop(0, I, fill, 0)
        for k in range(3):
            for j in range(3):
                at = side * (I + 6) * 3
                v = pltpu.roll(cols[at + (I + k) * 3 + j], 1, 0)
                cols[at + k * 3 + j] = jnp.where(row == 0, 0.0, v)
                v = pltpu.roll(cols[at + (3 + k) * 3 + j], S - 1, 0)
                cols[at + (I + 3 + k) * 3 + j] = jnp.where(row == S - 1, 0.0, v)

    PITCH = CW * S

    def step(i, _):
        at = pl.multiple_of(i * PITCH, PITCH)
        acc[pl.ds(at, PITCH), :] = base[pl.ds(at, PITCH), :].astype(f32)
        for side in range(2):
            for t in range(3):
                s = None
                for j in range(3):
                    b = 2 - t - j if side else t + 6 - j
                    if b < 0 or b > 6:
                        continue
                    for a in range(7):
                        pr = cols[side * (I + 6) * 3 + (i + 6 - a) * 3 + j] * w49[7 * a + b]
                        s = pr if s is None else s + pr
                c = CW - 1 - t if side else t
                at = pl.multiple_of(i * PITCH + c * S, S)
                acc[pl.ds(at, S), :] += s
        return 0

    lax.fori_loop(0, I, step, 0)

    def unt(r, _):
        s = r // I
        i = r % I
        out[r] = acc[pl.ds(i * PITCH + s, CW, stride=S), :].astype(bf16)
        return 0

    lax.fori_loop(3, R - 3, unt, 0, unroll=2)
    for r in list(range(3)) + list(range(R - 3, R)):
        v = acc[pl.ds((r % I) * PITCH + r // I, CW, stride=S), :]
        v = v + (low[r] if r < 3 else high[R - 1 - r])
        out[r] = v.astype(bf16)


def edges(base, south, north, gl, gr, dw, R, CW):
    C = base.shape[1]
    I = R // S
    return pl.pallas_call(
        functools.partial(edges_body, R, CW),
        out_shape=jax.ShapeDtypeStruct((R, CW, C), bf16),
        in_specs=[VMEM] * 6,
        out_specs=VMEM,
        scratch_shapes=[
            pltpu.VMEM((R * CW, C), f32),
            pltpu.VMEM((240, C), f32),
            pltpu.VMEM((2 * (I + 6) * 3, S, C), f32),
            pltpu.VMEM((49, S, C), f32),
        ],
        compiler_params=SMALL,
        cost_estimate=pl.CostEstimate(flops=10**8, bytes_accessed=10 * 2**20, transcendentals=0),
        name="edges",
    )(base, south, north, gl, gr, dw)


def finish_body(factor, chunk, mine, other, o_depth, o_up, o_down, o_sec, full):
    core = lax.axis_index("lat") % 2
    place = (lax.axis_index("lat") // 2) * 2 + lax.axis_index("lon") % 2
    half = 4 * chunk
    for j in range(4):
        src = lax.bitwise_xor(place, j)
        at = pl.multiple_of(core * half + j * chunk, 16)
        full[pl.ds(at, chunk), :] = mine[src]
        at = pl.multiple_of((1 - core) * half + j * chunk, 16)
        full[pl.ds(at, chunk), :] = other[src]

    def block(n):
        return full[n * 128 : (n + 1) * 128, :].astype(f32) * factor

    for s in range(3):
        for q in range(4):
            o_sec[s, q * 128 : (q + 1) * 128, :] = block(s * 4 + q).T
    for q in range(4):
        o_down[q * 128 : (q + 1) * 128, :] = block(12 + q).T
        o_up[:, q * 128 : (q + 1) * 128] = block(16 + q)
    o_depth[...] = block(20)[:49, :]


def finish(mine, other, factor):
    chunk = mine.shape[1]
    sd = jax.ShapeDtypeStruct
    return pl.pallas_call(
        functools.partial(finish_body, factor, chunk),
        out_shape=(sd((49, 128), f32), sd((128, 512), f32), sd((512, 128), f32), sd((3, 512, 128), f32)),
        in_specs=[VMEM, VMEM],
        out_specs=[VMEM] * 4,
        scratch_shapes=[pltpu.VMEM((8 * chunk, 128), bf16)],
        compiler_params=SMALL,
        name="finish_sums",
    )(mine, other)


def add_bf(*vals):
    vals = [v.astype(f32) for v in vals]
    while len(vals) > 1:
        vals = [vals[i] + vals[i + 1] for i in range(0, len(vals), 2)]
    return vals[0].astype(bf16)


def flip_pairs(axis, bits):
    return [(i, i ^ bits) for i in range(lax.axis_size(axis))]


def both_pairs(lat_bits, lon_bits):
    nl = lax.axis_size("lon")
    return [
        (a * nl + b, (a ^ lat_bits) * nl + (b ^ lon_bits))
        for a in range(lax.axis_size("lat"))
        for b in range(nl)
    ]


def square_pairs(k):
    return both_pairs((k // 2) * 2, k % 2)


def square_sum(held, place):
    own = lax.dynamic_index_in_dim(held, place, 0, keepdims=False)
    came = []
    for k in (1, 2, 3):
        part = lax.dynamic_index_in_dim(held, lax.bitwise_xor(place, k), 0, keepdims=False)
        came.append(lax.ppermute(part, ("lat", "lon"), square_pairs(k)))
    return add_bf(own, *came)


def line_sum(total):
    left = lax.axis_size("lon") // 2
    bit = 2
    while left > 1:
        if left % 4 == 0:
            total = add_bf(total, *[lax.ppermute(total, "lon", flip_pairs("lon", bit * k)) for k in (1, 2, 3)])
            left //= 4
            bit *= 4
        else:
            total = add_bf(total, lax.ppermute(total, "lon", flip_pairs("lon", bit)))
            left //= 2
            bit *= 2
    return total


def on_top():
    return lax.axis_index("lat") == lax.axis_size("lat") - 1


def rim_body(R, CW, field, mirror, near, send, last, place, low, high, mir, sems):
    odd = lax.axis_index("lat") % 2
    copies = [
        pltpu.make_async_copy(mirror, mir, sems.at[0]),
        pltpu.make_async_copy(field.at[0:3], low, sems.at[1]),
        pltpu.make_async_copy(field.at[R - 3 : R], high, sems.at[2]),
    ]
    for c in copies:
        c.start()
    for c in copies:
        c.wait()
    for k in range(3):
        lo = low[k]
        hi = high[k]
        last[k] = hi
        send[k] = jnp.where(odd == 1, hi, lo)
        near[k] = jnp.where(odd == 1, lo, hi)
    place[0] = mir[0] // CW
    place[1] = mir[0] % CW


def rim(field, mirror):
    R, CW, C = field.shape
    sd = jax.ShapeDtypeStruct
    hbm = pl.BlockSpec(memory_space=pltpu.HBM)
    return pl.pallas_call(
        functools.partial(rim_body, R, CW),
        out_shape=(sd((3, CW, C), bf16),) * 3 + (sd((2,), jnp.int32),),
        in_specs=[hbm, hbm],
        out_specs=[VMEM] * 3 + [SMEM],
        scratch_shapes=[
            pltpu.VMEM((3, CW, C), bf16),
            pltpu.VMEM((3, CW, C), bf16),
            pltpu.SMEM(mirror.shape, jnp.int32),
            pltpu.SemaphoreType.DMA((3,)),
        ],
        compiler_params=WHOLE,
        name="rim",
    )(field, mirror)


def sides_body(R, CW, field, lc, rc, low, high, cols, sems):
    copies = [
        pltpu.make_async_copy(field.at[:, 0:16], low, sems.at[0]),
        pltpu.make_async_copy(field.at[:, CW - 16 : CW], high, sems.at[1]),
    ]
    for c in copies:
        c.start()
    for c in copies:
        c.wait()
    cols[0 : R * 8, :] = low[:, 0:8, :].astype(f32).reshape(R * 8, 128)
    cols[R * 8 :, :] = high[:, 8:16, :].astype(f32).reshape(R * 8, 128)
    for k in range(3):
        lc[k] = cols[pl.ds(k, R, stride=8), :].astype(bf16)
        rc[k] = cols[pl.ds(R * 8 + 5 + k, R, stride=8), :].astype(bf16)


def sides(field):
    R, CW, C = field.shape
    sd = jax.ShapeDtypeStruct
    return pl.pallas_call(
        functools.partial(sides_body, R, CW),
        out_shape=(sd((3, R, C), bf16),) * 2,
        in_specs=[pl.BlockSpec(memory_space=pltpu.HBM)],
        out_specs=[VMEM] * 2,
        scratch_shapes=[
            pltpu.VMEM((R, 16, C), bf16),
            pltpu.VMEM((R, 16, C), bf16),
            pltpu.VMEM((2 * R * 8, C), f32),
            pltpu.SemaphoreType.DMA((2,)),
        ],
        compiler_params=SMALL,
        name="sides",
    )(field)


def join_body(CW, width, flip, place, near, far, blk_b, lc, rc, south, north, lp, rp, cat, scr):
    odd = lax.axis_index("lat") % 2 == 1
    top = on_top()
    rem = place[1]
    at = lax.broadcasted_iota(jnp.int32, (CW, CW), 0)
    turn = (at + lax.broadcasted_iota(jnp.int32, (CW, CW), 1) == CW - 1).astype(f32).astype(bf16)
    for k in range(3):
        cat[0:CW, :] = blk_b[k].astype(f32)
        cat[CW : 2 * CW, :] = far[k].astype(f32)
        win = cat[pl.ds(rem + 1, CW), :].astype(bf16)
        scr[k * CW : (k + 1) * CW, :] = dot(turn, win)
    for k in range(3):
        m = 2 - k if flip else k
        beyond = scr[m * CW : (m + 1) * CW, :]
        close = (near[k] if flip else near[HALF + k * CW : HALF + (k + 1) * CW, :]).astype(f32)
        above = jnp.where(odd, far[k].astype(f32), close)
        below = jnp.where(odd, close, far[k].astype(f32))
        above = jnp.where(top, beyond, above)
        south[k] = below.astype(bf16)
        north[k] = above.astype(bf16)
        scr[(3 + k) * CW : (4 + k) * CW, :] = below
        scr[(6 + k) * CW : (7 + k) * CW, :] = above
    for pay, core, lo in ((lp, lc, 0), (rp, rc, CW - 3)):
        if flip:
            for j in range(3):
                for k in range(3):
                    cat[k : k + 1, :] = scr[(3 + k) * CW + lo + j : (3 + k) * CW + lo + j + 1, :]
                    cat[3 + width + k : 4 + width + k, :] = scr[(6 + k) * CW + lo + j : (6 + k) * CW + lo + j + 1, :]
                cat[3 : 3 + width, :] = core[j].astype(f32)
                pay[j] = cat[0 : width + 6, :].astype(bf16)
        else:
            pay[0:width, :] = core[...]
            for end in range(2):
                for k in range(3):
                    src = (3 + 3 * end + k) * CW + lo
                    cat[end * 9 + k * 3 : end * 9 + k * 3 + 3, :] = scr[src : src + 3, :]
            pay[width : width + 32, :] = cat[0:32, :].astype(bf16)


def join(place, near, far, blk_b, lc, rc, flip):
    CW, C = far.shape[1:]
    width = lc.shape[1] if flip else lc.shape[0]
    sd = jax.ShapeDtypeStruct
    pay = sd((3, width + 6, C) if flip else (width + 32, C), bf16)
    return pl.pallas_call(
        functools.partial(join_body, CW, width, flip),
        out_shape=(sd((3, CW, C), bf16),) * 2 + (pay, pay),
        in_specs=[SMEM] + [VMEM] * 5,
        out_specs=[VMEM] * 4,
        scratch_shapes=[pltpu.VMEM((max(2 * CW + 8, width + 8), C), f32), pltpu.VMEM((9 * CW, C), f32)],
        compiler_params=SMALL,
        name="join",
    )(place, near, far, blk_b, lc, rc)


def far_rows(send, last, quot, work=lambda: ()):
    nl = lax.axis_size("lon")
    nt = lax.axis_size("lat")
    top = (nt - 1) * nl
    axes = ("lat", "lon")
    swap = [(a * nl + e, (a + 1) * nl + e) for a in range(1, nt - 1, 2) for e in range(nl)]
    swap += [(j, i) for i, j in swap]

    def branch(q):
        def run():
            fa = [(top + e, top + (q - e) % nl) for e in range(nl)]
            fb = [(top + e, top + (q - 1 - e) % nl) for e in range(nl)]
            return lax.ppermute(send, axes, swap + fa), lax.ppermute(last, axes, fb), work()

        return run

    return lax.switch(quot, [branch(q) for q in range(nl)])


def shift_pairs(axis, by):
    n = lax.axis_size(axis)
    return [(i, (i + by) % n) for i in range(n)]


def on_device(
    field, land, mirror, depth_weight, norm_gain, up_weight, up_bias, down_proj, layer_scale,
    section_gain, section_weight, section_bias, cotangent,
):
    R, CW, C = field.shape
    total = R * CW * lax.axis_size("lat") * lax.axis_size("lon")
    factor = 1.0 / math.sqrt(total / 64.0)
    near, send, last, shift = rim(field, mirror)
    near = lax.ppermute(near, "lat", flip_pairs("lat", 1))
    far, blk_b, (lc, rc) = far_rows(send, last, shift[0], lambda: sides(field))
    south_f, north_f, lpay, rpay = join(shift, near, far, blk_b, lc, rc, True)
    right_f = lax.ppermute(lpay, "lon", shift_pairs("lon", -1))
    left_f = lax.ppermute(rpay, "lon", shift_pairs("lon", 1))
    level, g, direct, send, last, lcol, rcol, keep, away = block_pass(
        field, south_f, north_f, left_f, right_f, land.T, depth_weight, norm_gain, up_weight, up_bias, down_proj,
        layer_scale, section_gain, section_weight, section_bias, cotangent,
    )

    place = (lax.axis_index("lat") // 2) * 2 + lax.axis_index("lon") % 2
    got = lax.ppermute(away, "lat", flip_pairs("lat", 1))
    held = add_bf(keep, got[:HALF]).reshape(4, HALF // 4, C)
    send, held = lax.optimization_barrier((send, held))
    chunk = square_sum(held, place)
    far, blk_b, base = far_rows(
        send, last, shift[0], lambda: conv_back(g, direct, depth_weight, R, CW)
    )
    chunk, far = lax.optimization_barrier((chunk, far))
    south_g, north_g, lpay, rpay = join(shift, got, far, blk_b, lcol, rcol, False)
    chunk, lpay = lax.optimization_barrier((chunk, lpay))
    gr = lax.ppermute(lpay, "lon", shift_pairs("lon", -1))
    gl = lax.ppermute(rpay, "lon", shift_pairs("lon", 1))
    chunk = line_sum(chunk)
    grad_field = edges(base, south_g, north_g, gl, gr, depth_weight, R, CW)
    axes = ("lat", "lon")
    back = [lax.ppermute(chunk, axes, square_pairs(k)) for k in (1, 2, 3)]
    back[0], grad_field = lax.optimization_barrier((back[0], grad_field))
    mine = jnp.stack([chunk] + back)
    other = lax.ppermute(mine, "lat", flip_pairs("lat", 1))
    g_depth, g_up, g_down, g_sec = finish(mine, other, factor)
    return level, grad_field, g_depth, g_up, g_down, g_sec


def solution(mesh):
    cells = P("lat", "lon", None)
    in_specs = (cells, P("lat", "lon")) + (P(),) * 10 + (cells,)
    out_specs = (cells, cells, P(), P(), P(), P())
    return jax.shard_map(on_device, mesh=mesh, in_specs=in_specs, out_specs=out_specs, check_vma=False)
```
